128 devices in a mesh: ctx: 32 (over x, z, y_hi), dp: 4 (over y_lo, core).
Axes of the slice: x: 4, y: 4 (y_hi: 2, y_lo: 2; y = y_hi * 2 + y_lo), z: 4, core: 2. Of those that a mesh axis runs over, the one named last changes fastest.
Arguments:
- hidden_states: bfloat16 [4, 8192, 5120], P('dp', 'ctx'), may hold values from -6 to 6
- block_order: int32 [64], replicated, may hold values from 0 to 63, as said below
- w_query: bfloat16 [5120, 512], P(('ctx', 'dp')), may hold values from -0.2 to 0.2
- w_key: bfloat16 [5120, 128], P(('ctx', 'dp')), may hold values from -0.2 to 0.2
- w_value: bfloat16 [5120, 128], P(('ctx', 'dp')), may hold values from -0.078125 to 0.078125
- gain_query: float32 [128], replicated, may hold values from 0.5 to 4.5
- gain_key: float32 [128], replicated, may hold values from 0.5 to 4.5
- cotangent: bfloat16 [4, 8192, 512], P('dp', 'ctx'), may hold values from -6 to 6
Outputs:
- context: bfloat16 [4, 8192, 512], P('dp', 'ctx')
- grad_states: bfloat16 [4, 8192, 5120], P('dp', 'ctx')
- grad_query: float32 [5120, 512], P(('ctx', 'dp'))
- grad_key: float32 [5120, 128], P(('ctx', 'dp'))
- grad_value: float32 [5120, 128], P(('ctx', 'dp'))
- grad_gain_query: float32 [128], replicated
- grad_gain_key: float32 [128], replicated
The draws below stay inside these ranges and needn't reach their ends.
Inputs may be any that keep to these rules, and one draw needn't show every extreme that they name: `block_order`: a permutation of the 64 sequence blocks; the stored slots 2 c and 2 c + 1 belong to index c of ctx and hold blocks b and 63 - b for some b, in either order.
All inputs are finite; a program needn't handle non-finite values.
Results may differ from the reference program's by a relative error of at most 0.04.
Values may be sent and summed in bfloat16 or wider, within the bound.
No kernel may reach another device: no remote copies, remote signals or barrier semaphores. Data moves between devices by JAX's collectives and lax.ppermute only.
A program may use at most 128 MiB of HBM per device.

```python
import math
import jax
import jax.numpy as jnp
from jax import lax

D = 5120
HQ = 4
HD = 128
SPAN = 128
SPANS = 64
LEN = 8192
SEQS = 4
N_CTX = 32


weight_limit = 0.199


def query_base(key):
    return jnp.clip(jax.random.normal(key, (D, HQ * HD), jnp.float32), -6.0, 6.0)


def draw_w_query(key, part):
    shared = query_base(key)
    return jnp.clip(shared * D ** (-0.5), -weight_limit, weight_limit).astype(jnp.bfloat16)


def draw_w_key(key, part):
    key = jax.random.fold_in(key, 2)
    noise = jnp.clip(jax.random.normal(key, (D, HD), jnp.float32), -6.0, 6.0)
    return jnp.clip(noise * D ** (-0.5), -weight_limit, weight_limit).astype(jnp.bfloat16)


def gain_values(key, lower, upper):
    return jnp.exp(jax.random.uniform(key, (HD,), jnp.float32, jnp.log(lower), jnp.log(upper)))


def draw_gain_query(key, part):
    key = jax.random.fold_in(key, 3)
    return gain_values(key, 0.6, 1.6)


def draw_gain_key(key, part):
    key = jax.random.fold_in(key, 4)
    return gain_values(key, 0.6, 1.6)


def draw_block_order(key, part):
    key = jax.random.fold_in(key, 5)
    pair_key, flip_key = jax.random.split(key)
    lower = jax.random.permutation(pair_key, N_CTX).astype(jnp.int32)
    upper = (SPANS - 1 - lower).astype(jnp.int32)
    flips = jax.random.randint(flip_key, (N_CTX,), 0, 2, jnp.int32)
    first = jnp.where(flips == 1, upper, lower)
    second = jnp.where(flips == 1, lower, upper)
    return jnp.stack([first, second], axis=1).reshape(SPANS).astype(jnp.int32)


def levels(stream_key, extent, cuts, smallest, top_value):
    def one(axis_at, parts):
        heights = jax.random.uniform(jax.random.fold_in(jax.random.fold_in(stream_key, 6), axis_at), (parts,), jnp.float32, smallest / len(cuts), top_value / len(cuts))
        return jnp.repeat(jnp.exp(heights), extent[axis_at] // parts).reshape((-1,) + (1,) * (len(extent) - axis_at - 1))

    factor_of = one(*cuts[0])
    for cut in cuts[1:]:
        factor_of = factor_of * one(*cut)
    return factor_of


def normal_values(key, extent, width, bound, cuts=(), kind=jnp.bfloat16):
    level = levels(key, extent, cuts, -0.22, 0.18) if cuts else 1.0
    array = jax.random.normal(key, extent, jnp.float32) * width * level
    return jnp.minimum(jnp.maximum(array, -bound), bound).astype(kind)


def setup_inputs(seed: int = 0) -> dict:
    keys = jax.random.split(jax.random.key(seed), 9)
    hidden_states = normal_values(keys[0], (SEQS, LEN, D), 1.0, 6.0, ((0, 4), (1, 32)))
    block_order = draw_block_order(jax.random.fold_in(keys[8], 71), 0)
    w_query = draw_w_query(jax.random.fold_in(keys[8], 71), 0)
    w_key = draw_w_key(jax.random.fold_in(keys[8], 71), 0)
    w_value = normal_values(keys[4], (D, HD), D ** -0.5, 0.078125, ((0, 128),))
    gain_query = draw_gain_query(jax.random.fold_in(keys[8], 71), 0)
    gain_key = draw_gain_key(jax.random.fold_in(keys[8], 71), 0)
    cotangent = normal_values(keys[7], (SEQS, LEN, HQ * HD), 1.0, 6.0, ((0, 4), (1, 32)))
    return {"hidden_states": hidden_states, "block_order": block_order, "w_query": w_query, "w_key": w_key, "w_value": w_value, "gain_query": gain_query, "gain_key": gain_key, "cotangent": cotangent}


theta = 1000000.0
floor_score = -1e+30

def rotation(positions, head_width):
    steps_half = jnp.arange(head_width // 2, dtype=jnp.float32)
    inverse = jnp.power(jnp.float32(theta), -2.0 * steps_half / head_width)
    angles = positions.astype(jnp.float32)[:, None] * inverse[None, :]
    cosine = jnp.cos(angles)
    sine = jnp.sin(angles)
    return (jnp.concatenate([cosine, cosine], 1), jnp.concatenate([sine, sine], 1))

def shape_heads(raw_rows, gain, cosine, sine):
    inverse_norm = lax.rsqrt(lax.optimization_barrier(jnp.mean(raw_rows * raw_rows, axis=-1, keepdims=True)) + 1e-06)
    normed = raw_rows * inverse_norm * gain
    half_width = normed.shape[-1] // 2
    turned = jnp.concatenate([-normed[..., half_width:], normed[..., :half_width]], axis=-1)
    return normed * cosine[:, None, :] + turned * sine[:, None, :]

def reference(hidden_states, block_order, w_query, w_key, w_value, gain_query, gain_key, cotangent):
    q_cols = HQ * HD
    score_scale = HD ** (-0.5)
    offsets = jnp.arange(SPAN, dtype=jnp.int32)
    positions = (block_order[:, None] * SPAN + offsets[None, :]).reshape(LEN).astype(jnp.int32)
    cosine, sine = rotation(positions, HD)
    rows_block = math.gcd(LEN, 512)
    block_count = LEN // rows_block
    contract = (((1,), (1,)), ((), ()))
    weight_grad = jnp.zeros((D, q_cols + 2 * HD), jnp.float32)
    gain_q_sum = jnp.zeros((HD,), jnp.float32)
    gain_k_sum = jnp.zeros((HD,), jnp.float32)
    contexts = []
    grads_states = []
    for seq in range(SEQS):
        tokens = hidden_states[seq]
        raw_q = jnp.dot(tokens, w_query, preferred_element_type=jnp.float32).reshape(LEN, HQ, HD)
        raw_k = jnp.dot(tokens, w_key, preferred_element_type=jnp.float32)[:, None, :]
        raw_v = jnp.dot(tokens, w_value, preferred_element_type=jnp.float32)

        def local_heads(rq, rk, gq, gk):
            return (shape_heads(rq, gq, cosine, sine), shape_heads(rk, gk, cosine, sine))
        (shaped_q, shaped_k), pullback = jax.vjp(local_heads, raw_q, raw_k, gain_query, gain_key)
        query32 = shaped_q.astype(jnp.bfloat16).astype(jnp.float32)
        key32 = shaped_k[:, 0, :].astype(jnp.bfloat16).astype(jnp.float32)
        value32 = raw_v.astype(jnp.bfloat16).astype(jnp.float32)
        grad_out = cotangent[seq].reshape(LEN, HQ, HD).astype(jnp.float32)

        def query_block(carry, index):
            grad_k, grad_v = carry
            start = (index * rows_block).astype(jnp.int32)
            q_part = lax.dynamic_slice_in_dim(query32, start, rows_block, 0)
            g_part = lax.dynamic_slice_in_dim(grad_out, start, rows_block, 0)
            p_part = lax.dynamic_slice_in_dim(positions, start, rows_block, 0)
            scores = jnp.einsum('qhd,kd->hqk', q_part, key32) * score_scale
            allowed = positions[None, :] <= p_part[:, None]
            scores = jnp.where(allowed[None], scores, floor_score)
            top = lax.optimization_barrier(jnp.max(scores, axis=2))
            total = lax.optimization_barrier(jnp.sum(jnp.exp(scores - top[..., None]), axis=2))
            log_total = top + jnp.log(total)
            probs = jnp.exp(scores - log_total[..., None])
            probs16 = lax.optimization_barrier(probs.astype(jnp.bfloat16)).astype(jnp.float32)
            ctx16 = jnp.einsum('hqk,kd->qhd', probs16, value32).astype(jnp.bfloat16)
            ctx32 = lax.optimization_barrier(ctx16).astype(jnp.float32)
            row_delta = lax.optimization_barrier(jnp.sum(g_part * ctx32, axis=2)).T
            grad_probs = jnp.einsum('qhd,kd->hqk', g_part, value32)
            grad_scores = (probs * (grad_probs - row_delta[..., None]) * score_scale).astype(jnp.bfloat16)
            grad_scores = lax.optimization_barrier(grad_scores).astype(jnp.float32)
            grad_q_part = jnp.einsum('hqk,kd->qhd', grad_scores, key32)
            grad_k = grad_k + jnp.einsum('hqk,qhd->kd', grad_scores, q_part)
            grad_v = grad_v + jnp.einsum('hqk,qhd->kd', probs16, g_part)
            return ((grad_k, grad_v), (ctx16, grad_q_part))
        start_pair = (jnp.zeros((LEN, HD), jnp.float32), jnp.zeros((LEN, HD), jnp.float32))
        (grad_k, grad_v), (ctx_blocks, grad_q_blocks) = lax.scan(query_block, start_pair, jnp.arange(block_count, dtype=jnp.int32))
        contexts.append(ctx_blocks.reshape(LEN, q_cols))
        grad_q = grad_q_blocks.reshape(LEN, HQ, HD)
        grad_raw_q, grad_raw_k, grad_gq, grad_gk = pullback((grad_q, grad_k[:, None, :]))
        grad_rows = jnp.concatenate([grad_raw_q.reshape(LEN, q_cols), grad_raw_k[:, 0, :], grad_v], axis=1).astype(jnp.bfloat16)
        grad_tokens = lax.dot_general(grad_rows[:, :q_cols], w_query, contract, preferred_element_type=jnp.float32)
        grad_tokens = grad_tokens + lax.dot_general(grad_rows[:, q_cols:q_cols + HD], w_key, contract, preferred_element_type=jnp.float32)
        grad_tokens = grad_tokens + lax.dot_general(grad_rows[:, q_cols + HD:], w_value, contract, preferred_element_type=jnp.float32)
        grads_states.append(grad_tokens.astype(jnp.bfloat16))
        weight_grad = weight_grad + lax.dot_general(tokens, grad_rows, (((0,), (0,)), ((), ())), preferred_element_type=jnp.float32)
        gain_q_sum = gain_q_sum + grad_gq
        gain_k_sum = gain_k_sum + grad_gk
    return (jnp.stack(contexts), jnp.stack(grads_states), weight_grad[:, :q_cols], weight_grad[:, q_cols:q_cols + HD], weight_grad[:, q_cols + HD:], gain_q_sum, gain_k_sum)
```

```python
import math

import jax
import jax.numpy as jnp
from jax import lax
from jax.experimental import pallas as pl
from jax.experimental.pallas import tpu as pltpu
from jax.sharding import Mesh
from jax.sharding import PartitionSpec as P

bf16, f32 = jnp.bfloat16, jnp.float32
theta = 1000000.0
floor_score = -1e30
span = 128
chunk = 512
per_chunk = chunk // span
mib = 2**20
smem = pl.BlockSpec(memory_space=pltpu.SMEM)
vmem = pl.BlockSpec(memory_space=pltpu.VMEM)


def mm(a, b):
    return jnp.dot(a, b, preferred_element_type=f32)


def rotation(positions, head_width):
    steps_half = jnp.arange(head_width // 2, dtype=f32)
    inverse = jnp.power(f32(theta), -2.0 * steps_half / head_width)
    angles = positions.astype(f32)[:, None] * inverse[None, :]
    cosine = jnp.cos(angles)
    sine = jnp.sin(angles)
    return jnp.concatenate([cosine, cosine], 1), jnp.concatenate([-sine, sine], 1)


def inverse_norm(raw):
    return lax.rsqrt(jnp.mean(raw * raw, axis=-1, keepdims=True) + 1e-06)


def shape_head(raw, gain, cosine, sine):
    normed = raw * inverse_norm(raw) * gain
    return normed * cosine + pltpu.roll(normed, span // 2, 1) * sine


def shape_head_grad(raw, gain, cosine, sine, grad):
    inverse = inverse_norm(raw)
    grad_normed = grad * cosine + pltpu.roll(grad * sine, span // 2, 1)
    grad_unit = grad_normed * gain
    unit = raw * inverse
    shrink = jnp.mean(grad_unit * unit, axis=-1, keepdims=True)
    return inverse * (grad_unit - unit * shrink), grad_normed * unit


def key_value_kernel(tok_ref, w_ref, gain_ref, cos_ref, sin_ref, kv_ref):
    raw = mm(tok_ref[...], w_ref[...])
    kv_ref[:, :span] = shape_head(raw[:, :span], gain_ref[...], cos_ref[...], sin_ref[...]).astype(bf16)
    kv_ref[:, span:] = raw[:, span:].astype(bf16)


def query_kernel(tok_ref, wq_ref, wkv_ref, gain_ref, cos_ref, sin_ref, q_ref, raw_ref):
    cols = wq_ref.shape[1]
    raw_ref[:, :cols] = mm(tok_ref[...], wq_ref[...])
    raw_ref[:, cols:] = mm(tok_ref[...], wkv_ref[...])[:, :span]
    gain = gain_ref[...] * (span**-0.5 / math.log(2.0))
    for h in range(cols // span):
        part = slice(h * span, (h + 1) * span)
        q_ref[:, part] = shape_head(raw_ref[:, part], gain, cos_ref[...], sin_ref[...]).astype(bf16)


def attention_kernel(
    order, own, q_ref, g_ref, kv_ref, kv_other_ref, ctx_ref, dq_ref, dkv_ref, dkv_other_ref,
    slot_of, ks, vs, kt, vt, acc_kv, qs, gs, qt, gt, acc_o, row_max, row_sum, row_delta, acc_q,
):
    spans, heads = order.shape[0], q_ref.shape[1] // span
    chunks = spans // per_chunk
    rows = heads * span
    core = own[2]

    def place(slot, carry):
        slot_of[order[slot]] = slot
        return carry

    lax.fori_loop(0, spans, place, 0)

    def arrange(c, carry):
        for j in range(per_chunk):
            slot = slot_of[c * per_chunk + j]
            pair, rows_at = slot // 4, pl.multiple_of(slot % 2 * span, span)
            mine = (slot // 2) % 2 == core
            both = jnp.where(
                mine, kv_ref[pair, pl.ds(rows_at, span), :], kv_other_ref[pair, pl.ds(rows_at, span), :]
            )
            part = slice(j * span, (j + 1) * span)
            ks[c, part, :] = both[:, :span]
            vs[c, part, :] = both[:, span:]
            kt[c, :, part] = both[:, :span].T
            vt[c, :, part] = both[:, span:].T
        acc_kv[c] = jnp.zeros_like(acc_kv[c])
        return carry

    lax.fori_loop(0, chunks, arrange, 0)

    first_upper = own[0] > own[1]
    for upper in (True, False):
        which = jnp.where(first_upper, 0, 1) if upper else jnp.where(first_upper, 1, 0)
        block = own[which]
        row0 = pl.multiple_of(which * span, span)
        last = block // per_chunk
        for h in range(heads):
            part = slice(h * span, (h + 1) * span)
            qh = q_ref[pl.ds(row0, span), part]
            gh = g_ref[pl.ds(row0, span), part]
            qs[part, :] = qh
            gs[part, :] = gh
            qt[:, part] = qh.T
            gt[:, part] = gh.T

        def allowed(c):
            key_pos = c * chunk + lax.broadcasted_iota(jnp.int32, (chunk, rows), 0)
            row = lax.broadcasted_iota(jnp.int32, (chunk, rows), 1)
            return key_pos <= block * span + jnp.bitwise_and(row, span - 1)

        row_max[...] = jnp.full_like(row_max, floor_score)
        row_sum[...] = jnp.zeros_like(row_sum)
        acc_o[...] = jnp.zeros_like(acc_o)

        def forward(c, masked):
            s = mm(ks[c], qt[...])
            if masked:
                s = jnp.where(allowed(c), s, floor_score)
            old = row_max[...]
            new = jnp.maximum(old, jnp.max(s, axis=0, keepdims=True))
            p = jnp.exp2(s - new)
            alpha = jnp.exp2(old - new)
            row_max[...] = new
            row_sum[...] = row_sum[...] * alpha + jnp.sum(p, axis=0, keepdims=True)
            acc_o[...] = acc_o[...] * alpha + mm(vt[c], p.astype(bf16))

        def forward_step(c, carry):
            forward(c, False)
            return carry

        lax.fori_loop(0, last, forward_step, 0)
        forward(last, True)

        total = row_sum[...]
        ctx_t = (acc_o[...] / total).astype(bf16)
        row_max[...] = row_max[...] + jnp.log2(total)
        row_delta[...] = jnp.sum(ctx_t.astype(f32) * gt[...].astype(f32), axis=0, keepdims=True)
        for h in range(heads):
            part = slice(h * span, (h + 1) * span)
            ctx_ref[pl.ds(row0, span), part] = ctx_t[:, part].T
        acc_q[...] = jnp.zeros_like(acc_q)

        def backward(c, masked):
            s = mm(ks[c], qt[...])
            p = jnp.exp2(s - row_max[...])
            if masked:
                p = jnp.where(allowed(c), p, 0.0)
            dp = mm(vs[c], gt[...])
            ds = (p * (dp - row_delta[...])).astype(bf16)
            acc_kv[c, :, span:] += mm(p.astype(bf16), gs[...])
            acc_kv[c, :, :span] += mm(ds, qs[...])
            acc_q[...] += mm(kt[c], ds)

        def backward_step(c, carry):
            backward(c, False)
            return carry

        lax.fori_loop(0, last, backward_step, 0)
        backward(last, True)
        for h in range(heads):
            part = slice(h * span, (h + 1) * span)
            dq_ref[pl.ds(row0, span), part] = acc_q[:, part].T * (span**-0.5)

    def give(c, carry):
        for j in range(per_chunk):
            part = slice(j * span, (j + 1) * span)
            slot = slot_of[c * per_chunk + j]
            pair, rows_at = slot // 4, pl.multiple_of(slot % 2 * span, span)
            mine = (slot // 2) % 2 == core
            dk = (acc_kv[c, part, :span] * math.log(2.0)).astype(bf16)
            dv = acc_kv[c, part, span:].astype(bf16)

            @pl.when(mine)
            def _():
                dkv_ref[pair, pl.ds(rows_at, span), :span] = dk
                dkv_ref[pair, pl.ds(rows_at, span), span:] = dv

            @pl.when(jnp.logical_not(mine))
            def _():
                dkv_other_ref[pair, pl.ds(rows_at, span), :span] = dk
                dkv_other_ref[pair, pl.ds(rows_at, span), span:] = dv

        return carry

    lax.fori_loop(0, chunks, give, 0)


def attention(order, own, q16, g16, kv, kv_other):
    rows_here, cols = q16.shape
    spans = order.shape[0]
    chunks = spans // per_chunk
    rows = cols
    share = jax.ShapeDtypeStruct(kv.shape, bf16)
    return pl.pallas_call(
        attention_kernel,
        out_shape=(
            jax.ShapeDtypeStruct((rows_here, cols), bf16),
            jax.ShapeDtypeStruct((rows_here, cols), f32),
            share,
            share,
        ),
        in_specs=[smem, smem] + [vmem] * 4,
        out_specs=(vmem,) * 4,
        scratch_shapes=[
            pltpu.SMEM((spans,), jnp.int32),
            pltpu.VMEM((chunks, chunk, span), bf16),
            pltpu.VMEM((chunks, chunk, span), bf16),
            pltpu.VMEM((chunks, span, chunk), bf16),
            pltpu.VMEM((chunks, span, chunk), bf16),
            pltpu.VMEM((chunks, chunk, 2 * span), f32),
            pltpu.VMEM((rows, span), bf16),
            pltpu.VMEM((rows, span), bf16),
            pltpu.VMEM((span, rows), bf16),
            pltpu.VMEM((span, rows), bf16),
            pltpu.VMEM((span, rows), f32),
            pltpu.VMEM((1, rows), f32),
            pltpu.VMEM((1, rows), f32),
            pltpu.VMEM((1, rows), f32),
            pltpu.VMEM((span, rows), f32),
        ],
        compiler_params=pltpu.CompilerParams(vmem_limit_bytes=48 * mib),
        cost_estimate=pl.CostEstimate(
            flops=8 * 10**9, bytes_accessed=10 * 10**6, transcendentals=9 * 10**6
        ),
        name="attention",
    )(order, own, q16, g16, kv, kv_other)


def grad_rows_kernel(raw_ref, dq_ref, dkv_ref, gq_ref, gk_ref, cos_ref, sin_ref, g_ref, gain_ref):
    cols = dq_ref.shape[1]
    cosine, sine = cos_ref[...], sin_ref[...]
    gain_q = jnp.zeros((1, span), f32)
    for h in range(cols // span):
        part = slice(h * span, (h + 1) * span)
        grad, terms = shape_head_grad(raw_ref[:, part], gq_ref[...], cosine, sine, dq_ref[:, part])
        g_ref[:, part] = grad.astype(bf16)
        gain_q = gain_q + jnp.sum(terms, axis=0, keepdims=True)
    dkv = jnp.sum(dkv_ref[...].astype(f32), axis=0)
    grad, terms = shape_head_grad(raw_ref[:, cols:], gk_ref[...], cosine, sine, dkv[:, :span])
    g_ref[:, cols : cols + span] = grad.astype(bf16)
    g_ref[:, cols + span :] = dkv[:, span:].astype(bf16)
    gain_k = jnp.sum(terms, axis=0, keepdims=True)
    pieces = []
    for gain in (gain_q, gain_k):
        high = gain.astype(bf16).astype(f32)
        pieces += [high, gain - high]
    row = jnp.concatenate(pieces + [jnp.zeros((1, 2 * span), f32)], axis=1)
    gain_ref[...] = jnp.where(lax.broadcasted_iota(jnp.int32, gain_ref.shape, 0) == 0, row, 0.0)


def weight_grad_kernel(mine_ref, other_ref, g_ref, g_other_ref, gain_ref, out_ref):
    total = mm(mine_ref[...], g_ref[...]) + mm(other_ref[...], g_other_ref[...])
    owners, padded = out_ref.shape[0], out_ref.shape[1]
    own_rows = padded - gain_ref.shape[0]
    for i in range(owners):
        part = total[i * own_rows : (i + 1) * own_rows]
        out_ref[i] = jnp.concatenate([part, gain_ref[...]], axis=0).astype(bf16)


def weight_grad(mine, other, g, g_other, gains, owners):
    rows, cols = mine.shape[0] // owners, g.shape[1]
    padded = rows + gains.shape[0]
    step = math.gcd(owners, 16)
    toks = mine.shape[1]
    whole = lambda shape: pl.BlockSpec(shape, lambda i: (0,) * len(shape))
    return pl.pallas_call(
        weight_grad_kernel,
        grid=(owners // step,),
        out_shape=jax.ShapeDtypeStruct((owners, padded, cols), bf16),
        in_specs=[
            pl.BlockSpec((step * rows, toks), lambda i: (i, 0)),
            pl.BlockSpec((step * rows, toks), lambda i: (i, 0)),
            whole(g.shape),
            whole(g.shape),
            whole(gains.shape),
        ],
        out_specs=pl.BlockSpec((step, padded, cols), lambda i: (i, 0, 0)),
        compiler_params=pltpu.CompilerParams(vmem_limit_bytes=40 * mib),
        name="weight_grad",
    )(mine, other, g, g_other, gains)


def call(kernel, shapes, *args, name):
    return pl.pallas_call(
        kernel,
        out_shape=shapes,
        in_specs=[vmem] * len(args),
        out_specs=jax.tree.map(lambda _: vmem, shapes),
        compiler_params=pltpu.CompilerParams(vmem_limit_bytes=48 * mib),
        name=name,
    )(*args)


plane = ("x", "z")
chips = ("x", "z", "y_hi", "y_lo")
swapped = [(0, 0), (1, 2), (2, 1), (3, 3)]
flipped = [(0, 1), (1, 0)]


def swap(array):
    return lax.ppermute(array, ("y_hi", "core"), swapped)


def flip(array):
    return lax.ppermute(array, "core", flipped)


def to_all(array, axes, count):
    return lax.all_to_all(jnp.broadcast_to(array[None], (count,) + array.shape), axes, 0, 0)


def pick(array, index, axis):
    return lax.dynamic_index_in_dim(array, index, axis, keepdims=False)


def local(hidden_states, block_order, w_query, w_key, w_value, gain_query, gain_key, cotangent):
    tokens = hidden_states[0]
    tok_rows, width = tokens.shape
    q_cols = w_query.shape[1]
    own_rows = w_query.shape[0]
    chip_count = width // own_rows // 2
    pairs = 16
    at_x, at_z = lax.axis_index("x"), lax.axis_index("z")
    y_hi, core = lax.axis_index("y_hi"), lax.axis_index("core")
    offsets = jnp.arange(span, dtype=jnp.int32)

    def slots_of(half):
        place = (at_x * 4 + at_z) * 2 + half
        blocks = lax.dynamic_slice_in_dim(block_order, 2 * place, 2)
        positions = (blocks[:, None] * span + offsets[None, :]).reshape(tok_rows)
        return blocks, rotation(positions, span)

    _, (cos_kv, sin_kv) = slots_of(y_hi)
    own_blocks, (cosine, sine) = slots_of(core)
    own = jnp.concatenate([own_blocks, core[None].astype(jnp.int32)])
    gain_q, gain_k = gain_query[None, :], gain_key[None, :]

    w_kv = jnp.concatenate([w_key, w_value], axis=1)
    kv_mine = to_all(w_kv, chips, chip_count)
    kv_theirs = flip(kv_mine)
    full_query = lax.all_gather(
        w_query, ("x", "z", "y_hi", "y_lo", "core"), axis=0, tiled=True
    )
    lower = jnp.where(core == 0, kv_mine, kv_theirs)
    upper = jnp.where(core == 0, kv_theirs, kv_mine)
    full_kv = jnp.stack([lower, upper], axis=1).reshape(width, 2 * span)

    toks = swap(tokens)
    grad_out = swap(cotangent[0])

    kv16 = call(
        key_value_kernel,
        jax.ShapeDtypeStruct((tok_rows, 2 * span), bf16),
        tokens, full_kv, gain_k, cos_kv, sin_kv,
        name="key_value",
    )
    kv_own = to_all(swap(kv16), plane, pairs)
    kv_other = flip(kv_own)

    q16, raw = call(
        query_kernel,
        (
            jax.ShapeDtypeStruct((tok_rows, q_cols), bf16),
            jax.ShapeDtypeStruct((tok_rows, q_cols + span), f32),
        ),
        toks, full_query, full_kv, gain_q, cosine, sine,
        name="query",
    )
    turned = toks.T.reshape(chip_count, 2, own_rows, tok_rows)
    turned_mine = pick(turned, core, 1).reshape(-1, tok_rows)
    turned_other = flip(pick(turned, 1 - core, 1).reshape(-1, tok_rows))

    ctx, dq, dkv_mine, dkv_theirs = attention(block_order, own, q16, grad_out, kv_own, kv_other)
    context = swap(ctx)
    dkv = (dkv_mine.astype(f32) + flip(dkv_theirs).astype(f32)).astype(bf16)
    dkv = lax.all_to_all(dkv, plane, 0, 0)

    grad_rows, gains = call(
        grad_rows_kernel,
        (
            jax.ShapeDtypeStruct((tok_rows, q_cols + 2 * span), bf16),
            jax.ShapeDtypeStruct((8, q_cols + 2 * span), f32),
        ),
        raw, dq, dkv, gain_q, gain_k, cosine, sine,
        name="grad_rows",
    )
    partial = weight_grad(turned_mine, turned_other, grad_rows, flip(grad_rows), gains, chip_count)
    parts = lax.all_to_all(partial, chips, 0, 0)
    sums = jnp.sum(parts.astype(f32), axis=0)
    own_grads = sums[:own_rows]
    gain_row = sums[own_rows, : 4 * span].reshape(2, 2, span).sum(axis=1)
    gain_sums = gain_row + flip(gain_row)

    own_grad_rows = swap(grad_rows)
    contract = (((1,), (1,)), ((), ()))
    grad_tokens = lax.dot_general(
        own_grad_rows[:, :q_cols], full_query, contract, preferred_element_type=f32
    ) + lax.dot_general(own_grad_rows[:, q_cols:], full_kv, contract, preferred_element_type=f32)
    return (
        context[None],
        grad_tokens.astype(bf16)[None],
        own_grads[:, :q_cols],
        own_grads[:, q_cols : q_cols + span],
        own_grads[:, q_cols + span :],
        gain_sums[0],
        gain_sums[1],
    )


def solution(mesh):
    fine = Mesh(mesh.devices.reshape(4, 4, 2, 2, 2), ("x", "z", "y_hi", "y_lo", "core"))
    ctx, dp = ("x", "z", "y_hi"), ("y_lo", "core")
    rows = P(ctx + dp, None)
    tokens = P(dp, ctx, None)
    in_specs = (tokens, P(), rows, rows, rows, P(), P(), tokens)
    out_specs = (tokens, tokens, rows, rows, rows, P(), P())
    return jax.shard_map(local, mesh=fine, in_specs=in_specs, out_specs=out_specs, check_vma=False)
```

```python
import math

import jax
import jax.numpy as jnp
from jax import lax
from jax.experimental import pallas as pl
from jax.experimental.pallas import tpu as pltpu
from jax.sharding import Mesh
from jax.sharding import PartitionSpec as P

bf16, f32 = jnp.bfloat16, jnp.float32
theta = 1000000.0
floor_score = -1e30
span = 128
chunk = 512
per_chunk = chunk // span
mib = 2**20
smem = pl.BlockSpec(memory_space=pltpu.SMEM)
vmem = pl.BlockSpec(memory_space=pltpu.VMEM)


def mm(a, b):
    return jnp.dot(a, b, preferred_element_type=f32)


def rotation(positions, head_width):
    steps_half = jnp.arange(head_width // 2, dtype=f32)
    inverse = jnp.power(f32(theta), -2.0 * steps_half / head_width)
    angles = positions.astype(f32)[:, None] * inverse[None, :]
    cosine = jnp.cos(angles)
    sine = jnp.sin(angles)
    return jnp.concatenate([cosine, cosine], 1), jnp.concatenate([-sine, sine], 1)


def inverse_norm(raw):
    return lax.rsqrt(jnp.mean(raw * raw, axis=-1, keepdims=True) + 1e-06)


def shape_head(raw, gain, cosine, sine):
    normed = raw * inverse_norm(raw) * gain
    return normed * cosine + pltpu.roll(normed, span // 2, 1) * sine


def shape_head_grad(raw, gain, cosine, sine, grad):
    inverse = inverse_norm(raw)
    grad_normed = grad * cosine + pltpu.roll(grad * sine, span // 2, 1)
    grad_unit = grad_normed * gain
    unit = raw * inverse
    shrink = jnp.mean(grad_unit * unit, axis=-1, keepdims=True)
    return inverse * (grad_unit - unit * shrink), grad_normed * unit


def prepare_kernel(where, src_ref, toks_ref, toks_theirs_ref, turned_ref):
    planes, columns = src_ref.shape[:2]
    core = where[1]

    def piece(plane, y, side):
        return src_ref[plane, y, side].astype(f32)

    group = 4
    for side, out_ref in ((core, toks_ref), (1 - core, toks_theirs_ref)):
        for i in range(0, planes, group):
            rows = jnp.concatenate(
                [piece(i + j, y, side) for j in range(group) for y in range(columns)], axis=0
            ).astype(bf16)
            wide = rows.shape[0]
            out_ref[:, i // group * wide : (i // group + 1) * wide] = rows.T
    for y in range(columns):
        for side in range(2):
            turned_ref[2 * y + side] = jnp.concatenate(
                [piece(i, y, side) for i in range(planes)], axis=0
            ).astype(bf16)


def key_value_kernel(mine_ref, other_ref, w_ref, w_other_ref, gain_ref, cos_ref, sin_ref, kv_ref, raw_ref):
    raw = mm(mine_ref[...], w_ref[...]) + mm(other_ref[...], w_other_ref[...])
    raw_ref[...] = raw[:, :span]
    kv_ref[:, :span] = shape_head(raw[:, :span], gain_ref[...], cos_ref[...], sin_ref[...]).astype(bf16)
    kv_ref[:, span:] = raw[:, span:].astype(bf16)


def query_part_kernel(mine_ref, other_ref, w_ref, part_ref, part_other_ref):
    part_ref[...] = mm(mine_ref[...], w_ref[...])
    part_other_ref[...] = mm(other_ref[...], w_ref[...])


def query_kernel(part_ref, part_theirs_ref, gain_ref, cos_ref, sin_ref, q_ref, raw_ref):
    gain = gain_ref[...] * (span**-0.5 / math.log(2.0))
    for h in range(raw_ref.shape[1] // span):
        part = slice(h * span, (h + 1) * span)
        raw = part_ref[:, part] + part_theirs_ref[:, part]
        raw_ref[:, part] = raw.astype(bf16)
        q_ref[:, part] = shape_head(raw, gain, cos_ref[...], sin_ref[...]).astype(bf16)


def attention_kernel(
    order, own, q_ref, g_ref, kv_ref, kv_other_ref, ctx_ref, dq_ref, dkv_ref, dkv_other_ref,
    slot_of, ks, vs, kt, vt, acc_kv, qs, gs, qt, gt, acc_o, row_max, row_sum, row_delta, acc_q,
):
    spans, heads = order.shape[0], q_ref.shape[1] // span
    chunks = spans // per_chunk
    rows = heads * span
    core = own[2]

    def place(slot, carry):
        slot_of[order[slot]] = slot
        return carry

    lax.fori_loop(0, spans, place, 0)

    def arrange(c, carry):
        for j in range(per_chunk):
            slot = slot_of[c * per_chunk + j]
            pair, rows_at = slot // 4, pl.multiple_of(slot % 2 * span, span)
            mine = (slot // 2) % 2 == core
            both = jnp.where(
                mine, kv_ref[pair, pl.ds(rows_at, span), :], kv_other_ref[pair, pl.ds(rows_at, span), :]
            )
            part = slice(j * span, (j + 1) * span)
            ks[c, part, :] = both[:, :span]
            vs[c, part, :] = both[:, span:]
            kt[c, :, part] = both[:, :span].T
            vt[c, :, part] = both[:, span:].T
        acc_kv[c] = jnp.zeros_like(acc_kv[c])
        return carry

    lax.fori_loop(0, chunks, arrange, 0)

    first_upper = own[0] > own[1]
    for upper in (True, False):
        which = jnp.where(first_upper, 0, 1) if upper else jnp.where(first_upper, 1, 0)
        block = own[which]
        row0 = pl.multiple_of(which * span, span)
        last = block // per_chunk
        for h in range(heads):
            part = slice(h * span, (h + 1) * span)
            qh = q_ref[pl.ds(row0, span), part]
            gh = g_ref[pl.ds(row0, span), part]
            qs[part, :] = qh
            gs[part, :] = gh
            qt[:, part] = qh.T
            gt[:, part] = gh.T

        def allowed(c):
            key_pos = c * chunk + lax.broadcasted_iota(jnp.int32, (chunk, rows), 0)
            row = lax.broadcasted_iota(jnp.int32, (chunk, rows), 1)
            return key_pos <= block * span + jnp.bitwise_and(row, span - 1)

        row_max[...] = jnp.full_like(row_max, floor_score)
        row_sum[...] = jnp.zeros_like(row_sum)
        acc_o[...] = jnp.zeros_like(acc_o)

        def forward(c, masked):
            s = mm(ks[c], qt[...])
            if masked:
                s = jnp.where(allowed(c), s, floor_score)
            old = row_max[...]
            new = jnp.maximum(old, jnp.max(s, axis=0, keepdims=True))
            p = jnp.exp2(s - new)
            alpha = jnp.exp2(old - new)
            row_max[...] = new
            row_sum[...] = row_sum[...] * alpha + jnp.sum(p, axis=0, keepdims=True)
            acc_o[...] = acc_o[...] * alpha + mm(vt[c], p.astype(bf16))

        def forward_step(c, carry):
            forward(c, False)
            return carry

        lax.fori_loop(0, last, forward_step, 0)
        forward(last, True)

        total = row_sum[...]
        ctx_t = (acc_o[...] / total).astype(bf16)
        row_max[...] = row_max[...] + jnp.log2(total)
        row_delta[...] = jnp.sum(ctx_t.astype(f32) * gt[...].astype(f32), axis=0, keepdims=True)
        for h in range(heads):
            part = slice(h * span, (h + 1) * span)
            ctx_ref[pl.ds(row0, span), part] = ctx_t[:, part].T
        acc_q[...] = jnp.zeros_like(acc_q)

        def backward(c, masked):
            s = mm(ks[c], qt[...])
            p = jnp.exp2(s - row_max[...])
            if masked:
                p = jnp.where(allowed(c), p, 0.0)
            dp = mm(vs[c], gt[...])
            ds = (p * (dp - row_delta[...])).astype(bf16)
            acc_kv[c, :, span:] += mm(p.astype(bf16), gs[...])
            acc_kv[c, :, :span] += mm(ds, qs[...])
            acc_q[...] += mm(kt[c], ds)

        def backward_step(c, carry):
            backward(c, False)
            return carry

        lax.fori_loop(0, last, backward_step, 0)
        backward(last, True)
        for h in range(heads):
            part = slice(h * span, (h + 1) * span)
            dq_ref[pl.ds(row0, span), part] = acc_q[:, part].T * (span**-0.5)

    def give(c, carry):
        for j in range(per_chunk):
            part = slice(j * span, (j + 1) * span)
            slot = slot_of[c * per_chunk + j]
            pair, rows_at = slot // 4, pl.multiple_of(slot % 2 * span, span)
            mine = (slot // 2) % 2 == core
            dk = (acc_kv[c, part, :span] * math.log(2.0)).astype(bf16)
            dv = acc_kv[c, part, span:].astype(bf16)

            @pl.when(mine)
            def _():
                dkv_ref[pair, pl.ds(rows_at, span), :span] = dk
                dkv_ref[pair, pl.ds(rows_at, span), span:] = dv

            @pl.when(jnp.logical_not(mine))
            def _():
                dkv_other_ref[pair, pl.ds(rows_at, span), :span] = dk
                dkv_other_ref[pair, pl.ds(rows_at, span), span:] = dv

        return carry

    lax.fori_loop(0, chunks, give, 0)


def attention(order, own, q16, g16, kv, kv_other):
    rows_here, cols = q16.shape
    spans = order.shape[0]
    chunks = spans // per_chunk
    rows = cols
    share = jax.ShapeDtypeStruct(kv.shape, bf16)
    return pl.pallas_call(
        attention_kernel,
        out_shape=(
            jax.ShapeDtypeStruct((rows_here, cols), bf16),
            jax.ShapeDtypeStruct((rows_here, cols), f32),
            share,
            share,
        ),
        in_specs=[smem, smem] + [vmem] * 4,
        out_specs=(vmem,) * 4,
        scratch_shapes=[
            pltpu.SMEM((spans,), jnp.int32),
            pltpu.VMEM((chunks, chunk, span), bf16),
            pltpu.VMEM((chunks, chunk, span), bf16),
            pltpu.VMEM((chunks, span, chunk), bf16),
            pltpu.VMEM((chunks, span, chunk), bf16),
            pltpu.VMEM((chunks, chunk, 2 * span), f32),
            pltpu.VMEM((rows, span), bf16),
            pltpu.VMEM((rows, span), bf16),
            pltpu.VMEM((span, rows), bf16),
            pltpu.VMEM((span, rows), bf16),
            pltpu.VMEM((span, rows), f32),
            pltpu.VMEM((1, rows), f32),
            pltpu.VMEM((1, rows), f32),
            pltpu.VMEM((1, rows), f32),
            pltpu.VMEM((span, rows), f32),
        ],
        compiler_params=pltpu.CompilerParams(vmem_limit_bytes=48 * mib),
        cost_estimate=pl.CostEstimate(
            flops=3 * 10**10, bytes_accessed=10 * 10**6, transcendentals=9 * 10**6
        ),
        name="attention",
    )(order, own, q16, g16, kv, kv_other)


def grad_query_kernel(raw_ref, dq_ref, gain_ref, cos_ref, sin_ref, g_ref, gain_out):
    cosine, sine = cos_ref[...], sin_ref[...]
    sums = jnp.zeros((1, span), f32)
    for h in range(dq_ref.shape[1] // span):
        part = slice(h * span, (h + 1) * span)
        grad, terms = shape_head_grad(
            raw_ref[:, part].astype(f32), gain_ref[...], cosine, sine, dq_ref[:, part]
        )
        g_ref[:, part] = grad.astype(bf16)
        sums = sums + jnp.sum(terms, axis=0, keepdims=True)
    gain_out[...] = jnp.broadcast_to(sums, gain_out.shape)


def grad_key_value_kernel(raw_ref, dkv_ref, gain_ref, cos_ref, sin_ref, gain_q_ref, g_ref):
    rows = raw_ref.shape[0]
    dkv = jnp.sum(dkv_ref[...].astype(f32), axis=0)
    grad, terms = shape_head_grad(
        raw_ref[...].astype(f32), gain_ref[...], cos_ref[...], sin_ref[...], dkv[:, :span]
    )
    g_ref[:rows, :span] = grad.astype(bf16)
    g_ref[:rows, span:] = dkv[:, span:].astype(bf16)
    gain_k = jnp.sum(terms, axis=0, keepdims=True)
    split = []
    for gain in (gain_q_ref[0:1], gain_k):
        high = gain.astype(bf16).astype(f32)
        split.append(jnp.concatenate([high, gain - high], axis=1))
    row = lax.broadcasted_iota(jnp.int32, (g_ref.shape[0] - rows, 2 * span), 0)
    g_ref[rows:] = jnp.where(row == 0, split[0], jnp.where(row == 1, split[1], 0.0)).astype(bf16)


def weight_grad_kernel(where, turned_ref, *rest):
    blocks, out_ref = rest[:-1], rest[-1]
    columns = len(blocks) // 2
    toks = turned_ref.shape[2]
    y, core = where[0], where[1]
    total, gains = None, None
    for side in range(2):
        for k in range(columns):
            from_y = lax.rem(y + k, columns)
            from_core = core if side == 0 else 1 - core
            at = (from_core * 2 + lax.rem(from_y, 2)) * 2 + from_y // 2
            block = blocks[side * columns + k]
            part = mm(turned_ref[at], block[:toks])
            total = part if total is None else total + part
            if block.shape[0] > toks:
                row = block[toks:].astype(f32)
                gains = row if gains is None else gains + row
    own_rows = total.shape[0] // out_ref.shape[0]
    extra = []
    if gains is not None:
        gain = gains[:, :span] + gains[:, span:]
        high = gain.astype(bf16).astype(f32)
        extra = [jnp.concatenate([high, gain - high], axis=1)[:8]]
    for i in range(out_ref.shape[0]):
        part = total[i * own_rows : (i + 1) * own_rows]
        out_ref[i] = jnp.concatenate([part] + extra, axis=0).astype(bf16)


def weight_grad(where, turned, blocks, planes, padded):
    return pl.pallas_call(
        weight_grad_kernel,
        out_shape=jax.ShapeDtypeStruct((planes, padded, blocks[0].shape[1]), bf16),
        in_specs=[smem] + [vmem] * (1 + len(blocks)),
        out_specs=vmem,
        compiler_params=pltpu.CompilerParams(vmem_limit_bytes=48 * mib),
        name="weight_grad",
    )(where, turned, *blocks)


def grad_states_kernel(where, gq_ref, gkv_ref, q_ref, q_theirs_ref, kv_ref, kv_theirs_ref, out_ref):
    core = where[1]
    own_rows, group = 40, 640
    transposed = (((1,), (1,)), ((), ()))

    def product(q, kv, i):
        part = slice(i * group, (i + 1) * group)
        return lax.dot_general(
            q[part], gq_ref[...], transposed, preferred_element_type=f32
        ) + lax.dot_general(kv[part], gkv_ref[...], transposed, preferred_element_type=f32)

    for i in range(q_ref.shape[0] // group):
        mine, theirs = product(q_ref, kv_ref, i), product(q_theirs_ref, kv_theirs_ref, i)
        sides = (jnp.where(core == 0, mine, theirs), jnp.where(core == 0, theirs, mine))
        rows = jnp.concatenate(
            [side[j : j + own_rows] for j in range(0, group, own_rows) for side in sides], axis=0
        )
        out_ref[:, 2 * i * group : 2 * (i + 1) * group] = rows.astype(bf16).T


def finish_kernel(parts_ref, key_ref, value_ref, gain_q_ref, gain_k_ref):
    sums = jnp.sum(parts_ref[...].astype(f32), axis=0)
    rows = key_ref.shape[0]
    key_ref[...] = sums[:rows, :span]
    value_ref[...] = sums[:rows, span:]
    gains = sums[rows:, :span] + sums[rows:, span:]
    gain_q_ref[...] = gains[0:1]
    gain_k_ref[...] = gains[1:2]


def call(kernel, shapes, *args, name, cost=None):
    return pl.pallas_call(
        kernel,
        out_shape=shapes,
        in_specs=[smem if a.dtype == jnp.int32 else vmem for a in args],
        out_specs=jax.tree.map(lambda _: vmem, shapes),
        compiler_params=pltpu.CompilerParams(vmem_limit_bytes=48 * mib),
        cost_estimate=cost,
        name=name,
    )(*args)


plane = ("x", "z")
column = ("y_hi", "y_lo")
chips = plane + column
swapped = [(0, 0), (1, 2), (2, 1), (3, 3)]
flipped = [(0, 1), (1, 0)]


def swap(array):
    return lax.ppermute(array, ("y_hi", "core"), swapped)


def flip(array):
    return lax.ppermute(array, "core", flipped)


def to_all(array, axes, count):
    return lax.all_to_all(jnp.broadcast_to(array[None], (count,) + array.shape), axes, 0, 0)


def ring(array, step):
    return lax.ppermute(array, column, [(i, (i - step) % 4) for i in range(4)])


def around(array):
    mine = [array] + [ring(array, k) for k in range(1, 4)]
    return mine + [flip(a) for a in mine]


def local(hidden_states, block_order, w_query, w_key, w_value, gain_query, gain_key, cotangent):
    tokens = hidden_states[0]
    tok_rows, width = tokens.shape
    q_cols = w_query.shape[1]
    kv_cols = 2 * span
    own_rows = w_query.shape[0]
    planes, columns = 16, 4
    half = width // 2
    place = lax.axis_index("x") * 4 + lax.axis_index("z")
    y_hi, core = lax.axis_index("y_hi"), lax.axis_index("core")
    y = y_hi * 2 + lax.axis_index("y_lo")
    where = jnp.stack([y, core]).astype(jnp.int32)
    offsets = jnp.arange(span, dtype=jnp.int32)

    def angles_of(part):
        blocks = lax.dynamic_slice_in_dim(block_order, 2 * (place * 2 + part), 2)
        positions = (blocks[:, None] * span + offsets[None, :]).reshape(tok_rows)
        return blocks, rotation(positions, span)

    _, (cosine, sine) = angles_of(y_hi)
    own_blocks, (cos_there, sin_there) = angles_of(core)
    own = jnp.concatenate([own_blocks, core[None].astype(jnp.int32)])
    gain_q, gain_k = gain_query[None, :], gain_key[None, :]
    shape = jax.ShapeDtypeStruct

    q_mine = lax.all_gather(w_query, chips, axis=0, tiled=True)
    kv_mine = to_all(jnp.concatenate([w_key, w_value], axis=1), chips, planes * columns)
    kv_mine = kv_mine.reshape(half, kv_cols)

    toks_mine, toks_theirs, turned = pl.pallas_call(
        prepare_kernel,
        out_shape=(shape((tok_rows, half), bf16),) * 2 + (shape((2 * columns, width // 8, tok_rows), bf16),),
        in_specs=[smem, vmem],
        out_specs=(vmem,) * 3,
        compiler_params=pltpu.CompilerParams(vmem_limit_bytes=48 * mib),
        name="prepare",
    )(where, tokens.T.reshape(planes, columns, 2, own_rows, tok_rows))

    toks_other = flip(toks_theirs)
    kv_mine, toks_mine, toks_theirs, turned, cosine, sine, cos_there, sin_there, own = (
        lax.optimization_barrier(
            (kv_mine, toks_mine, toks_theirs, turned, cosine, sine, cos_there, sin_there, own)
        )
    )
    kv_theirs = flip(kv_mine)

    kv16, raw_k = call(
        key_value_kernel,
        (shape((tok_rows, kv_cols), bf16), shape((tok_rows, span), f32)),
        toks_mine, toks_theirs, kv_mine, kv_theirs, gain_k, cosine, sine,
        name="key_value",
    )
    kv_send = jnp.broadcast_to(swap(kv16)[None], (planes, tok_rows, kv_cols))
    q_mine, _ = lax.optimization_barrier((q_mine, kv_send))
    kv_own = lax.all_to_all(kv_send, plane, 0, 0)
    cheap = pl.CostEstimate(flops=1000, bytes_accessed=1000, transcendentals=0)
    q_part, q_part_other = call(
        query_part_kernel,
        (shape((tok_rows, q_cols), f32),) * 2,
        toks_mine, toks_other, q_mine,
        name="query_part",
        cost=cheap,
    )
    kv_own, q_part, q_part_other, grad_out = lax.optimization_barrier(
        (kv_own, q_part, q_part_other, swap(cotangent[0]))
    )
    q16, raw_q = call(
        query_kernel,
        (shape((tok_rows, q_cols), bf16),) * 2,
        q_part, flip(q_part_other), gain_q, cosine, sine,
        name="query",
        cost=cheap,
    )
    kv_other = flip(kv_own)
    q16 = swap(q16)
    turned, raw_q, _ = lax.optimization_barrier((turned, raw_q, q16))
    turned = lax.all_to_all(turned, column + ("core",), 0, 0)
    raw_there = swap(jnp.concatenate([raw_q, raw_k.astype(bf16)], axis=1))

    ctx, dq, dkv_mine, dkv_theirs = attention(
        block_order, own, q16, grad_out, kv_own, kv_other
    )
    q_theirs = flip(q_mine)
    dkv_theirs, dq, turned, raw_there, q_theirs = lax.optimization_barrier(
        (dkv_theirs, dq, turned, raw_there, q_theirs)
    )
    dkv = (dkv_mine.astype(f32) + flip(dkv_theirs).astype(f32)).astype(bf16)
    dkv = lax.all_to_all(dkv, plane, 0, 0)

    g_q, gains_q = call(
        grad_query_kernel,
        (shape((tok_rows, q_cols), bf16), shape((8, span), f32)),
        raw_there[:, :q_cols], dq, gain_q, cos_there, sin_there,
        name="grad_query",
    )
    parts = weight_grad(where, turned, around(g_q), planes, own_rows)
    parts = lax.all_to_all(parts, plane, 0, 0)
    own_query = jnp.sum(parts.astype(f32), axis=0)

    g_kv = call(
        grad_key_value_kernel,
        shape((tok_rows + 16, kv_cols), bf16),
        raw_there[:, q_cols:], dkv, gain_k, cos_there, sin_there, gains_q,
        name="grad_key_value",
    )
    blocks, g_q_back = lax.optimization_barrier((around(g_kv), swap(g_q)))
    parts = weight_grad(where, turned, blocks, planes, own_rows + 8)
    parts = lax.all_to_all(parts, plane, 0, 0)
    own_key, own_value, gain_sum_q, gain_sum_k = call(
        finish_kernel,
        (shape((own_rows, span), f32),) * 2 + (shape((1, span), f32),) * 2,
        parts,
        name="finish",
    )

    grad_states = call(
        grad_states_kernel,
        shape((tok_rows, width), bf16),
        where, g_q_back, swap(g_kv[:tok_rows]), q_mine, q_theirs, kv_mine, kv_theirs,
        name="grad_states",
    )
    return (
        swap(ctx)[None],
        grad_states[None],
        own_query,
        own_key,
        own_value,
        gain_sum_q[0],
        gain_sum_k[0],
    )


def solution(mesh):
    fine = Mesh(mesh.devices.reshape(4, 4, 2, 2, 2), ("x", "z", "y_hi", "y_lo", "core"))
    ctx, dp = ("x", "z", "y_hi"), ("y_lo", "core")
    rows = P(ctx + dp, None)
    tokens = P(dp, ctx, None)
    in_specs = (tokens, P(), rows, rows, rows, P(), P(), tokens)
    out_specs = (tokens, tokens, rows, rows, rows, P(), P())
    return jax.shard_map(local, mesh=fine, in_specs=in_specs, out_specs=out_specs, check_vma=False)
```

```python
import functools
import math

import jax
import jax.numpy as jnp
from jax import lax
from jax.experimental import pallas as pl
from jax.experimental.pallas import tpu as pltpu
from jax.sharding import Mesh
from jax.sharding import PartitionSpec as P

bf16, f32 = jnp.bfloat16, jnp.float32
theta = 1000000.0
floor_score = -1e30
span = 128
chunk = 512
per_chunk = chunk // span
mib = 2**20
smem = pl.BlockSpec(memory_space=pltpu.SMEM)
vmem = pl.BlockSpec(memory_space=pltpu.VMEM)


def mm(a, b):
    return jnp.dot(a, b, preferred_element_type=f32)


def rotation(positions, head_width):
    steps_half = jnp.arange(head_width // 2, dtype=f32)
    inverse = jnp.power(f32(theta), -2.0 * steps_half / head_width)
    angles = positions.astype(f32)[:, None] * inverse[None, :]
    cosine = jnp.cos(angles)
    sine = jnp.sin(angles)
    return jnp.concatenate([cosine, cosine], 1), jnp.concatenate([-sine, sine], 1)


def inverse_norm(raw):
    return lax.rsqrt(jnp.mean(raw * raw, axis=-1, keepdims=True) + 1e-06)


def shape_head(raw, gain, cosine, sine):
    normed = raw * inverse_norm(raw) * gain
    return normed * cosine + pltpu.roll(normed, span // 2, 1) * sine


def shape_head_grad(raw, gain, cosine, sine, grad):
    inverse = inverse_norm(raw)
    grad_normed = grad * cosine + pltpu.roll(grad * sine, span // 2, 1)
    grad_unit = grad_normed * gain
    unit = raw * inverse
    shrink = jnp.mean(grad_unit * unit, axis=-1, keepdims=True)
    return inverse * (grad_unit - unit * shrink), grad_normed * unit


def prepare_kernel(where, src_ref, toks_ref, toks_theirs_ref, turned_ref):
    sizes = src_ref.shape[:3]
    core = where[1]

    def rows(y, side):
        pieces = [src_ref[x, z, y, side].astype(f32) for z in range(sizes[1]) for x in range(sizes[0])]
        return jnp.concatenate(pieces, axis=0).astype(bf16)

    for y in range(sizes[2]):
        toks_ref[y] = rows(y, core).T
        toks_theirs_ref[y] = rows(y, 1 - core).T
        for side in range(2):
            turned_ref[2 * y + side] = rows(y, side)


def key_value_kernel(mine_ref, other_ref, w_ref, w_other_ref, gain_ref, cos_ref, sin_ref, kv_ref, raw_ref):
    raw = sum(mm(mine_ref[y], w_ref[y]) + mm(other_ref[y], w_other_ref[y]) for y in range(w_ref.shape[0]))
    raw_ref[...] = raw[:, :span]
    kv_ref[:, :span] = shape_head(raw[:, :span], gain_ref[...], cos_ref[...], sin_ref[...]).astype(bf16)
    kv_ref[:, span:] = raw[:, span:].astype(bf16)


def query_part_kernel(mine_ref, other_ref, w_ref, w_upper_ref, part_ref, part_other_ref):
    cols = w_ref.shape[2]
    for toks_ref, out_ref in ((mine_ref, part_ref), (other_ref, part_other_ref)):
        for i, w in enumerate((w_ref, w_upper_ref)):
            out_ref[:, i * cols : (i + 1) * cols] = sum(
                mm(toks_ref[y], w[y]) for y in range(w.shape[0])
            )


def query_kernel(part_ref, part_theirs_ref, gain_ref, cos_ref, sin_ref, q_ref, raw_ref):
    gain = gain_ref[...] * (span**-0.5 / math.log(2.0))
    for h in range(raw_ref.shape[1] // span):
        part = slice(h * span, (h + 1) * span)
        raw = part_ref[:, part] + part_theirs_ref[:, part]
        raw_ref[:, part] = raw.astype(bf16)
        q_ref[:, part] = shape_head(raw, gain, cos_ref[...], sin_ref[...]).astype(bf16)


def attention_kernel(
    order, own, q_ref, g_ref, kv_ref, kv_other_ref, ctx_ref, dq_ref, dkv_ref, dkv_other_ref,
    slot_of, ks, vs, kt, vt, acc_kv, qs, gs, qt, gt, acc_o, row_max, row_sum, row_delta, acc_q,
):
    spans, heads = order.shape[0], q_ref.shape[1] // span
    chunks = spans // per_chunk
    rows = heads * span
    core = own[2]

    def place(slot, carry):
        slot_of[order[slot]] = slot
        return carry

    lax.fori_loop(0, spans, place, 0)

    def arrange(c, carry):
        for j in range(per_chunk):
            slot = slot_of[c * per_chunk + j]
            pair, rows_at = slot // 4, pl.multiple_of(slot % 2 * span, span)
            mine = (slot // 2) % 2 == core
            both = jnp.where(
                mine, kv_ref[pair, pl.ds(rows_at, span), :], kv_other_ref[pair, pl.ds(rows_at, span), :]
            )
            part = slice(j * span, (j + 1) * span)
            ks[c, part, :] = both[:, :span]
            vs[c, part, :] = both[:, span:]
            kt[c, :, part] = both[:, :span].T
            vt[c, :, part] = both[:, span:].T
        acc_kv[c] = jnp.zeros_like(acc_kv[c])
        return carry

    lax.fori_loop(0, chunks, arrange, 0)

    first_upper = own[0] > own[1]
    for upper in (True, False):
        which = jnp.where(first_upper, 0, 1) if upper else jnp.where(first_upper, 1, 0)
        block = own[which]
        row0 = pl.multiple_of(which * span, span)
        last = block // per_chunk
        for h in range(heads):
            part = slice(h * span, (h + 1) * span)
            qh = q_ref[pl.ds(row0, span), part]
            gh = g_ref[pl.ds(row0, span), part]
            qs[part, :] = qh
            gs[part, :] = gh
            qt[:, part] = qh.T
            gt[:, part] = gh.T

        def allowed(c):
            key_pos = c * chunk + lax.broadcasted_iota(jnp.int32, (chunk, rows), 0)
            row = lax.broadcasted_iota(jnp.int32, (chunk, rows), 1)
            return key_pos <= block * span + jnp.bitwise_and(row, span - 1)

        row_max[...] = jnp.full_like(row_max, floor_score)
        row_sum[...] = jnp.zeros_like(row_sum)
        acc_o[...] = jnp.zeros_like(acc_o)

        def forward(c, masked):
            s = mm(ks[c], qt[...])
            if masked:
                s = jnp.where(allowed(c), s, floor_score)
            old = row_max[...]
            new = jnp.maximum(old, jnp.max(s, axis=0, keepdims=True))
            p = jnp.exp2(s - new)
            alpha = jnp.exp2(old - new)
            row_max[...] = new
            row_sum[...] = row_sum[...] * alpha + jnp.sum(p, axis=0, keepdims=True)
            acc_o[...] = acc_o[...] * alpha + mm(vt[c], p.astype(bf16))

        def forward_step(c, carry):
            forward(c, False)
            return carry

        lax.fori_loop(0, last, forward_step, 0)
        forward(last, True)

        total = row_sum[...]
        ctx_t = (acc_o[...] / total).astype(bf16)
        row_max[...] = row_max[...] + jnp.log2(total)
        row_delta[...] = jnp.sum(ctx_t.astype(f32) * gt[...].astype(f32), axis=0, keepdims=True)
        for h in range(heads):
            part = slice(h * span, (h + 1) * span)
            ctx_ref[pl.ds(row0, span), part] = ctx_t[:, part].T
        acc_q[...] = jnp.zeros_like(acc_q)

        def backward(c, masked):
            s = mm(ks[c], qt[...])
            p = jnp.exp2(s - row_max[...])
            if masked:
                p = jnp.where(allowed(c), p, 0.0)
            dp = mm(vs[c], gt[...])
            ds = (p * (dp - row_delta[...])).astype(bf16)
            acc_kv[c, :, span:] += mm(p.astype(bf16), gs[...])
            acc_kv[c, :, :span] += mm(ds, qs[...])
            acc_q[...] += mm(kt[c], ds)

        def backward_step(c, carry):
            backward(c, False)
            return carry

        lax.fori_loop(0, last, backward_step, 0)
        backward(last, True)
        for h in range(heads):
            part = slice(h * span, (h + 1) * span)
            dq_ref[pl.ds(row0, span), part] = acc_q[:, part].T * (span**-0.5)

    def give(c, carry):
        for j in range(per_chunk):
            part = slice(j * span, (j + 1) * span)
            slot = slot_of[c * per_chunk + j]
            pair, rows_at = slot // 4, pl.multiple_of(slot % 2 * span, span)
            mine = (slot // 2) % 2 == core
            dk = (acc_kv[c, part, :span] * math.log(2.0)).astype(bf16)
            dv = acc_kv[c, part, span:].astype(bf16)

            @pl.when(mine)
            def _():
                dkv_ref[pair, pl.ds(rows_at, span), :span] = dk
                dkv_ref[pair, pl.ds(rows_at, span), span:] = dv

            @pl.when(jnp.logical_not(mine))
            def _():
                dkv_other_ref[pair, pl.ds(rows_at, span), :span] = dk
                dkv_other_ref[pair, pl.ds(rows_at, span), span:] = dv

        return carry

    lax.fori_loop(0, chunks, give, 0)


def attention(order, own, q16, g16, kv, kv_other):
    rows_here, cols = q16.shape
    spans = order.shape[0]
    chunks = spans // per_chunk
    rows = cols
    share = jax.ShapeDtypeStruct(kv.shape, bf16)
    return pl.pallas_call(
        attention_kernel,
        out_shape=(
            jax.ShapeDtypeStruct((rows_here, cols), bf16),
            jax.ShapeDtypeStruct((rows_here, cols), f32),
            share,
            share,
        ),
        in_specs=[smem, smem] + [vmem] * 4,
        out_specs=(vmem,) * 4,
        scratch_shapes=[
            pltpu.SMEM((spans,), jnp.int32),
            pltpu.VMEM((chunks, chunk, span), bf16),
            pltpu.VMEM((chunks, chunk, span), bf16),
            pltpu.VMEM((chunks, span, chunk), bf16),
            pltpu.VMEM((chunks, span, chunk), bf16),
            pltpu.VMEM((chunks, chunk, 2 * span), f32),
            pltpu.VMEM((rows, span), bf16),
            pltpu.VMEM((rows, span), bf16),
            pltpu.VMEM((span, rows), bf16),
            pltpu.VMEM((span, rows), bf16),
            pltpu.VMEM((span, rows), f32),
            pltpu.VMEM((1, rows), f32),
            pltpu.VMEM((1, rows), f32),
            pltpu.VMEM((1, rows), f32),
            pltpu.VMEM((span, rows), f32),
        ],
        compiler_params=pltpu.CompilerParams(vmem_limit_bytes=48 * mib),
        cost_estimate=cheap,
        name="attention",
    )(order, own, q16, g16, kv, kv_other)


def grad_query_kernel(raw_ref, dq_ref, gain_ref, cos_ref, sin_ref, g_ref, gain_out):
    cosine, sine = cos_ref[...], sin_ref[...]
    sums = jnp.zeros((1, span), f32)
    for h in range(dq_ref.shape[1] // span):
        part = slice(h * span, (h + 1) * span)
        grad, terms = shape_head_grad(
            raw_ref[:, part].astype(f32), gain_ref[...], cosine, sine, dq_ref[:, part]
        )
        g_ref[:, part] = grad.astype(bf16)
        sums = sums + jnp.sum(terms, axis=0, keepdims=True)
    gain_out[...] = jnp.broadcast_to(sums, gain_out.shape)


def grad_key_value_kernel(raw_ref, dkv_ref, gain_ref, cos_ref, sin_ref, gain_q_ref, g_ref):
    rows = raw_ref.shape[0]
    dkv = jnp.sum(dkv_ref[...].astype(f32), axis=0)
    grad, terms = shape_head_grad(
        raw_ref[...].astype(f32), gain_ref[...], cos_ref[...], sin_ref[...], dkv[:, :span]
    )
    g_ref[:rows, :span] = grad.astype(bf16)
    g_ref[:rows, span:] = dkv[:, span:].astype(bf16)
    gain_k = jnp.sum(terms, axis=0, keepdims=True)
    split = []
    for gain in (gain_q_ref[0:1], gain_k):
        high = gain.astype(bf16).astype(f32)
        split.append(jnp.concatenate([high, gain - high], axis=1))
    row = lax.broadcasted_iota(jnp.int32, (g_ref.shape[0] - rows, 2 * span), 0)
    g_ref[rows:] = jnp.where(row == 0, split[0], jnp.where(row == 1, split[1], 0.0)).astype(bf16)


def weight_grad_kernel(where, turned_ref, *rest):
    blocks, out_ref = rest[:-1], rest[-1]
    columns = len(blocks) // 2
    toks = turned_ref.shape[2]
    y, core = where[0], where[1]
    total, gains = None, None
    for side in range(2):
        for k in range(columns):
            from_y = lax.rem(y + k, columns)
            from_core = core if side == 0 else 1 - core
            at = (from_core * 2 + lax.rem(from_y, 2)) * 2 + from_y // 2
            block = blocks[side * columns + k]
            part = mm(turned_ref[at], block[:toks])
            total = part if total is None else total + part
            if block.shape[0] > toks:
                row = block[toks:].astype(f32)
                gains = row if gains is None else gains + row
    own_rows = total.shape[0] // out_ref.shape[0]
    extra = []
    if gains is not None:
        gain = gains[:, :span] + gains[:, span:]
        high = gain.astype(bf16).astype(f32)
        extra = [jnp.concatenate([high, gain - high], axis=1)[:8]]
    for i in range(out_ref.shape[0]):
        part = total[i * own_rows : (i + 1) * own_rows]
        out_ref[i] = jnp.concatenate([part] + extra, axis=0).astype(bf16)


def weight_grad(where, turned, blocks, planes, padded):
    return pl.pallas_call(
        weight_grad_kernel,
        out_shape=jax.ShapeDtypeStruct((planes, padded, blocks[0].shape[1]), bf16),
        in_specs=[smem] + [vmem] * (1 + len(blocks)),
        out_specs=vmem,
        compiler_params=pltpu.CompilerParams(vmem_limit_bytes=48 * mib),
        cost_estimate=cheap,
        name="weight_grad",
    )(where, turned, *blocks)


def grad_states_kernel(
    where, gq_ref, gkv_ref, kv_ref, kv_theirs_ref, q_ref, q_theirs_ref, upper_ref, upper_theirs_ref, out_ref, blocks,
):
    core = where[1]
    columns, cols = kv_ref.shape[0], kv_ref.shape[2]
    own_rows = 40
    grads = (gkv_ref[...], gq_ref[:, :cols], gq_ref[:, cols:])
    sides = ((core, (kv_ref, q_ref, upper_ref)), (1 - core, (kv_theirs_ref, q_theirs_ref, upper_theirs_ref)))
    for at_core, weights in sides:
        for y in range(columns):
            blocks[y, at_core] = sum(
                lax.dot_general(w[y], grad, (((1,), (1,)), ((), ())), preferred_element_type=f32)
                for w, grad in zip(weights, grads)
            )
    for x in range(4):
        pieces = []
        for z in range(4):
            part = slice((z * 4 + x) * own_rows, (z * 4 + x + 1) * own_rows)
            pieces += [blocks[y, c, part] for y in range(columns) for c in range(2)]
        rows = jnp.concatenate(pieces, axis=0)
        out_ref[:, x * rows.shape[0] : (x + 1) * rows.shape[0]] = rows.astype(bf16).T


def finish_kernel(parts_ref, key_ref, value_ref, gain_q_ref, gain_k_ref):
    sums = jnp.sum(parts_ref[...].astype(f32), axis=0)
    rows = key_ref.shape[0]
    key_ref[...] = sums[:rows, :span]
    value_ref[...] = sums[:rows, span:]
    gains = sums[rows:, :span] + sums[rows:, span:]
    gain_q_ref[...] = gains[0:1]
    gain_k_ref[...] = gains[1:2]


cheap = pl.CostEstimate(flops=1000, bytes_accessed=1000, transcendentals=0)


def call(kernel, shapes, *args, name):
    return pl.pallas_call(
        kernel,
        out_shape=shapes,
        in_specs=[smem if a.dtype == jnp.int32 else vmem for a in args],
        out_specs=jax.tree.map(lambda _: vmem, shapes),
        compiler_params=pltpu.CompilerParams(vmem_limit_bytes=48 * mib),
        cost_estimate=cheap,
        name=name,
    )(*args)


plane = ("x", "z")
owners = ("z", "x")
column = ("y_hi", "y_lo")
chips = column + owners
swapped = [(0, 0), (1, 2), (2, 1), (3, 3)]
flipped = [(0, 1), (1, 0)]


def swap(array):
    return lax.ppermute(array, ("y_hi", "core"), swapped)


def flip(array):
    return lax.ppermute(array, "core", flipped)


def to_all(array, axes, count):
    return lax.all_to_all(jnp.broadcast_to(array[None], (count,) + array.shape), axes, 0, 0)


def ring(array, step):
    return lax.ppermute(array, column, [(i, (i - step) % 4) for i in range(4)])


def place_kernel(axis, where, *refs):
    out_ref = refs[-1]
    inner = out_ref.shape[:axis]
    for k, block in enumerate(refs[:-1]):
        at = lax.rem(where[0] + k, 4)
        if axis == 0:
            out_ref[at] = block[...]
        elif axis == 1:
            for i in range(inner[0]):
                out_ref[i, at] = block[i]
        else:
            for i in range(inner[0]):
                for j in range(inner[1]):
                    out_ref[i, j, at] = block[i, j]


def collect(array, name, axis):
    parts = [array] + [
        lax.ppermute(array, name, [(i, (i - k) % 4) for i in range(4)]) for k in range(1, 4)
    ]
    where = lax.axis_index(name).astype(jnp.int32)[None]
    shape = array.shape[:axis] + (4,) + array.shape[axis:]
    return call(
        functools.partial(place_kernel, axis), jax.ShapeDtypeStruct(shape, bf16), where, *parts, name="place"
    )


def around(array):
    mine = [array] + [ring(array, k) for k in range(1, 4)]
    return mine + [flip(a) for a in mine]


def local(hidden_states, block_order, w_query, w_key, w_value, gain_query, gain_key, cotangent):
    tokens = hidden_states[0]
    tok_rows, width = tokens.shape
    q_cols = w_query.shape[1]
    kv_cols = 2 * span
    own_rows = w_query.shape[0]
    planes, columns = 16, 4
    half = width // 2
    place = lax.axis_index("x") * 4 + lax.axis_index("z")
    y_hi, core = lax.axis_index("y_hi"), lax.axis_index("core")
    y = y_hi * 2 + lax.axis_index("y_lo")
    where = jnp.stack([y, core]).astype(jnp.int32)
    offsets = jnp.arange(span, dtype=jnp.int32)

    def angles_of(part):
        blocks = lax.dynamic_slice_in_dim(block_order, 2 * (place * 2 + part), 2)
        positions = (blocks[:, None] * span + offsets[None, :]).reshape(tok_rows)
        return blocks, rotation(positions, span)

    _, (cosine, sine) = angles_of(y_hi)
    own_blocks, (cos_there, sin_there) = angles_of(core)
    own = jnp.concatenate([own_blocks, core[None].astype(jnp.int32)])
    gain_q, gain_k = gain_query[None, :], gain_key[None, :]
    shape = jax.ShapeDtypeStruct

    w_kv = jnp.concatenate([w_key, w_value], axis=1)
    kv_mine, q_low = collect(w_kv, "x", 0), collect(w_query[:, :kv_cols], column, 0)
    kv_mine, q_low = lax.optimization_barrier((kv_mine, q_low))
    kv_mine, q_low = collect(kv_mine, column, 0), collect(q_low, "z", 1)
    q_high = collect(w_query[:, kv_cols:], "z", 0)
    kv_mine, q_low, q_high = lax.optimization_barrier((kv_mine, q_low, q_high))
    kv_mine, q_low = collect(kv_mine, "z", 1), collect(q_low, "x", 2)
    q_high = collect(q_high, "x", 1)
    kv_mine, q_low, q_high = lax.optimization_barrier((kv_mine, q_low, q_high))
    q_high = collect(q_high, column, 0)
    by_y = (columns, half // columns, kv_cols)
    kv_mine, q_low, q_high = kv_mine.reshape(by_y), q_low.reshape(by_y), q_high.reshape(by_y)

    toks_mine, toks_theirs, turned = pl.pallas_call(
        prepare_kernel,
        out_shape=(shape((columns, tok_rows, half // columns), bf16),) * 2
        + (shape((2 * columns, half // columns, tok_rows), bf16),),
        in_specs=[smem, vmem],
        out_specs=(vmem,) * 3,
        compiler_params=pltpu.CompilerParams(vmem_limit_bytes=48 * mib),
        cost_estimate=cheap,
        name="prepare",
    )(where, tokens.T.reshape(4, 4, columns, 2, own_rows, tok_rows))

    toks_other = flip(toks_theirs)
    kv_mine, toks_mine, toks_theirs, turned, cosine, sine, cos_there, sin_there, own = (
        lax.optimization_barrier(
            (kv_mine, toks_mine, toks_theirs, turned, cosine, sine, cos_there, sin_there, own)
        )
    )
    kv_theirs = flip(kv_mine)

    kv16, raw_k = call(
        key_value_kernel,
        (shape((tok_rows, kv_cols), bf16), shape((tok_rows, span), f32)),
        toks_mine, toks_theirs, kv_mine, kv_theirs, gain_k, cosine, sine,
        name="key_value",
    )
    kv_send = jnp.broadcast_to(swap(kv16)[None], (planes, tok_rows, kv_cols))
    kv_own = lax.all_to_all(kv_send, plane, 0, 0)
    q_part, q_part_other = call(
        query_part_kernel,
        (shape((tok_rows, q_cols), f32),) * 2,
        toks_mine, toks_other, q_low, q_high,
        name="query_part",
    )
    kv_own, q_part, q_part_other, grad_out = lax.optimization_barrier(
        (kv_own, q_part, q_part_other, swap(cotangent[0]))
    )
    q16, raw_q = call(
        query_kernel,
        (shape((tok_rows, q_cols), bf16),) * 2,
        q_part, flip(q_part_other), gain_q, cosine, sine,
        name="query",
    )
    kv_other = flip(kv_own)
    q16 = swap(q16)
    turned, raw_q, _ = lax.optimization_barrier((turned, raw_q, q16))
    turned = lax.all_to_all(turned, column + ("core",), 0, 0)
    raw_there = swap(jnp.concatenate([raw_q, raw_k.astype(bf16)], axis=1))

    ctx, dq, dkv_mine, dkv_theirs = attention(
        block_order, own, q16, grad_out, kv_own, kv_other
    )
    dkv_theirs, dq, turned, raw_there, low_theirs, high_theirs = lax.optimization_barrier(
        (dkv_theirs, dq, turned, raw_there, flip(q_low), flip(q_high))
    )
    dkv = (dkv_mine.astype(f32) + flip(dkv_theirs).astype(f32)).astype(bf16)
    dkv = lax.all_to_all(dkv, plane, 0, 0)

    g_q, gains_q = call(
        grad_query_kernel,
        (shape((tok_rows, q_cols), bf16), shape((8, span), f32)),
        raw_there[:, :q_cols], dq, gain_q, cos_there, sin_there,
        name="grad_query",
    )
    parts = weight_grad(where, turned, around(g_q), planes, own_rows)
    parts = lax.all_to_all(parts, owners, 0, 0)
    own_query = jnp.sum(parts.astype(f32), axis=0)

    g_kv = call(
        grad_key_value_kernel,
        shape((tok_rows + 16, kv_cols), bf16),
        raw_there[:, q_cols:], dkv, gain_k, cos_there, sin_there, gains_q,
        name="grad_key_value",
    )
    blocks, g_q_back, g_kv_back = lax.optimization_barrier((around(g_kv), swap(g_q), swap(g_kv)))
    parts = weight_grad(where, turned, blocks, planes, own_rows + 8)
    parts = lax.all_to_all(parts, owners, 0, 0)
    own_key, own_value, gain_sum_q, gain_sum_k = call(
        finish_kernel,
        (shape((own_rows, span), f32),) * 2 + (shape((1, span), f32),) * 2,
        parts,
        name="finish",
    )

    grad_states = pl.pallas_call(
        grad_states_kernel,
        out_shape=shape((tok_rows, width), bf16),
        in_specs=[smem] + [vmem] * 8,
        out_specs=vmem,
        scratch_shapes=[pltpu.VMEM((columns, 2, half // columns, tok_rows), f32)],
        compiler_params=pltpu.CompilerParams(vmem_limit_bytes=48 * mib),
        cost_estimate=cheap,
        name="grad_states",
    )(where, g_q_back, g_kv_back[:tok_rows], kv_mine, kv_theirs, q_low, low_theirs, q_high, high_theirs)
    return (
        swap(ctx)[None],
        grad_states[None],
        own_query,
        own_key,
        own_value,
        gain_sum_q[0],
        gain_sum_k[0],
    )


def solution(mesh):
    fine = Mesh(mesh.devices.reshape(4, 4, 2, 2, 2), ("x", "z", "y_hi", "y_lo", "core"))
    ctx, dp = ("x", "z", "y_hi"), ("y_lo", "core")
    rows = P(ctx + dp, None)
    tokens = P(dp, ctx, None)
    in_specs = (tokens, P(), rows, rows, rows, P(), P(), tokens)
    out_specs = (tokens, tokens, rows, rows, rows, P(), P())
    return jax.shard_map(local, mesh=fine, in_specs=in_specs, out_specs=out_specs, check_vma=False)
```

```python
import math

import jax
import jax.numpy as jnp
from jax import lax
from jax.experimental import pallas as pl
from jax.experimental.pallas import tpu as pltpu
from jax.sharding import Mesh
from jax.sharding import PartitionSpec as P

bf16, f32 = jnp.bfloat16, jnp.float32
theta = 1000000.0
floor_score = -1e30
span = 128
chunk = 512
per_chunk = chunk // span
mib = 2**20
smem = pl.BlockSpec(memory_space=pltpu.SMEM)
vmem = pl.BlockSpec(memory_space=pltpu.VMEM)


def mm(a, b):
    return jnp.dot(a, b, preferred_element_type=f32)


def rotation(positions, head_width):
    steps_half = jnp.arange(head_width // 2, dtype=f32)
    inverse = jnp.power(f32(theta), -2.0 * steps_half / head_width)
    angles = positions.astype(f32)[:, None] * inverse[None, :]
    cosine = jnp.cos(angles)
    sine = jnp.sin(angles)
    return jnp.concatenate([cosine, cosine], 1), jnp.concatenate([-sine, sine], 1)


def inverse_norm(raw):
    return lax.rsqrt(jnp.mean(raw * raw, axis=-1, keepdims=True) + 1e-06)


def shape_head(raw, gain, cosine, sine):
    normed = raw * inverse_norm(raw) * gain
    return normed * cosine + pltpu.roll(normed, span // 2, 1) * sine


def shape_head_grad(raw, gain, cosine, sine, grad):
    inverse = inverse_norm(raw)
    grad_normed = grad * cosine + pltpu.roll(grad * sine, span // 2, 1)
    grad_unit = grad_normed * gain
    unit = raw * inverse
    shrink = jnp.mean(grad_unit * unit, axis=-1, keepdims=True)
    return inverse * (grad_unit - unit * shrink), grad_normed * unit


def prepare_kernel(where, src_ref, toks_ref, toks_theirs_ref, turned_ref):
    sizes = src_ref.shape[:3]
    core = where[1]

    def rows(y, side):
        pieces = [src_ref[x, z, y, side].astype(f32) for z in range(sizes[1]) for x in range(sizes[0])]
        return jnp.concatenate(pieces, axis=0).astype(bf16)

    for y in range(sizes[2]):
        toks_ref[y] = rows(y, core).T
        toks_theirs_ref[y] = rows(y, 1 - core).T
        for side in range(2):
            turned_ref[2 * y + side] = rows(y, side)


def key_value_kernel(mine_ref, other_ref, w_ref, w_other_ref, gain_ref, cos_ref, sin_ref, kv_ref, raw_ref):
    raw = sum(mm(mine_ref[y], w_ref[y]) + mm(other_ref[y], w_other_ref[y]) for y in range(w_ref.shape[0]))
    raw_ref[...] = raw[:, :span]
    kv_ref[:, :span] = shape_head(raw[:, :span], gain_ref[...], cos_ref[...], sin_ref[...]).astype(bf16)
    kv_ref[:, span:] = raw[:, span:].astype(bf16)


def query_part_kernel(where, mine_ref, other_ref, w0, w1, w2, w3, part_ref, part_other_ref):
    for toks_ref, out_ref in ((mine_ref, part_ref), (other_ref, part_other_ref)):
        total = 0.0
        for k, w in enumerate((w0, w1, w2, w3)):
            total = total + mm(toks_ref[lax.rem(where[0] + k, 4)], w[...])
        out_ref[...] = total


def query_kernel(part_ref, part_theirs_ref, gain_ref, cos_ref, sin_ref, q_ref, raw_ref):
    gain = gain_ref[...] * (span**-0.5 / math.log(2.0))
    for h in range(raw_ref.shape[1] // span):
        part = slice(h * span, (h + 1) * span)
        raw = part_ref[:, part] + part_theirs_ref[:, part]
        raw_ref[:, part] = raw.astype(bf16)
        q_ref[:, part] = shape_head(raw, gain, cos_ref[...], sin_ref[...]).astype(bf16)


def attention_kernel(
    order, own, q_ref, g_ref, kv_ref, kv_other_ref, ctx_ref, dq_ref, dkv_ref, dkv_other_ref,
    slot_of, ks, vs, kt, vt, acc_kv, qs, gs, qt, gt, acc_o, row_max, row_sum, row_delta, acc_q,
):
    spans, heads = order.shape[0], q_ref.shape[1] // span
    chunks = spans // per_chunk
    rows = heads * span
    core = own[2]

    def place(slot, carry):
        slot_of[order[slot]] = slot
        return carry

    lax.fori_loop(0, spans, place, 0)

    def arrange(c, carry):
        for j in range(per_chunk):
            slot = slot_of[c * per_chunk + j]
            pair, rows_at = slot // 4, pl.multiple_of(slot % 2 * span, span)
            mine = (slot // 2) % 2 == core
            both = jnp.where(
                mine, kv_ref[pair, pl.ds(rows_at, span), :], kv_other_ref[pair, pl.ds(rows_at, span), :]
            )
            part = slice(j * span, (j + 1) * span)
            ks[c, part, :] = both[:, :span]
            vs[c, part, :] = both[:, span:]
            kt[c, :, part] = both[:, :span].T
            vt[c, :, part] = both[:, span:].T
        acc_kv[c] = jnp.zeros_like(acc_kv[c])
        return carry

    lax.fori_loop(0, chunks, arrange, 0)

    first_upper = own[0] > own[1]
    for upper in (True, False):
        which = jnp.where(first_upper, 0, 1) if upper else jnp.where(first_upper, 1, 0)
        block = own[which]
        row0 = pl.multiple_of(which * span, span)
        last = block // per_chunk
        for h in range(heads):
            part = slice(h * span, (h + 1) * span)
            qh = q_ref[pl.ds(row0, span), part]
            gh = g_ref[pl.ds(row0, span), part]
            qs[part, :] = qh
            gs[part, :] = gh
            qt[:, part] = qh.T
            gt[:, part] = gh.T

        def allowed(c):
            key_pos = c * chunk + lax.broadcasted_iota(jnp.int32, (chunk, rows), 0)
            row = lax.broadcasted_iota(jnp.int32, (chunk, rows), 1)
            return key_pos <= block * span + jnp.bitwise_and(row, span - 1)

        row_max[...] = jnp.full_like(row_max, floor_score)
        row_sum[...] = jnp.zeros_like(row_sum)
        acc_o[...] = jnp.zeros_like(acc_o)

        def forward(c, masked):
            s = mm(ks[c], qt[...])
            if masked:
                s = jnp.where(allowed(c), s, floor_score)
            old = row_max[...]
            new = jnp.maximum(old, jnp.max(s, axis=0, keepdims=True))
            p = jnp.exp2(s - new)
            alpha = jnp.exp2(old - new)
            row_max[...] = new
            row_sum[...] = row_sum[...] * alpha + jnp.sum(p, axis=0, keepdims=True)
            acc_o[...] = acc_o[...] * alpha + mm(vt[c], p.astype(bf16))

        def forward_step(c, carry):
            forward(c, False)
            return carry

        lax.fori_loop(0, last, forward_step, 0)
        forward(last, True)

        total = row_sum[...]
        ctx_t = (acc_o[...] / total).astype(bf16)
        row_max[...] = row_max[...] + jnp.log2(total)
        row_delta[...] = jnp.sum(ctx_t.astype(f32) * gt[...].astype(f32), axis=0, keepdims=True)
        for h in range(heads):
            part = slice(h * span, (h + 1) * span)
            ctx_ref[pl.ds(row0, span), part] = ctx_t[:, part].T
        acc_q[...] = jnp.zeros_like(acc_q)

        def backward(c, masked):
            s = mm(ks[c], qt[...])
            p = jnp.exp2(s - row_max[...])
            if masked:
                p = jnp.where(allowed(c), p, 0.0)
            dp = mm(vs[c], gt[...])
            ds = (p * (dp - row_delta[...])).astype(bf16)
            acc_kv[c, :, span:] += mm(p.astype(bf16), gs[...])
            acc_kv[c, :, :span] += mm(ds, qs[...])
            acc_q[...] += mm(kt[c], ds)

        def backward_step(c, carry):
            backward(c, False)
            return carry

        lax.fori_loop(0, last, backward_step, 0)
        backward(last, True)
        for h in range(heads):
            part = slice(h * span, (h + 1) * span)
            dq_ref[pl.ds(row0, span), part] = acc_q[:, part].T * (span**-0.5)

    def give(c, carry):
        for j in range(per_chunk):
            part = slice(j * span, (j + 1) * span)
            slot = slot_of[c * per_chunk + j]
            pair, rows_at = slot // 4, pl.multiple_of(slot % 2 * span, span)
            mine = (slot // 2) % 2 == core
            dk = (acc_kv[c, part, :span] * math.log(2.0)).astype(bf16)
            dv = acc_kv[c, part, span:].astype(bf16)

            @pl.when(mine)
            def _():
                dkv_ref[pair, pl.ds(rows_at, span), :span] = dk
                dkv_ref[pair, pl.ds(rows_at, span), span:] = dv

            @pl.when(jnp.logical_not(mine))
            def _():
                dkv_other_ref[pair, pl.ds(rows_at, span), :span] = dk
                dkv_other_ref[pair, pl.ds(rows_at, span), span:] = dv

        return carry

    lax.fori_loop(0, chunks, give, 0)


def attention(order, own, q16, g16, kv, kv_other):
    rows_here, cols = q16.shape
    spans = order.shape[0]
    chunks = spans // per_chunk
    rows = cols
    share = jax.ShapeDtypeStruct(kv.shape, bf16)
    return pl.pallas_call(
        attention_kernel,
        out_shape=(
            jax.ShapeDtypeStruct((rows_here, cols), bf16),
            jax.ShapeDtypeStruct((rows_here, cols), f32),
            share,
            share,
        ),
        in_specs=[smem, smem] + [vmem] * 4,
        out_specs=(vmem,) * 4,
        scratch_shapes=[
            pltpu.SMEM((spans,), jnp.int32),
            pltpu.VMEM((chunks, chunk, span), bf16),
            pltpu.VMEM((chunks, chunk, span), bf16),
            pltpu.VMEM((chunks, span, chunk), bf16),
            pltpu.VMEM((chunks, span, chunk), bf16),
            pltpu.VMEM((chunks, chunk, 2 * span), f32),
            pltpu.VMEM((rows, span), bf16),
            pltpu.VMEM((rows, span), bf16),
            pltpu.VMEM((span, rows), bf16),
            pltpu.VMEM((span, rows), bf16),
            pltpu.VMEM((span, rows), f32),
            pltpu.VMEM((1, rows), f32),
            pltpu.VMEM((1, rows), f32),
            pltpu.VMEM((1, rows), f32),
            pltpu.VMEM((span, rows), f32),
        ],
        compiler_params=pltpu.CompilerParams(vmem_limit_bytes=48 * mib),
        cost_estimate=cheap,
        name="attention",
    )(order, own, q16, g16, kv, kv_other)


def grad_query_kernel(raw_ref, dq_ref, gain_ref, cos_ref, sin_ref, g_ref, gain_out):
    cosine, sine = cos_ref[...], sin_ref[...]
    sums = jnp.zeros((1, span), f32)
    for h in range(dq_ref.shape[1] // span):
        part = slice(h * span, (h + 1) * span)
        grad, terms = shape_head_grad(
            raw_ref[:, part].astype(f32), gain_ref[...], cosine, sine, dq_ref[:, part]
        )
        g_ref[:, part] = grad.astype(bf16)
        sums = sums + jnp.sum(terms, axis=0, keepdims=True)
    gain_out[...] = jnp.broadcast_to(sums, gain_out.shape)


def grad_key_value_kernel(raw_ref, dkv_ref, gain_ref, cos_ref, sin_ref, gain_q_ref, g_ref):
    rows = raw_ref.shape[0]
    dkv = jnp.sum(dkv_ref[...].astype(f32), axis=0)
    grad, terms = shape_head_grad(
        raw_ref[:, -span:].astype(f32), gain_ref[...], cos_ref[...], sin_ref[...], dkv[:, :span]
    )
    g_ref[:rows, :span] = grad.astype(bf16)
    g_ref[:rows, span:] = dkv[:, span:].astype(bf16)
    gain_k = jnp.sum(terms, axis=0, keepdims=True)
    split = []
    for gain in (gain_q_ref[0:1], gain_k):
        high = gain.astype(bf16).astype(f32)
        split.append(jnp.concatenate([high, gain - high], axis=1))
    row = lax.broadcasted_iota(jnp.int32, (g_ref.shape[0] - rows, 2 * span), 0)
    g_ref[rows:] = jnp.where(row == 0, split[0], jnp.where(row == 1, split[1], 0.0)).astype(bf16)


def weight_grad_kernel(where, turned_ref, *rest):
    blocks, out_ref = rest[:-1], rest[-1]
    columns = len(blocks) // 2
    toks = turned_ref.shape[2]
    y, core = where[0], where[1]
    total, gains = None, None
    for side in range(2):
        for k in range(columns):
            from_y = lax.rem(y + k, columns)
            from_core = core if side == 0 else 1 - core
            at = (from_core * 2 + lax.rem(from_y, 2)) * 2 + from_y // 2
            block = blocks[side * columns + k]
            part = mm(turned_ref[at], block[:toks])
            total = part if total is None else total + part
            if block.shape[0] > toks:
                row = block[toks:].astype(f32)
                gains = row if gains is None else gains + row
    own_rows = total.shape[0] // out_ref.shape[0]
    extra = []
    if gains is not None:
        gain = gains[:, :span] + gains[:, span:]
        high = gain.astype(bf16).astype(f32)
        extra = [jnp.concatenate([high, gain - high], axis=1)[:8]]
    for i in range(out_ref.shape[0]):
        part = total[i * own_rows : (i + 1) * own_rows]
        out_ref[i] = jnp.concatenate([part] + extra, axis=0).astype(bf16)


def weight_grad(where, turned, blocks, planes, padded):
    return pl.pallas_call(
        weight_grad_kernel,
        out_shape=jax.ShapeDtypeStruct((planes, padded, blocks[0].shape[1]), bf16),
        in_specs=[smem] + [vmem] * (1 + len(blocks)),
        out_specs=vmem,
        compiler_params=pltpu.CompilerParams(vmem_limit_bytes=48 * mib),
        cost_estimate=cheap,
        name="weight_grad",
    )(where, turned, *blocks)


def grad_states_kernel(where, gq_ref, gkv_ref, kv_ref, kv_theirs_ref, *rest):
    weights, (out_ref, blocks) = rest[:-2], rest[-2:]
    columns = len(weights) // 2
    y, core = where[0], where[1]
    own_rows = 40
    toks = gq_ref.shape[0]
    transposed = (((1,), (1,)), ((), ()))
    for side, kv in ((0, kv_ref), (1, kv_theirs_ref)):
        at_core = core if side == 0 else 1 - core
        for k in range(columns):
            at = lax.rem(y + k, columns)
            blocks[at, at_core] = lax.dot_general(
                weights[side * columns + k][...], gq_ref[...], transposed, preferred_element_type=f32
            ) + lax.dot_general(kv[at], gkv_ref[:toks], transposed, preferred_element_type=f32)
    for x in range(4):
        pieces = []
        for z in range(4):
            part = slice((z * 4 + x) * own_rows, (z * 4 + x + 1) * own_rows)
            pieces += [blocks[at, c, part] for at in range(columns) for c in range(2)]
        rows = jnp.concatenate(pieces, axis=0)
        out_ref[:, x * rows.shape[0] : (x + 1) * rows.shape[0]] = rows.astype(bf16).T


def finish_kernel(parts_ref, key_ref, value_ref, gain_q_ref, gain_k_ref):
    sums = jnp.sum(parts_ref[...].astype(f32), axis=0)
    rows = key_ref.shape[0]
    key_ref[...] = sums[:rows, :span]
    value_ref[...] = sums[:rows, span:]
    gains = sums[rows:, :span] + sums[rows:, span:]
    gain_q_ref[...] = gains[0:1]
    gain_k_ref[...] = gains[1:2]


cheap = pl.CostEstimate(flops=1000, bytes_accessed=1000, transcendentals=0)


def call(kernel, shapes, *args, name):
    return pl.pallas_call(
        kernel,
        out_shape=shapes,
        in_specs=[smem if a.dtype == jnp.int32 else vmem for a in args],
        out_specs=jax.tree.map(lambda _: vmem, shapes),
        compiler_params=pltpu.CompilerParams(vmem_limit_bytes=48 * mib),
        cost_estimate=cheap,
        name=name,
    )(*args)


plane = ("x", "z")
owners = ("z", "x")
column = ("y_hi", "y_lo")
chips = column + owners
swapped = [(0, 0), (1, 2), (2, 1), (3, 3)]
flipped = [(0, 1), (1, 0)]


def swap(array):
    return lax.ppermute(array, ("y_hi", "core"), swapped)


def flip(array):
    return lax.ppermute(array, "core", flipped)


def to_all(array, axes, count):
    return lax.all_to_all(jnp.broadcast_to(array[None], (count,) + array.shape), axes, 0, 0)


def ring(array, step):
    return lax.ppermute(array, column, [(i, (i - step) % 4) for i in range(4)])


def around(array):
    mine = [array] + [ring(array, k) for k in range(1, 4)]
    return mine + [flip(a) for a in mine]


def local(hidden_states, block_order, w_query, w_key, w_value, gain_query, gain_key, cotangent):
    tokens = hidden_states[0]
    tok_rows, width = tokens.shape
    q_cols = w_query.shape[1]
    kv_cols = 2 * span
    own_rows = w_query.shape[0]
    planes, columns = 16, 4
    half = width // 2
    place = lax.axis_index("x") * 4 + lax.axis_index("z")
    y_hi, core = lax.axis_index("y_hi"), lax.axis_index("core")
    y = y_hi * 2 + lax.axis_index("y_lo")
    where = jnp.stack([y, core]).astype(jnp.int32)
    offsets = jnp.arange(span, dtype=jnp.int32)

    def angles_of(part):
        blocks = lax.dynamic_slice_in_dim(block_order, 2 * (place * 2 + part), 2)
        positions = (blocks[:, None] * span + offsets[None, :]).reshape(tok_rows)
        return blocks, rotation(positions, span)

    _, (cosine, sine) = angles_of(y_hi)
    own_blocks, (cos_there, sin_there) = angles_of(core)
    own = jnp.concatenate([own_blocks, core[None].astype(jnp.int32)])
    gain_q, gain_k = gain_query[None, :], gain_key[None, :]
    shape = jax.ShapeDtypeStruct

    kv_mine = to_all(jnp.concatenate([w_key, w_value], axis=1), chips, planes * columns)
    kv_mine = kv_mine.reshape(columns, half // columns, kv_cols)

    toks_mine, toks_theirs, turned = pl.pallas_call(
        prepare_kernel,
        out_shape=(shape((columns, tok_rows, half // columns), bf16),) * 2
        + (shape((2 * columns, half // columns, tok_rows), bf16),),
        in_specs=[smem, vmem],
        out_specs=(vmem,) * 3,
        compiler_params=pltpu.CompilerParams(vmem_limit_bytes=48 * mib),
        cost_estimate=cheap,
        name="prepare",
    )(where, tokens.T.reshape(4, 4, columns, 2, own_rows, tok_rows))

    toks_other = flip(toks_theirs)
    kv_mine, toks_mine, toks_theirs, turned, cosine, sine, cos_there, sin_there, own = (
        lax.optimization_barrier(
            (kv_mine, toks_mine, toks_theirs, turned, cosine, sine, cos_there, sin_there, own)
        )
    )
    kv_theirs = flip(kv_mine)
    q_rows, _ = lax.optimization_barrier((w_query, kv_mine))
    q_rows = to_all(q_rows, owners, planes).reshape(planes * own_rows, q_cols)

    kv16, raw_k = call(
        key_value_kernel,
        (shape((tok_rows, kv_cols), bf16), shape((tok_rows, span), f32)),
        toks_mine, toks_theirs, kv_mine, kv_theirs, gain_k, cosine, sine,
        name="key_value",
    )
    kv_send = jnp.broadcast_to(swap(kv16)[None], (planes, tok_rows, kv_cols))
    kv_send, q_rows = lax.optimization_barrier((kv_send, q_rows))
    kv_own = lax.all_to_all(kv_send, plane, 0, 0)
    q_mine = [q_rows] + [ring(q_rows, k) for k in range(1, columns)]
    q_part, q_part_other = call(
        query_part_kernel,
        (shape((tok_rows, q_cols), f32),) * 2,
        where, toks_mine, toks_other, *q_mine,
        name="query_part",
    )
    kv_own, q_part, q_part_other, grad_out = lax.optimization_barrier(
        (kv_own, q_part, q_part_other, swap(cotangent[0]))
    )
    q16, raw_q = call(
        query_kernel,
        (shape((tok_rows, q_cols), bf16),) * 2,
        q_part, flip(q_part_other), gain_q, cosine, sine,
        name="query",
    )
    kv_other, q16, raw_q = lax.optimization_barrier((flip(kv_own), q16, raw_q))
    q16 = swap(q16)
    turned, raw_q, _ = lax.optimization_barrier((turned, raw_q, q16))
    turned = lax.all_to_all(turned, column + ("core",), 0, 0)
    raw_there = swap(jnp.concatenate([raw_q, raw_k.astype(bf16)], axis=1))

    ctx, dq, dkv_mine, dkv_theirs = attention(
        block_order, own, q16, grad_out, kv_own, kv_other
    )
    q_theirs = [flip(block) for block in q_mine]
    dkv_theirs, dq, turned, raw_there, q_theirs = lax.optimization_barrier(
        (dkv_theirs, dq, turned, raw_there, q_theirs)
    )
    dkv = (dkv_mine.astype(f32) + flip(dkv_theirs).astype(f32)).astype(bf16)
    dkv = lax.all_to_all(dkv, plane, 0, 0)

    g_q, gains_q = call(
        grad_query_kernel,
        (shape((tok_rows, q_cols), bf16), shape((8, span), f32)),
        raw_there, dq, gain_q, cos_there, sin_there,
        name="grad_query",
    )
    parts = weight_grad(where, turned, around(g_q), planes, own_rows)
    parts = lax.all_to_all(parts, owners, 0, 0)
    own_query = jnp.sum(parts.astype(f32), axis=0)

    g_kv = call(
        grad_key_value_kernel,
        shape((tok_rows + 16, kv_cols), bf16),
        raw_there, dkv, gain_k, cos_there, sin_there, gains_q,
        name="grad_key_value",
    )
    blocks, g_q_back, g_kv_back = lax.optimization_barrier((around(g_kv), swap(g_q), swap(g_kv)))
    parts = weight_grad(where, turned, blocks, planes, own_rows + 8)
    parts = lax.all_to_all(parts, owners, 0, 0)
    own_key, own_value, gain_sum_q, gain_sum_k = call(
        finish_kernel,
        (shape((own_rows, span), f32),) * 2 + (shape((1, span), f32),) * 2,
        parts,
        name="finish",
    )

    grad_states = pl.pallas_call(
        grad_states_kernel,
        out_shape=shape((tok_rows, width), bf16),
        in_specs=[smem] + [vmem] * (4 + 2 * columns),
        out_specs=vmem,
        scratch_shapes=[pltpu.VMEM((columns, 2, half // columns, tok_rows), f32)],
        compiler_params=pltpu.CompilerParams(vmem_limit_bytes=48 * mib),
        cost_estimate=cheap,
        name="grad_states",
    )(where, g_q_back, g_kv_back, kv_mine, kv_theirs, *q_mine, *q_theirs)
    return (
        swap(ctx)[None],
        grad_states[None],
        own_query,
        own_key,
        own_value,
        gain_sum_q[0],
        gain_sum_k[0],
    )


def solution(mesh):
    fine = Mesh(mesh.devices.reshape(4, 4, 2, 2, 2), ("x", "z", "y_hi", "y_lo", "core"))
    ctx, dp = ("x", "z", "y_hi"), ("y_lo", "core")
    rows = P(ctx + dp, None)
    tokens = P(dp, ctx, None)
    in_specs = (tokens, P(), rows, rows, rows, P(), P(), tokens)
    out_specs = (tokens, tokens, rows, rows, rows, P(), P())
    return jax.shard_map(local, mesh=fine, in_specs=in_specs, out_specs=out_specs, check_vma=False)
```

```python
import math

import jax
import jax.numpy as jnp
from jax import lax
from jax.experimental import pallas as pl
from jax.experimental.pallas import tpu as pltpu
from jax.sharding import Mesh
from jax.sharding import PartitionSpec as P

bf16, f32 = jnp.bfloat16, jnp.float32
theta = 1000000.0
floor_score = -1e30
span = 128
chunk = 512
per_chunk = chunk // span
mib = 2**20
smem = pl.BlockSpec(memory_space=pltpu.SMEM)
vmem = pl.BlockSpec(memory_space=pltpu.VMEM)
anywhere = pl.BlockSpec(memory_space=pl.ANY)


def mm(a, b):
    return jnp.dot(a, b, preferred_element_type=f32)


def rotation(positions, head_width):
    steps_half = jnp.arange(head_width // 2, dtype=f32)
    inverse = jnp.power(f32(theta), -2.0 * steps_half / head_width)
    angles = positions.astype(f32)[:, None] * inverse[None, :]
    cosine = jnp.cos(angles)
    sine = jnp.sin(angles)
    return jnp.concatenate([cosine, cosine], 1), jnp.concatenate([-sine, sine], 1)


def inverse_norm(raw):
    return lax.rsqrt(jnp.mean(raw * raw, axis=-1, keepdims=True) + 1e-06)


def shape_head(raw, gain, cosine, sine):
    normed = raw * inverse_norm(raw) * gain
    return normed * cosine + pltpu.roll(normed, span // 2, 1) * sine


def shape_head_grad(raw, gain, cosine, sine, grad):
    inverse = inverse_norm(raw)
    grad_normed = grad * cosine + pltpu.roll(grad * sine, span // 2, 1)
    grad_unit = grad_normed * gain
    unit = raw * inverse
    shrink = jnp.mean(grad_unit * unit, axis=-1, keepdims=True)
    return inverse * (grad_unit - unit * shrink), grad_normed * unit


def prepare_kernel(where, src_ref, *rest):
    toks_ref, toks_theirs_ref, turned_ref, done_ref = rest[-4:]
    sizes = src_ref.shape[:3]
    core = where[1]
    done_ref[...] = jnp.zeros_like(done_ref)

    def rows(y, side):
        pieces = [src_ref[x, z, y, side].astype(f32) for z in range(sizes[1]) for x in range(sizes[0])]
        return jnp.concatenate(pieces, axis=0).astype(bf16)

    for y in range(sizes[2]):
        toks_ref[y] = rows(y, core).T
        toks_theirs_ref[y] = rows(y, 1 - core).T
        for side in range(2):
            turned_ref[2 * y + side] = rows(y, side)


def key_value_kernel(mine_ref, other_ref, w_ref, w_other_ref, gain_ref, cos_ref, sin_ref, kv_ref, raw_ref):
    raw = sum(mm(mine_ref[y], w_ref[y]) + mm(other_ref[y], w_other_ref[y]) for y in range(w_ref.shape[0]))
    raw_ref[...] = raw[:, :span]
    kv_ref[:, :span] = shape_head(raw[:, :span], gain_ref[...], cos_ref[...], sin_ref[...]).astype(bf16)
    kv_ref[:, span:] = raw[:, span:].astype(bf16)


def query_part_kernel(where, mine_ref, other_ref, w0, w1, w2, w3, part_ref, part_other_ref, done_ref):
    done_ref[...] = jnp.zeros_like(done_ref)
    for toks_ref, out_ref in ((mine_ref, part_ref), (other_ref, part_other_ref)):
        total = 0.0
        for k, w in enumerate((w0, w1, w2, w3)):
            total = total + mm(toks_ref[lax.rem(where[0] + k, 4)], w[...])
        out_ref[...] = total


def query_kernel(part_ref, part_theirs_ref, raw_k_ref, gain_ref, cos_ref, sin_ref, q_ref, raw_ref):
    gain = gain_ref[...] * (span**-0.5 / math.log(2.0))
    raw_ref[:, -span:] = raw_k_ref[...].astype(bf16)
    for h in range(q_ref.shape[1] // span):
        part = slice(h * span, (h + 1) * span)
        raw = part_ref[:, part] + part_theirs_ref[:, part]
        raw_ref[:, part] = raw.astype(bf16)
        q_ref[:, part] = shape_head(raw, gain, cos_ref[...], sin_ref[...]).astype(bf16)


def attention_kernel(
    order, own, q_ref, g_ref, kv_ref, kv_other_ref, ctx_ref, dq_ref, dkv_ref, dkv_other_ref,
    slot_of, ks, vs, kt, vt, acc_kv, qs, gs, qt, gt, acc_o, row_max, row_sum, row_delta, acc_q,
):
    spans, heads = order.shape[0], q_ref.shape[1] // span
    chunks = spans // per_chunk
    rows = heads * span
    core = own[2]

    def place(slot, carry):
        slot_of[order[slot]] = slot
        return carry

    lax.fori_loop(0, spans, place, 0)

    def arrange(c, carry):
        for j in range(per_chunk):
            slot = slot_of[c * per_chunk + j]
            pair, rows_at = slot // 4, pl.multiple_of(slot % 2 * span, span)
            mine = (slot // 2) % 2 == core
            both = jnp.where(
                mine, kv_ref[pair, pl.ds(rows_at, span), :], kv_other_ref[pair, pl.ds(rows_at, span), :]
            )
            part = slice(j * span, (j + 1) * span)
            ks[c, part, :] = both[:, :span]
            vs[c, part, :] = both[:, span:]
            kt[c, :, part] = both[:, :span].T
            vt[c, :, part] = both[:, span:].T
        acc_kv[c] = jnp.zeros_like(acc_kv[c])
        return carry

    lax.fori_loop(0, chunks, arrange, 0)

    first_upper = own[0] > own[1]
    for upper in (True, False):
        which = jnp.where(first_upper, 0, 1) if upper else jnp.where(first_upper, 1, 0)
        block = own[which]
        row0 = pl.multiple_of(which * span, span)
        last = block // per_chunk
        for h in range(heads):
            part = slice(h * span, (h + 1) * span)
            qh = q_ref[pl.ds(row0, span), part]
            gh = g_ref[pl.ds(row0, span), part]
            qs[part, :] = qh
            gs[part, :] = gh
            qt[:, part] = qh.T
            gt[:, part] = gh.T

        def allowed(c):
            key_pos = c * chunk + lax.broadcasted_iota(jnp.int32, (chunk, rows), 0)
            row = lax.broadcasted_iota(jnp.int32, (chunk, rows), 1)
            return key_pos <= block * span + jnp.bitwise_and(row, span - 1)

        row_max[...] = jnp.full_like(row_max, floor_score)
        row_sum[...] = jnp.zeros_like(row_sum)
        acc_o[...] = jnp.zeros_like(acc_o)

        def forward(c, masked):
            s = mm(ks[c], qt[...])
            if masked:
                s = jnp.where(allowed(c), s, floor_score)
            old = row_max[...]
            new = jnp.maximum(old, jnp.max(s, axis=0, keepdims=True))
            p = jnp.exp2(s - new)
            alpha = jnp.exp2(old - new)
            row_max[...] = new
            row_sum[...] = row_sum[...] * alpha + jnp.sum(p, axis=0, keepdims=True)
            acc_o[...] = acc_o[...] * alpha + mm(vt[c], p.astype(bf16))

        def forward_step(c, carry):
            forward(c, False)
            return carry

        lax.fori_loop(0, last, forward_step, 0)
        forward(last, True)

        total = row_sum[...]
        ctx_t = (acc_o[...] / total).astype(bf16)
        row_max[...] = row_max[...] + jnp.log2(total)
        row_delta[...] = jnp.sum(ctx_t.astype(f32) * gt[...].astype(f32), axis=0, keepdims=True)
        for h in range(heads):
            part = slice(h * span, (h + 1) * span)
            ctx_ref[pl.ds(row0, span), part] = ctx_t[:, part].T
        acc_q[...] = jnp.zeros_like(acc_q)

        def backward(c, masked):
            s = mm(ks[c], qt[...])
            p = jnp.exp2(s - row_max[...])
            if masked:
                p = jnp.where(allowed(c), p, 0.0)
            dp = mm(vs[c], gt[...])
            ds = (p * (dp - row_delta[...])).astype(bf16)
            acc_kv[c, :, span:] += mm(p.astype(bf16), gs[...])
            acc_kv[c, :, :span] += mm(ds, qs[...])
            acc_q[...] += mm(kt[c], ds)

        def backward_step(c, carry):
            backward(c, False)
            return carry

        lax.fori_loop(0, last, backward_step, 0)
        backward(last, True)
        for h in range(heads):
            part = slice(h * span, (h + 1) * span)
            dq_ref[pl.ds(row0, span), part] = acc_q[:, part].T * (span**-0.5)

    def give(c, carry):
        for j in range(per_chunk):
            part = slice(j * span, (j + 1) * span)
            slot = slot_of[c * per_chunk + j]
            pair, rows_at = slot // 4, pl.multiple_of(slot % 2 * span, span)
            mine = (slot // 2) % 2 == core
            dk = (acc_kv[c, part, :span] * math.log(2.0)).astype(bf16)
            dv = acc_kv[c, part, span:].astype(bf16)

            @pl.when(mine)
            def _():
                dkv_ref[pair, pl.ds(rows_at, span), :span] = dk
                dkv_ref[pair, pl.ds(rows_at, span), span:] = dv

            @pl.when(jnp.logical_not(mine))
            def _():
                dkv_other_ref[pair, pl.ds(rows_at, span), :span] = dk
                dkv_other_ref[pair, pl.ds(rows_at, span), span:] = dv

        return carry

    lax.fori_loop(0, chunks, give, 0)


def attention(order, own, q16, g16, kv, kv_other):
    rows_here, cols = q16.shape
    spans = order.shape[0]
    chunks = spans // per_chunk
    rows = cols
    share = jax.ShapeDtypeStruct(kv.shape, bf16)
    return pl.pallas_call(
        attention_kernel,
        out_shape=(
            jax.ShapeDtypeStruct((rows_here, cols), bf16),
            jax.ShapeDtypeStruct((rows_here, cols), f32),
            share,
            share,
        ),
        in_specs=[smem, smem] + [vmem] * 4,
        out_specs=(vmem,) * 4,
        scratch_shapes=[
            pltpu.SMEM((spans,), jnp.int32),
            pltpu.VMEM((chunks, chunk, span), bf16),
            pltpu.VMEM((chunks, chunk, span), bf16),
            pltpu.VMEM((chunks, span, chunk), bf16),
            pltpu.VMEM((chunks, span, chunk), bf16),
            pltpu.VMEM((chunks, chunk, 2 * span), f32),
            pltpu.VMEM((rows, span), bf16),
            pltpu.VMEM((rows, span), bf16),
            pltpu.VMEM((span, rows), bf16),
            pltpu.VMEM((span, rows), bf16),
            pltpu.VMEM((span, rows), f32),
            pltpu.VMEM((1, rows), f32),
            pltpu.VMEM((1, rows), f32),
            pltpu.VMEM((1, rows), f32),
            pltpu.VMEM((span, rows), f32),
        ],
        compiler_params=pltpu.CompilerParams(vmem_limit_bytes=48 * mib),
        cost_estimate=cheap,
        name="attention",
    )(order, own, q16, g16, kv, kv_other)


def grad_query_kernel(raw_ref, dq_ref, gain_ref, cos_ref, sin_ref, g_ref, gain_out):
    cosine, sine = cos_ref[...], sin_ref[...]
    sums = jnp.zeros((1, span), f32)
    for h in range(dq_ref.shape[1] // span):
        part = slice(h * span, (h + 1) * span)
        grad, terms = shape_head_grad(
            raw_ref[:, part].astype(f32), gain_ref[...], cosine, sine, dq_ref[:, part]
        )
        g_ref[:, part] = grad.astype(bf16)
        sums = sums + jnp.sum(terms, axis=0, keepdims=True)
    gain_out[...] = jnp.broadcast_to(sums, gain_out.shape)


def grad_key_value_kernel(raw_ref, dkv_ref, gain_ref, cos_ref, sin_ref, gain_q_ref, g_ref):
    rows = raw_ref.shape[0]
    dkv = jnp.sum(dkv_ref[...].astype(f32), axis=0)
    grad, terms = shape_head_grad(
        raw_ref[:, -span:].astype(f32), gain_ref[...], cos_ref[...], sin_ref[...], dkv[:, :span]
    )
    g_ref[:rows, :span] = grad.astype(bf16)
    g_ref[:rows, span:] = dkv[:, span:].astype(bf16)
    gain_k = jnp.sum(terms, axis=0, keepdims=True)
    split = []
    for gain in (gain_q_ref[0:1], gain_k):
        high = gain.astype(bf16).astype(f32)
        split.append(jnp.concatenate([high, gain - high], axis=1))
    row = lax.broadcasted_iota(jnp.int32, (g_ref.shape[0] - rows, 2 * span), 0)
    g_ref[rows:] = jnp.where(row == 0, split[0], jnp.where(row == 1, split[1], 0.0)).astype(bf16)


def weight_grad_kernel(where, turned_ref, *rest):
    blocks, out_ref = rest[:-1], rest[-1]
    columns = len(blocks) // 2
    toks = turned_ref.shape[2]
    y, core = where[0], where[1]
    total, gains = None, None
    for side in range(2):
        for k in range(columns):
            from_y = lax.rem(y + k, columns)
            from_core = core if side == 0 else 1 - core
            at = (from_core * 2 + lax.rem(from_y, 2)) * 2 + from_y // 2
            block = blocks[side * columns + k]
            part = mm(turned_ref[at], block[:toks])
            total = part if total is None else total + part
            if block.shape[0] > toks:
                row = block[toks:].astype(f32)
                gains = row if gains is None else gains + row
    own_rows = total.shape[0] // out_ref.shape[0]
    extra = []
    if gains is not None:
        gain = gains[:, :span] + gains[:, span:]
        high = gain.astype(bf16).astype(f32)
        extra = [jnp.concatenate([high, gain - high], axis=1)[:8]]
    for i in range(out_ref.shape[0]):
        part = total[i * own_rows : (i + 1) * own_rows]
        out_ref[i] = jnp.concatenate([part] + extra, axis=0).astype(bf16)


def weight_grad(where, turned, blocks, planes, padded):
    return pl.pallas_call(
        weight_grad_kernel,
        out_shape=jax.ShapeDtypeStruct((planes, padded, blocks[0].shape[1]), bf16),
        in_specs=[smem] + [vmem] * (1 + len(blocks)),
        out_specs=vmem,
        compiler_params=pltpu.CompilerParams(vmem_limit_bytes=48 * mib),
        cost_estimate=cheap,
        name="weight_grad",
    )(where, turned, *blocks)


def grad_states_kernel(where, gq_ref, gkv_ref, *rest):
    sources, (out_ref, blocks, loaded_kv, loaded_q, sems) = rest[:-5], rest[-5:]
    columns = loaded_q.shape[0] // 2
    y, core = where[0], where[1]
    own_rows = 40
    toks = gq_ref.shape[0]
    kv, weights = sources[:2], sources[2:]
    copies = [pltpu.make_async_copy(kv[i], loaded_kv.at[i], sems.at[i]) for i in range(2)]
    copies += [pltpu.make_async_copy(w, loaded_q.at[i], sems.at[2 + i]) for i, w in enumerate(weights)]
    for copy in copies:
        copy.start()
    transposed = (((1,), (1,)), ((), ()))
    for side in range(2):
        at_core = core if side == 0 else 1 - core
        copies[side].wait()
        for k in range(columns):
            at = lax.rem(y + k, columns)
            copies[2 + side * columns + k].wait()
            blocks[at, at_core] = lax.dot_general(
                loaded_q[side * columns + k], gq_ref[...], transposed, preferred_element_type=f32
            ) + lax.dot_general(loaded_kv[side, at], gkv_ref[:toks], transposed, preferred_element_type=f32)
    for x in range(4):
        pieces = []
        for z in range(4):
            part = slice((z * 4 + x) * own_rows, (z * 4 + x + 1) * own_rows)
            pieces += [blocks[at, c, part] for at in range(columns) for c in range(2)]
        rows = jnp.concatenate(pieces, axis=0)
        out_ref[:, x * rows.shape[0] : (x + 1) * rows.shape[0]] = rows.astype(bf16).T


def finish_kernel(parts_ref, key_ref, value_ref, gain_q_ref, gain_k_ref):
    sums = jnp.sum(parts_ref[...].astype(f32), axis=0)
    rows = key_ref.shape[0]
    key_ref[...] = sums[:rows, :span]
    value_ref[...] = sums[:rows, span:]
    gains = sums[rows:, :span] + sums[rows:, span:]
    gain_q_ref[...] = gains[0:1]
    gain_k_ref[...] = gains[1:2]


cheap = pl.CostEstimate(flops=1000, bytes_accessed=1000, transcendentals=0)


def call(kernel, shapes, *args, name, after=()):
    count = len(args)

    def run(*refs):
        kernel(*refs[:count], *refs[count + len(after) :])

    return pl.pallas_call(
        run,
        out_shape=shapes,
        in_specs=[smem if a.dtype == jnp.int32 else vmem for a in args] + [anywhere] * len(after),
        out_specs=jax.tree.map(lambda _: vmem, shapes),
        compiler_params=pltpu.CompilerParams(vmem_limit_bytes=48 * mib),
        cost_estimate=cheap,
        name=name,
    )(*args, *after)


plane = ("x", "z")
owners = ("z", "x")
column = ("y_hi", "y_lo")
chips = column + owners
swapped = [(0, 0), (1, 2), (2, 1), (3, 3)]
flipped = [(0, 1), (1, 0)]


def swap(array):
    return lax.ppermute(array, ("y_hi", "core"), swapped)


def flip(array):
    return lax.ppermute(array, "core", flipped)


def to_all(array, axes, count):
    return lax.all_to_all(jnp.broadcast_to(array[None], (count,) + array.shape), axes, 0, 0)


def ring(array, step):
    return lax.ppermute(array, column, [(i, (i - step) % 4) for i in range(4)])


def place_kernel(where, *refs):
    for k, block in enumerate(refs[:-1]):
        refs[-1][lax.rem(where[0] + k, 4)] = block[...]


def collect(array, name):
    parts = [array] + [
        lax.ppermute(array, name, [(i, (i - k) % 4) for i in range(4)]) for k in range(1, 4)
    ]
    at = lax.axis_index(name).astype(jnp.int32)[None]
    return call(place_kernel, jax.ShapeDtypeStruct((4,) + array.shape, bf16), at, *parts, name="place")


def around(array):
    mine = [array] + [ring(array, k) for k in range(1, 4)]
    return mine + [flip(a) for a in mine]


def local(hidden_states, block_order, w_query, w_key, w_value, gain_query, gain_key, cotangent):
    tokens = hidden_states[0]
    tok_rows, width = tokens.shape
    q_cols = w_query.shape[1]
    kv_cols = 2 * span
    own_rows = w_query.shape[0]
    planes, columns = 16, 4
    half = width // 2
    place = lax.axis_index("x") * 4 + lax.axis_index("z")
    y_hi, core = lax.axis_index("y_hi"), lax.axis_index("core")
    y = y_hi * 2 + lax.axis_index("y_lo")
    where = jnp.stack([y, core]).astype(jnp.int32)
    offsets = jnp.arange(span, dtype=jnp.int32)

    def angles_of(part):
        blocks = lax.dynamic_slice_in_dim(block_order, 2 * (place * 2 + part), 2)
        positions = (blocks[:, None] * span + offsets[None, :]).reshape(tok_rows)
        return blocks, rotation(positions, span)

    _, (cosine, sine) = angles_of(y_hi)
    own_blocks, (cos_there, sin_there) = angles_of(core)
    own = jnp.concatenate([own_blocks, core[None].astype(jnp.int32)])
    gain_q, gain_k = gain_query[None, :], gain_key[None, :]
    shape = jax.ShapeDtypeStruct

    kv_mine = to_all(jnp.concatenate([w_key, w_value], axis=1), chips, planes * columns)
    kv_mine = kv_mine.reshape(columns, half // columns, kv_cols)

    early = (cosine, sine, cos_there, sin_there)
    toks_mine, toks_theirs, turned, done = pl.pallas_call(
        prepare_kernel,
        out_shape=(shape((columns, tok_rows, half // columns), bf16),) * 2
        + (shape((2 * columns, half // columns, tok_rows), bf16), shape((8, span), f32)),
        in_specs=[smem, vmem] + [anywhere] * len(early),
        out_specs=(vmem,) * 4,
        compiler_params=pltpu.CompilerParams(vmem_limit_bytes=48 * mib),
        cost_estimate=cheap,
        name="prepare",
    )(where, tokens.T.reshape(4, 4, columns, 2, own_rows, tok_rows), *early)
    toks_other = flip(toks_theirs)
    q_rows = collect(collect(w_query, "x"), "z").reshape(planes * own_rows, q_cols)
    kv_mine, q_rows, done, own = lax.optimization_barrier((kv_mine, q_rows, done, own))
    kv_theirs = flip(kv_mine)

    kv16, raw_k = call(
        key_value_kernel,
        (shape((tok_rows, kv_cols), bf16), shape((tok_rows, span), f32)),
        toks_mine, toks_theirs, kv_mine, kv_theirs, gain_k, cosine, sine,
        name="key_value",
        after=(done,),
    )
    kv_send = jnp.broadcast_to(swap(kv16)[None], (planes, tok_rows, kv_cols))
    kv_own = lax.all_to_all(kv_send, plane, 0, 0)
    q_mine = [q_rows] + [ring(q_rows, k) for k in range(1, columns)]
    grad_out = swap(cotangent[0])
    q_part, q_part_other, done = call(
        query_part_kernel,
        (shape((tok_rows, q_cols), f32),) * 2 + (shape((8, span), f32),),
        where, toks_mine, toks_other, *q_mine,
        name="query_part",
        after=(grad_out,),
    )
    kv_own, q_part_other = lax.optimization_barrier((kv_own, q_part_other))
    q16, raw = call(
        query_kernel,
        (shape((tok_rows, q_cols), bf16), shape((tok_rows, q_cols + span), bf16)),
        q_part, flip(q_part_other), raw_k, gain_q, cosine, sine,
        name="query",
    )
    kv_other = flip(kv_own)
    q16 = swap(q16)
    turned, done = lax.optimization_barrier((turned, done))
    turned = lax.all_to_all(turned, column + ("core",), 0, 0)
    raw, q_piece = lax.optimization_barrier((raw, q16[:8, :span]))
    raw_there = swap(raw)

    ctx, dq, dkv_mine, dkv_theirs = attention(
        block_order, own, q16, grad_out, kv_own, kv_other
    )
    dkv_theirs, turned, raw_there = lax.optimization_barrier((dkv_theirs, turned, raw_there))
    q_theirs = [flip(block) for block in q_mine]
    dkv = (dkv_mine.astype(f32) + flip(dkv_theirs).astype(f32)).astype(bf16)
    dkv = lax.all_to_all(dkv, plane, 0, 0)

    g_q, gains_q = call(
        grad_query_kernel,
        (shape((tok_rows, q_cols), bf16), shape((8, span), f32)),
        raw_there, dq, gain_q, cos_there, sin_there,
        name="grad_query",
        after=(done, q_piece),
    )
    parts = weight_grad(where, turned, around(g_q), planes, own_rows)
    parts = lax.all_to_all(parts, owners, 0, 0)
    own_query = jnp.sum(parts.astype(f32), axis=0)

    g_kv = call(
        grad_key_value_kernel,
        shape((tok_rows + 16, kv_cols), bf16),
        raw_there, dkv, gain_k, cos_there, sin_there, gains_q,
        name="grad_key_value",
    )
    blocks, g_q_back, g_kv_back = lax.optimization_barrier((around(g_kv), swap(g_q), swap(g_kv)))
    parts = weight_grad(where, turned, blocks, planes, own_rows + 8)
    parts = lax.all_to_all(parts, owners, 0, 0)
    own_key, own_value, gain_sum_q, gain_sum_k = call(
        finish_kernel,
        (shape((own_rows, span), f32),) * 2 + (shape((1, span), f32),) * 2,
        parts,
        name="finish",
    )

    grad_states = pl.pallas_call(
        grad_states_kernel,
        out_shape=shape((tok_rows, width), bf16),
        in_specs=[smem] + [vmem] * 2 + [anywhere] * (2 + 2 * columns),
        out_specs=vmem,
        scratch_shapes=[
            pltpu.VMEM((columns, 2, half // columns, tok_rows), f32),
            pltpu.VMEM((2, columns, half // columns, kv_cols), bf16),
            pltpu.VMEM((2 * columns, half // columns, q_cols), bf16),
            pltpu.SemaphoreType.DMA((2 + 2 * columns,)),
        ],
        compiler_params=pltpu.CompilerParams(vmem_limit_bytes=48 * mib),
        cost_estimate=cheap,
        name="grad_states",
    )(where, g_q_back, g_kv_back, kv_mine, kv_theirs, *q_mine, *q_theirs)
    return (
        swap(ctx)[None],
        grad_states[None],
        own_query,
        own_key,
        own_value,
        gain_sum_q[0],
        gain_sum_k[0],
    )


def solution(mesh):
    fine = Mesh(mesh.devices.reshape(4, 4, 2, 2, 2), ("x", "z", "y_hi", "y_lo", "core"))
    ctx, dp = ("x", "z", "y_hi"), ("y_lo", "core")
    rows = P(ctx + dp, None)
    tokens = P(dp, ctx, None)
    in_specs = (tokens, P(), rows, rows, rows, P(), P(), tokens)
    out_specs = (tokens, tokens, rows, rows, rows, P(), P())
    return jax.shard_map(local, mesh=fine, in_specs=in_specs, out_specs=out_specs, check_vma=False)
```

```python
import math

import jax
import jax.numpy as jnp
from jax import lax
from jax.experimental import pallas as pl
from jax.experimental.pallas import tpu as pltpu
from jax.sharding import Mesh
from jax.sharding import PartitionSpec as P

bf16, f32 = jnp.bfloat16, jnp.float32
theta = 1000000.0
floor_score = -1e30
span = 128
chunk = 512
per_chunk = chunk // span
mib = 2**20
smem = pl.BlockSpec(memory_space=pltpu.SMEM)
vmem = pl.BlockSpec(memory_space=pltpu.VMEM)
anywhere = pl.BlockSpec(memory_space=pl.ANY)


def mm(a, b):
    return jnp.dot(a, b, preferred_element_type=f32)


def rotation(positions, head_width):
    steps_half = jnp.arange(head_width // 2, dtype=f32)
    inverse = jnp.power(f32(theta), -2.0 * steps_half / head_width)
    angles = positions.astype(f32)[:, None] * inverse[None, :]
    cosine = jnp.cos(angles)
    sine = jnp.sin(angles)
    return jnp.concatenate([cosine, cosine], 1), jnp.concatenate([-sine, sine], 1)


def inverse_norm(raw):
    return lax.rsqrt(jnp.mean(raw * raw, axis=-1, keepdims=True) + 1e-06)


def shape_head(raw, gain, cosine, sine):
    normed = raw * inverse_norm(raw) * gain
    return normed * cosine + pltpu.roll(normed, span // 2, 1) * sine


def shape_head_grad(raw, gain, cosine, sine, grad):
    inverse = inverse_norm(raw)
    grad_normed = grad * cosine + pltpu.roll(grad * sine, span // 2, 1)
    grad_unit = grad_normed * gain
    unit = raw * inverse
    shrink = jnp.mean(grad_unit * unit, axis=-1, keepdims=True)
    return inverse * (grad_unit - unit * shrink), grad_normed * unit


def prepare_kernel(where, src_ref, *rest):
    toks_ref, toks_theirs_ref, turned_ref, done_ref = rest[-4:]
    sizes = src_ref.shape[:3]
    core = where[1]
    done_ref[...] = jnp.zeros_like(done_ref)

    def rows(y, side):
        pieces = [src_ref[x, z, y, side].astype(f32) for z in range(sizes[1]) for x in range(sizes[0])]
        return jnp.concatenate(pieces, axis=0).astype(bf16)

    for y in range(sizes[2]):
        toks_ref[y] = rows(y, core).T
        toks_theirs_ref[y] = rows(y, 1 - core).T
        for side in range(2):
            turned_ref[2 * y + side] = rows(y, side)


def key_value_kernel(mine_ref, other_ref, w_ref, w_other_ref, gain_ref, cos_ref, sin_ref, kv_ref, raw_ref):
    raw = sum(mm(mine_ref[y], w_ref[y]) + mm(other_ref[y], w_other_ref[y]) for y in range(w_ref.shape[0]))
    raw_ref[...] = raw[:, :span]
    kv_ref[:, :span] = shape_head(raw[:, :span], gain_ref[...], cos_ref[...], sin_ref[...]).astype(bf16)
    kv_ref[:, span:] = raw[:, span:].astype(bf16)


def split_kernel(where, src_ref, low_ref, high_ref):
    planes = src_ref.shape[0]
    columns = low_ref.shape[0]
    rows = src_ref.shape[1] // (columns + 1)
    blocks = [src_ref[i].astype(f32) for i in range(planes)]
    for k in range(columns + 1):
        part = jnp.concatenate([block[k * rows : (k + 1) * rows] for block in blocks], axis=0).astype(bf16)
        if k < columns:
            low_ref[lax.rem(where[0] + k, columns)] = part
        else:
            high_ref[...] = part


def query_kernel(where, mine_ref, theirs_ref, low_ref, low_theirs_ref, *rest):
    highs, (raw_k_ref, gain_ref, cos_ref, sin_ref, q_ref, raw_ref) = rest[:-6], rest[-6:]
    columns, cols = low_ref.shape[0], low_ref.shape[2]
    low, high = 0.0, 0.0
    for y in range(columns):
        low = low + mm(mine_ref[y], low_ref[y]) + mm(theirs_ref[y], low_theirs_ref[y])
    for k in range(columns):
        at = lax.rem(where[0] + k, columns)
        high = high + mm(mine_ref[at], highs[k][...]) + mm(theirs_ref[at], highs[columns + k][...])
    raw_ref[:, -span:] = raw_k_ref[...].astype(bf16)
    gain = gain_ref[...] * (span**-0.5 / math.log(2.0))
    for h in range(q_ref.shape[1] // span):
        part = slice(h * span, (h + 1) * span)
        half, at = (low, h * span) if h * span < cols else (high, h * span - cols)
        raw = half[:, at : at + span]
        raw_ref[:, part] = raw.astype(bf16)
        q_ref[:, part] = shape_head(raw, gain, cos_ref[...], sin_ref[...]).astype(bf16)


def attention_kernel(
    order, own, q_ref, g_ref, kv_ref, kv_other_ref, ctx_ref, dq_ref, dkv_ref, dkv_other_ref,
    slot_of, ks, vs, kt, vt, acc_kv, qs, gs, qt, gt, acc_o, row_max, row_sum, row_delta, acc_q,
):
    spans, heads = order.shape[0], q_ref.shape[1] // span
    chunks = spans // per_chunk
    rows = heads * span
    core = own[2]

    def place(slot, carry):
        slot_of[order[slot]] = slot
        return carry

    lax.fori_loop(0, spans, place, 0)

    def arrange(c, carry):
        for j in range(per_chunk):
            slot = slot_of[c * per_chunk + j]
            pair, rows_at = slot // 4, pl.multiple_of(slot % 2 * span, span)
            mine = (slot // 2) % 2 == core
            both = jnp.where(
                mine, kv_ref[pair, pl.ds(rows_at, span), :], kv_other_ref[pair, pl.ds(rows_at, span), :]
            )
            part = slice(j * span, (j + 1) * span)
            ks[c, part, :] = both[:, :span]
            vs[c, part, :] = both[:, span:]
            kt[c, :, part] = both[:, :span].T
            vt[c, :, part] = both[:, span:].T
        acc_kv[c] = jnp.zeros_like(acc_kv[c])
        return carry

    lax.fori_loop(0, chunks, arrange, 0)

    first_upper = own[0] > own[1]
    for upper in (True, False):
        which = jnp.where(first_upper, 0, 1) if upper else jnp.where(first_upper, 1, 0)
        block = own[which]
        row0 = pl.multiple_of(which * span, span)
        last = block // per_chunk
        for h in range(heads):
            part = slice(h * span, (h + 1) * span)
            qh = q_ref[pl.ds(row0, span), part]
            gh = g_ref[pl.ds(row0, span), part]
            qs[part, :] = qh
            gs[part, :] = gh
            qt[:, part] = qh.T
            gt[:, part] = gh.T

        def allowed(c):
            key_pos = c * chunk + lax.broadcasted_iota(jnp.int32, (chunk, rows), 0)
            row = lax.broadcasted_iota(jnp.int32, (chunk, rows), 1)
            return key_pos <= block * span + jnp.bitwise_and(row, span - 1)

        row_max[...] = jnp.full_like(row_max, floor_score)
        row_sum[...] = jnp.zeros_like(row_sum)
        acc_o[...] = jnp.zeros_like(acc_o)

        def forward(c, masked):
            s = mm(ks[c], qt[...])
            if masked:
                s = jnp.where(allowed(c), s, floor_score)
            old = row_max[...]
            new = jnp.maximum(old, jnp.max(s, axis=0, keepdims=True))
            p = jnp.exp2(s - new)
            alpha = jnp.exp2(old - new)
            row_max[...] = new
            row_sum[...] = row_sum[...] * alpha + jnp.sum(p, axis=0, keepdims=True)
            acc_o[...] = acc_o[...] * alpha + mm(vt[c], p.astype(bf16))

        def forward_step(c, carry):
            forward(c, False)
            return carry

        lax.fori_loop(0, last, forward_step, 0)
        forward(last, True)

        total = row_sum[...]
        ctx_t = (acc_o[...] / total).astype(bf16)
        row_max[...] = row_max[...] + jnp.log2(total)
        row_delta[...] = jnp.sum(ctx_t.astype(f32) * gt[...].astype(f32), axis=0, keepdims=True)
        for h in range(heads):
            part = slice(h * span, (h + 1) * span)
            ctx_ref[pl.ds(row0, span), part] = ctx_t[:, part].T
        acc_q[...] = jnp.zeros_like(acc_q)

        def backward(c, masked):
            s = mm(ks[c], qt[...])
            p = jnp.exp2(s - row_max[...])
            if masked:
                p = jnp.where(allowed(c), p, 0.0)
            dp = mm(vs[c], gt[...])
            ds = (p * (dp - row_delta[...])).astype(bf16)
            acc_kv[c, :, span:] += mm(p.astype(bf16), gs[...])
            acc_kv[c, :, :span] += mm(ds, qs[...])
            acc_q[...] += mm(kt[c], ds)

        def backward_step(c, carry):
            backward(c, False)
            return carry

        lax.fori_loop(0, last, backward_step, 0)
        backward(last, True)
        for h in range(heads):
            part = slice(h * span, (h + 1) * span)
            dq_ref[pl.ds(row0, span), part] = acc_q[:, part].T * (span**-0.5)

    def give(c, carry):
        for j in range(per_chunk):
            part = slice(j * span, (j + 1) * span)
            slot = slot_of[c * per_chunk + j]
            pair, rows_at = slot // 4, pl.multiple_of(slot % 2 * span, span)
            mine = (slot // 2) % 2 == core
            dk = (acc_kv[c, part, :span] * math.log(2.0)).astype(bf16)
            dv = acc_kv[c, part, span:].astype(bf16)

            @pl.when(mine)
            def _():
                dkv_ref[pair, pl.ds(rows_at, span), :span] = dk
                dkv_ref[pair, pl.ds(rows_at, span), span:] = dv

            @pl.when(jnp.logical_not(mine))
            def _():
                dkv_other_ref[pair, pl.ds(rows_at, span), :span] = dk
                dkv_other_ref[pair, pl.ds(rows_at, span), span:] = dv

        return carry

    lax.fori_loop(0, chunks, give, 0)


def attention(order, own, q16, g16, kv, kv_other):
    rows_here, cols = q16.shape
    spans = order.shape[0]
    chunks = spans // per_chunk
    rows = cols
    share = jax.ShapeDtypeStruct(kv.shape, bf16)
    return pl.pallas_call(
        attention_kernel,
        out_shape=(
            jax.ShapeDtypeStruct((rows_here, cols), bf16),
            jax.ShapeDtypeStruct((rows_here, cols), f32),
            share,
            share,
        ),
        in_specs=[smem, smem] + [vmem] * 4,
        out_specs=(vmem,) * 4,
        scratch_shapes=[
            pltpu.SMEM((spans,), jnp.int32),
            pltpu.VMEM((chunks, chunk, span), bf16),
            pltpu.VMEM((chunks, chunk, span), bf16),
            pltpu.VMEM((chunks, span, chunk), bf16),
            pltpu.VMEM((chunks, span, chunk), bf16),
            pltpu.VMEM((chunks, chunk, 2 * span), f32),
            pltpu.VMEM((rows, span), bf16),
            pltpu.VMEM((rows, span), bf16),
            pltpu.VMEM((span, rows), bf16),
            pltpu.VMEM((span, rows), bf16),
            pltpu.VMEM((span, rows), f32),
            pltpu.VMEM((1, rows), f32),
            pltpu.VMEM((1, rows), f32),
            pltpu.VMEM((1, rows), f32),
            pltpu.VMEM((span, rows), f32),
        ],
        compiler_params=pltpu.CompilerParams(vmem_limit_bytes=48 * mib),
        cost_estimate=cheap,
        name="attention",
    )(order, own, q16, g16, kv, kv_other)


def grad_query_kernel(raw_ref, dq_ref, gain_ref, cos_ref, sin_ref, g_ref, gain_out):
    cosine, sine = cos_ref[...], sin_ref[...]
    sums = jnp.zeros((1, span), f32)
    for h in range(dq_ref.shape[1] // span):
        part = slice(h * span, (h + 1) * span)
        grad, terms = shape_head_grad(
            raw_ref[:, part].astype(f32), gain_ref[...], cosine, sine, dq_ref[:, part]
        )
        g_ref[:, part] = grad.astype(bf16)
        sums = sums + jnp.sum(terms, axis=0, keepdims=True)
    gain_out[...] = jnp.broadcast_to(sums, gain_out.shape)


def grad_key_value_kernel(raw_ref, dkv_ref, gain_ref, cos_ref, sin_ref, gain_q_ref, g_ref):
    rows = raw_ref.shape[0]
    dkv = jnp.sum(dkv_ref[...].astype(f32), axis=0)
    grad, terms = shape_head_grad(
        raw_ref[:, -span:].astype(f32), gain_ref[...], cos_ref[...], sin_ref[...], dkv[:, :span]
    )
    g_ref[:rows, :span] = grad.astype(bf16)
    g_ref[:rows, span:] = dkv[:, span:].astype(bf16)
    gain_k = jnp.sum(terms, axis=0, keepdims=True)
    split = []
    for gain in (gain_q_ref[0:1], gain_k):
        high = gain.astype(bf16).astype(f32)
        split.append(jnp.concatenate([high, gain - high], axis=1))
    row = lax.broadcasted_iota(jnp.int32, (g_ref.shape[0] - rows, 2 * span), 0)
    g_ref[rows:] = jnp.where(row == 0, split[0], jnp.where(row == 1, split[1], 0.0)).astype(bf16)


def weight_grad_kernel(where, turned_ref, *rest):
    blocks, out_ref = rest[:-1], rest[-1]
    columns = len(blocks) // 2
    toks = turned_ref.shape[2]
    y, core = where[0], where[1]
    total, gains = None, None
    for side in range(2):
        for k in range(columns):
            from_y = lax.rem(y + k, columns)
            from_core = core if side == 0 else 1 - core
            at = (from_core * 2 + lax.rem(from_y, 2)) * 2 + from_y // 2
            block = blocks[side * columns + k]
            part = mm(turned_ref[at], block[:toks])
            total = part if total is None else total + part
            if block.shape[0] > toks:
                row = block[toks:].astype(f32)
                gains = row if gains is None else gains + row
    own_rows = total.shape[0] // out_ref.shape[0]
    extra = []
    if gains is not None:
        gain = gains[:, :span] + gains[:, span:]
        high = gain.astype(bf16).astype(f32)
        extra = [jnp.concatenate([high, gain - high], axis=1)[:8]]
    for i in range(out_ref.shape[0]):
        part = total[i * own_rows : (i + 1) * own_rows]
        out_ref[i] = jnp.concatenate([part] + extra, axis=0).astype(bf16)


def weight_grad(where, turned, blocks, planes, padded, after=()):
    return call(
        weight_grad_kernel,
        jax.ShapeDtypeStruct((planes, padded, blocks[0].shape[1]), bf16),
        where, turned, *blocks,
        name="weight_grad",
        after=after,
    )


transposed = (((1,), (1,)), ((), ()))


def grad_states_query_kernel(where, gq_ref, low_ref, low_theirs_ref, *rest):
    highs, (out_ref, loaded, loaded_high, sems) = rest[:-4], rest[-4:]
    columns, cols = loaded.shape[1], loaded.shape[3]
    y, core = where[0], where[1]
    copies = [pltpu.make_async_copy(low, loaded.at[i], sems.at[i]) for i, low in enumerate((low_ref, low_theirs_ref))]
    copies += [pltpu.make_async_copy(high, loaded_high.at[i], sems.at[2 + i]) for i, high in enumerate(highs)]
    for copy in copies:
        copy.start()
    for side in range(2):
        at_core = core if side == 0 else 1 - core
        copies[side].wait()
        for k in range(columns):
            at = lax.rem(y + k, columns)
            copies[2 + side * columns + k].wait()
            out_ref[at, at_core] = (
                lax.dot_general(loaded[side, at], gq_ref[:, :cols], transposed, preferred_element_type=f32)
                + lax.dot_general(
                    loaded_high[side * columns + k], gq_ref[:, cols:], transposed, preferred_element_type=f32
                )
            ).astype(bf16)


def grad_states_kernel(where, gkv_ref, query_ref, kv_ref, kv_theirs_ref, out_ref, blocks):
    core = where[1]
    columns, own_rows = kv_ref.shape[0], 40
    toks = out_ref.shape[0]
    for at_core, kv in ((core, kv_ref), (1 - core, kv_theirs_ref)):
        for y in range(columns):
            blocks[y, at_core] = query_ref[y, at_core].astype(f32) + lax.dot_general(
                kv[y], gkv_ref[:toks], transposed, preferred_element_type=f32
            )
    for x in range(4):
        pieces = []
        for z in range(4):
            part = slice((z * 4 + x) * own_rows, (z * 4 + x + 1) * own_rows)
            pieces += [blocks[at, c, part] for at in range(columns) for c in range(2)]
        rows = jnp.concatenate(pieces, axis=0)
        out_ref[:, x * rows.shape[0] : (x + 1) * rows.shape[0]] = rows.astype(bf16).T


def finish_kernel(parts_ref, key_ref, value_ref, gain_q_ref, gain_k_ref):
    sums = jnp.sum(parts_ref[...].astype(f32), axis=0)
    rows = key_ref.shape[0]
    key_ref[...] = sums[:rows, :span]
    value_ref[...] = sums[:rows, span:]
    gains = sums[rows:, :span] + sums[rows:, span:]
    gain_q_ref[...] = gains[0:1]
    gain_k_ref[...] = gains[1:2]


cheap = pl.CostEstimate(flops=1000, bytes_accessed=1000, transcendentals=0)


def call(kernel, shapes, *args, name, after=()):
    count = len(args)

    def run(*refs):
        kernel(*refs[:count], *refs[count + len(after) :])

    return pl.pallas_call(
        run,
        out_shape=shapes,
        in_specs=[smem if a.dtype == jnp.int32 else vmem for a in args] + [anywhere] * len(after),
        out_specs=jax.tree.map(lambda _: vmem, shapes),
        compiler_params=pltpu.CompilerParams(vmem_limit_bytes=48 * mib),
        cost_estimate=cheap,
        name=name,
    )(*args, *after)


plane = ("x", "z")
owners = ("z", "x")
column = ("y_hi", "y_lo")
chips = column + owners
swapped = [(0, 0), (1, 2), (2, 1), (3, 3)]
flipped = [(0, 1), (1, 0)]


def swap(array):
    return lax.ppermute(array, ("y_hi", "core"), swapped)


def flip(array):
    return lax.ppermute(array, "core", flipped)


def to_all(array, axes, count):
    return lax.all_to_all(jnp.broadcast_to(array[None], (count,) + array.shape), axes, 0, 0)


def ring(array, step):
    return lax.ppermute(array, column, [(i, (i - step) % 4) for i in range(4)])


def around(array):
    mine = [array] + [ring(array, k) for k in range(1, 4)]
    return mine + [flip(a) for a in mine]


def local(hidden_states, block_order, w_query, w_key, w_value, gain_query, gain_key, cotangent):
    tokens = hidden_states[0]
    tok_rows, width = tokens.shape
    q_cols = w_query.shape[1]
    kv_cols = 2 * span
    own_rows = w_query.shape[0]
    planes, columns = 16, 4
    half = width // 2
    place = lax.axis_index("x") * 4 + lax.axis_index("z")
    y_hi, core = lax.axis_index("y_hi"), lax.axis_index("core")
    y = y_hi * 2 + lax.axis_index("y_lo")
    where = jnp.stack([y, core]).astype(jnp.int32)
    offsets = jnp.arange(span, dtype=jnp.int32)

    def angles_of(part):
        blocks = lax.dynamic_slice_in_dim(block_order, 2 * (place * 2 + part), 2)
        positions = (blocks[:, None] * span + offsets[None, :]).reshape(tok_rows)
        return blocks, rotation(positions, span)

    _, (cosine, sine) = angles_of(y_hi)
    own_blocks, (cos_there, sin_there) = angles_of(core)
    own = jnp.concatenate([own_blocks, core[None].astype(jnp.int32)])
    gain_q, gain_k = gain_query[None, :], gain_key[None, :]
    shape = jax.ShapeDtypeStruct

    kv_mine = to_all(jnp.concatenate([w_key, w_value], axis=1), chips, planes * columns)
    kv_mine = kv_mine.reshape(columns, half // columns, kv_cols)

    early = (cosine, sine, cos_there, sin_there)
    toks_mine, toks_theirs, turned, done = pl.pallas_call(
        prepare_kernel,
        out_shape=(shape((columns, tok_rows, half // columns), bf16),) * 2
        + (shape((2 * columns, half // columns, tok_rows), bf16), shape((8, span), f32)),
        in_specs=[smem, vmem] + [anywhere] * len(early),
        out_specs=(vmem,) * 4,
        compiler_params=pltpu.CompilerParams(vmem_limit_bytes=48 * mib),
        cost_estimate=cheap,
        name="prepare",
    )(where, tokens.T.reshape(4, 4, columns, 2, own_rows, tok_rows), *early)
    w_low = w_query[:, :kv_cols]
    w_both = jnp.concatenate([w_low] + [ring(w_low, k) for k in range(1, columns)] + [w_query[:, kv_cols:]])
    kv_mine, w_both, done, own = lax.optimization_barrier((kv_mine, w_both, done, own))
    kv_theirs = flip(kv_mine)
    q_low, q_high = call(
        split_kernel,
        (shape((columns, half // columns, kv_cols), bf16), shape((half // columns, kv_cols), bf16)),
        where, to_all(w_both, owners, planes),
        name="split",
    )

    kv16, raw_k = call(
        key_value_kernel,
        (shape((tok_rows, kv_cols), bf16), shape((tok_rows, span), f32)),
        toks_mine, toks_theirs, kv_mine, kv_theirs, gain_k, cosine, sine,
        name="key_value",
        after=(done,),
    )
    kv_send = jnp.broadcast_to(swap(kv16)[None], (planes, tok_rows, kv_cols))
    kv_send, q_high = lax.optimization_barrier((kv_send, q_high))
    kv_own = lax.all_to_all(kv_send, plane, 0, 0)
    low_theirs = flip(q_low)
    highs = [q_high] + [ring(q_high, k) for k in range(1, columns)]
    highs += [flip(block) for block in highs]
    grad_out = swap(cotangent[0])
    q16, raw = call(
        query_kernel,
        (shape((tok_rows, q_cols), bf16), shape((tok_rows, q_cols + span), bf16)),
        where, toks_mine, toks_theirs, q_low, low_theirs, *highs, raw_k, gain_q, cosine, sine,
        name="query",
        after=(grad_out,),
    )
    kv_own, raw = lax.optimization_barrier((kv_own, raw))
    kv_other = flip(kv_own)
    q16 = swap(q16)
    turned, raw, q_piece = lax.optimization_barrier((turned, raw, q16[:8, :span]))
    turned = lax.all_to_all(turned, column + ("core",), 0, 0)
    raw_there = swap(raw)

    ctx, dq, dkv_mine, dkv_theirs = attention(
        block_order, own, q16, grad_out, kv_own, kv_other
    )
    dkv_theirs, turned, raw_there = lax.optimization_barrier((dkv_theirs, turned, raw_there))
    dkv = (dkv_mine.astype(f32) + flip(dkv_theirs).astype(f32)).astype(bf16)
    dkv = lax.all_to_all(dkv, plane, 0, 0)

    g_q, gains_q = call(
        grad_query_kernel,
        (shape((tok_rows, q_cols), bf16), shape((8, span), f32)),
        raw_there, dq, gain_q, cos_there, sin_there,
        name="grad_query",
        after=(q_piece,),
    )
    grad_states_query = pl.pallas_call(
        grad_states_query_kernel,
        out_shape=shape((columns, 2, half // columns, tok_rows), bf16),
        in_specs=[smem, vmem] + [anywhere] * (2 + 2 * columns),
        out_specs=vmem,
        scratch_shapes=[
            pltpu.VMEM((2, columns, half // columns, kv_cols), bf16),
            pltpu.VMEM((2 * columns, half // columns, kv_cols), bf16),
            pltpu.SemaphoreType.DMA((2 + 2 * columns,)),
        ],
        compiler_params=pltpu.CompilerParams(vmem_limit_bytes=48 * mib),
        cost_estimate=cheap,
        name="grad_states_query",
    )(where, swap(g_q), q_low, low_theirs, *highs)
    blocks_q = around(g_q)
    dkv, grad_states_query = lax.optimization_barrier((dkv, grad_states_query))

    g_kv = call(
        grad_key_value_kernel,
        shape((tok_rows + 16, kv_cols), bf16),
        raw_there, dkv, gain_k, cos_there, sin_there, gains_q,
        name="grad_key_value",
    )
    blocks_kv = around(g_kv)
    parts = weight_grad(where, turned, blocks_q, planes, own_rows, after=(blocks_kv[1],))
    parts = lax.all_to_all(parts, owners, 0, 0)
    own_query = jnp.sum(parts.astype(f32), axis=0)
    parts = weight_grad(where, turned, blocks_kv, planes, own_rows + 8)
    parts = lax.all_to_all(parts, owners, 0, 0)
    own_key, own_value, gain_sum_q, gain_sum_k = call(
        finish_kernel,
        (shape((own_rows, span), f32),) * 2 + (shape((1, span), f32),) * 2,
        parts,
        name="finish",
    )

    grad_states = pl.pallas_call(
        grad_states_kernel,
        out_shape=shape((tok_rows, width), bf16),
        in_specs=[smem] + [vmem] * 4,
        out_specs=vmem,
        scratch_shapes=[pltpu.VMEM((columns, 2, half // columns, tok_rows), f32)],
        compiler_params=pltpu.CompilerParams(vmem_limit_bytes=48 * mib),
        cost_estimate=cheap,
        name="grad_states",
    )(where, swap(g_kv), grad_states_query, kv_mine, kv_theirs)
    return (
        swap(ctx)[None],
        grad_states[None],
        own_query,
        own_key,
        own_value,
        gain_sum_q[0],
        gain_sum_k[0],
    )


def solution(mesh):
    fine = Mesh(mesh.devices.reshape(4, 4, 2, 2, 2), ("x", "z", "y_hi", "y_lo", "core"))
    ctx, dp = ("x", "z", "y_hi"), ("y_lo", "core")
    rows = P(ctx + dp, None)
    tokens = P(dp, ctx, None)
    in_specs = (tokens, P(), rows, rows, rows, P(), P(), tokens)
    out_specs = (tokens, tokens, rows, rows, rows, P(), P())
    return jax.shard_map(local, mesh=fine, in_specs=in_specs, out_specs=out_specs, check_vma=False)
```

```python
import math

import jax
import jax.numpy as jnp
from jax import lax
from jax.experimental import pallas as pl
from jax.experimental.pallas import tpu as pltpu
from jax.sharding import Mesh
from jax.sharding import PartitionSpec as P

bf16, f32 = jnp.bfloat16, jnp.float32
theta = 1000000.0
floor_score = -1e30
span = 128
chunk = 512
per_chunk = chunk // span
mib = 2**20
smem = pl.BlockSpec(memory_space=pltpu.SMEM)
vmem = pl.BlockSpec(memory_space=pltpu.VMEM)
anywhere = pl.BlockSpec(memory_space=pl.ANY)


def mm(a, b):
    return jnp.dot(a, b, preferred_element_type=f32)


def rotation(positions, head_width):
    steps_half = jnp.arange(head_width // 2, dtype=f32)
    inverse = jnp.power(f32(theta), -2.0 * steps_half / head_width)
    angles = positions.astype(f32)[:, None] * inverse[None, :]
    cosine = jnp.cos(angles)
    sine = jnp.sin(angles)
    return jnp.concatenate([cosine, cosine], 1), jnp.concatenate([-sine, sine], 1)


def inverse_norm(raw):
    return lax.rsqrt(jnp.mean(raw * raw, axis=-1, keepdims=True) + 1e-06)


def shape_head(raw, gain, cosine, sine):
    normed = raw * inverse_norm(raw) * gain
    return normed * cosine + pltpu.roll(normed, span // 2, 1) * sine


def shape_head_grad(raw, gain, cosine, sine, grad):
    inverse = inverse_norm(raw)
    grad_normed = grad * cosine + pltpu.roll(grad * sine, span // 2, 1)
    grad_unit = grad_normed * gain
    unit = raw * inverse
    shrink = jnp.mean(grad_unit * unit, axis=-1, keepdims=True)
    return inverse * (grad_unit - unit * shrink), grad_normed * unit


def prepare_kernel(where, src_ref, toks_ref, toks_theirs_ref, turned_ref, done_ref):
    planes, columns = src_ref.shape[:2]
    core = where[1]
    done_ref[...] = jnp.zeros_like(done_ref)

    def piece(plane, y, side):
        return src_ref[plane, y, side].astype(f32)

    group = 4
    for side, out_ref in ((core, toks_ref), (1 - core, toks_theirs_ref)):
        for i in range(0, planes, group):
            rows = jnp.concatenate(
                [piece(i + j, y, side) for j in range(group) for y in range(columns)], axis=0
            ).astype(bf16)
            wide = rows.shape[0]
            out_ref[:, i // group * wide : (i // group + 1) * wide] = rows.T
    for y in range(columns):
        for side in range(2):
            turned_ref[2 * y + side] = jnp.concatenate(
                [piece(i, y, side) for i in range(planes)], axis=0
            ).astype(bf16)


def key_value_kernel(mine_ref, other_ref, w_ref, w_other_ref, gain_ref, cos_ref, sin_ref, kv_ref, raw_ref):
    raw = mm(mine_ref[...], w_ref[...]) + mm(other_ref[...], w_other_ref[...])
    raw_ref[...] = raw[:, :span]
    kv_ref[:, :span] = shape_head(raw[:, :span], gain_ref[...], cos_ref[...], sin_ref[...]).astype(bf16)
    kv_ref[:, span:] = raw[:, span:].astype(bf16)


def query_kernel(mine_ref, other_ref, w_ref, w_other_ref, raw_k_ref, gain_ref, cos_ref, sin_ref, q_ref, raw_ref):
    rows = mm(mine_ref[...], w_ref[...]) + mm(other_ref[...], w_other_ref[...])
    raw_ref[:, -span:] = raw_k_ref[...].astype(bf16)
    gain = gain_ref[...] * (span**-0.5 / math.log(2.0))
    for h in range(q_ref.shape[1] // span):
        part = slice(h * span, (h + 1) * span)
        raw_ref[:, part] = rows[:, part].astype(bf16)
        q_ref[:, part] = shape_head(rows[:, part], gain, cos_ref[...], sin_ref[...]).astype(bf16)


def attention_kernel(
    order, own, q_ref, g_ref, kv_ref, kv_other_ref, ctx_ref, dq_ref, dkv_ref, dkv_other_ref,
    slot_of, ks, vs, kt, vt, acc_kv, qs, gs, qt, gt, acc_o, row_max, row_sum, row_delta, acc_q,
):
    spans, heads = order.shape[0], q_ref.shape[1] // span
    chunks = spans // per_chunk
    rows = heads * span
    core = own[2]

    def place(slot, carry):
        slot_of[order[slot]] = slot
        return carry

    lax.fori_loop(0, spans, place, 0)

    def arrange(c, carry):
        for j in range(per_chunk):
            slot = slot_of[c * per_chunk + j]
            pair, rows_at = slot // 4, pl.multiple_of(slot % 2 * span, span)
            mine = (slot // 2) % 2 == core
            both = jnp.where(
                mine, kv_ref[pair, pl.ds(rows_at, span), :], kv_other_ref[pair, pl.ds(rows_at, span), :]
            )
            part = slice(j * span, (j + 1) * span)
            ks[c, part, :] = both[:, :span]
            vs[c, part, :] = both[:, span:]
            kt[c, :, part] = both[:, :span].T
            vt[c, :, part] = both[:, span:].T
        acc_kv[c] = jnp.zeros_like(acc_kv[c])
        return carry

    lax.fori_loop(0, chunks, arrange, 0)

    first_upper = own[0] > own[1]
    for upper in (True, False):
        which = jnp.where(first_upper, 0, 1) if upper else jnp.where(first_upper, 1, 0)
        block = own[which]
        row0 = pl.multiple_of(which * span, span)
        last = block // per_chunk
        for h in range(heads):
            part = slice(h * span, (h + 1) * span)
            qh = q_ref[pl.ds(row0, span), part]
            gh = g_ref[pl.ds(row0, span), part]
            qs[part, :] = qh
            gs[part, :] = gh
            qt[:, part] = qh.T
            gt[:, part] = gh.T

        def allowed(c):
            key_pos = c * chunk + lax.broadcasted_iota(jnp.int32, (chunk, rows), 0)
            row = lax.broadcasted_iota(jnp.int32, (chunk, rows), 1)
            return key_pos <= block * span + jnp.bitwise_and(row, span - 1)

        row_max[...] = jnp.full_like(row_max, floor_score)
        row_sum[...] = jnp.zeros_like(row_sum)
        acc_o[...] = jnp.zeros_like(acc_o)

        def forward(c, masked):
            s = mm(ks[c], qt[...])
            if masked:
                s = jnp.where(allowed(c), s, floor_score)
            old = row_max[...]
            new = jnp.maximum(old, jnp.max(s, axis=0, keepdims=True))
            p = jnp.exp2(s - new)
            alpha = jnp.exp2(old - new)
            row_max[...] = new
            row_sum[...] = row_sum[...] * alpha + jnp.sum(p, axis=0, keepdims=True)
            acc_o[...] = acc_o[...] * alpha + mm(vt[c], p.astype(bf16))

        def forward_step(c, carry):
            forward(c, False)
            return carry

        lax.fori_loop(0, last, forward_step, 0)
        forward(last, True)

        total = row_sum[...]
        ctx_t = (acc_o[...] / total).astype(bf16)
        row_max[...] = row_max[...] + jnp.log2(total)
        row_delta[...] = jnp.sum(ctx_t.astype(f32) * gt[...].astype(f32), axis=0, keepdims=True)
        for h in range(heads):
            part = slice(h * span, (h + 1) * span)
            ctx_ref[pl.ds(row0, span), part] = ctx_t[:, part].T
        acc_q[...] = jnp.zeros_like(acc_q)

        def backward(c, masked):
            s = mm(ks[c], qt[...])
            p = jnp.exp2(s - row_max[...])
            if masked:
                p = jnp.where(allowed(c), p, 0.0)
            dp = mm(vs[c], gt[...])
            ds = (p * (dp - row_delta[...])).astype(bf16)
            acc_kv[c, :, span:] += mm(p.astype(bf16), gs[...])
            acc_kv[c, :, :span] += mm(ds, qs[...])
            acc_q[...] += mm(kt[c], ds)

        def backward_step(c, carry):
            backward(c, False)
            return carry

        lax.fori_loop(0, last, backward_step, 0)
        backward(last, True)
        for h in range(heads):
            part = slice(h * span, (h + 1) * span)
            dq_ref[pl.ds(row0, span), part] = acc_q[:, part].T * (span**-0.5)

    def give(c, carry):
        for j in range(per_chunk):
            part = slice(j * span, (j + 1) * span)
            slot = slot_of[c * per_chunk + j]
            pair, rows_at = slot // 4, pl.multiple_of(slot % 2 * span, span)
            mine = (slot // 2) % 2 == core
            dk = (acc_kv[c, part, :span] * math.log(2.0)).astype(bf16)
            dv = acc_kv[c, part, span:].astype(bf16)

            @pl.when(mine)
            def _():
                dkv_ref[pair, pl.ds(rows_at, span), :span] = dk
                dkv_ref[pair, pl.ds(rows_at, span), span:] = dv

            @pl.when(jnp.logical_not(mine))
            def _():
                dkv_other_ref[pair, pl.ds(rows_at, span), :span] = dk
                dkv_other_ref[pair, pl.ds(rows_at, span), span:] = dv

        return carry

    lax.fori_loop(0, chunks, give, 0)


def attention(order, own, q16, g16, kv, kv_other):
    rows_here, cols = q16.shape
    spans = order.shape[0]
    chunks = spans // per_chunk
    rows = cols
    share = jax.ShapeDtypeStruct(kv.shape, bf16)
    return pl.pallas_call(
        attention_kernel,
        out_shape=(
            jax.ShapeDtypeStruct((rows_here, cols), bf16),
            jax.ShapeDtypeStruct((rows_here, cols), f32),
            share,
            share,
        ),
        in_specs=[smem, smem] + [vmem] * 4,
        out_specs=(vmem,) * 4,
        scratch_shapes=[
            pltpu.SMEM((spans,), jnp.int32),
            pltpu.VMEM((chunks, chunk, span), bf16),
            pltpu.VMEM((chunks, chunk, span), bf16),
            pltpu.VMEM((chunks, span, chunk), bf16),
            pltpu.VMEM((chunks, span, chunk), bf16),
            pltpu.VMEM((chunks, chunk, 2 * span), f32),
            pltpu.VMEM((rows, span), bf16),
            pltpu.VMEM((rows, span), bf16),
            pltpu.VMEM((span, rows), bf16),
            pltpu.VMEM((span, rows), bf16),
            pltpu.VMEM((span, rows), f32),
            pltpu.VMEM((1, rows), f32),
            pltpu.VMEM((1, rows), f32),
            pltpu.VMEM((1, rows), f32),
            pltpu.VMEM((span, rows), f32),
        ],
        compiler_params=pltpu.CompilerParams(vmem_limit_bytes=28 * mib),
        cost_estimate=pl.CostEstimate(
            flops=1000, bytes_accessed=1000, transcendentals=0
        ),
        name="attention",
    )(order, own, q16, g16, kv, kv_other)


def grad_query_kernel(raw_ref, dq_ref, gain_ref, cos_ref, sin_ref, g_ref, gain_out):
    cosine, sine = cos_ref[...], sin_ref[...]
    sums = jnp.zeros((1, span), f32)
    for h in range(dq_ref.shape[1] // span):
        part = slice(h * span, (h + 1) * span)
        grad, terms = shape_head_grad(
            raw_ref[:, part].astype(f32), gain_ref[...], cosine, sine, dq_ref[:, part]
        )
        g_ref[:, part] = grad.astype(bf16)
        sums = sums + jnp.sum(terms, axis=0, keepdims=True)
    gain_out[...] = jnp.broadcast_to(sums, gain_out.shape)


def grad_key_value_kernel(raw_ref, dkv_ref, gain_ref, cos_ref, sin_ref, gain_q_ref, g_ref):
    rows = raw_ref.shape[0]
    dkv = jnp.sum(dkv_ref[...].astype(f32), axis=0)
    grad, terms = shape_head_grad(
        raw_ref[:, -span:].astype(f32), gain_ref[...], cos_ref[...], sin_ref[...], dkv[:, :span]
    )
    g_ref[:rows, :span] = grad.astype(bf16)
    g_ref[:rows, span:] = dkv[:, span:].astype(bf16)
    gain_k = jnp.sum(terms, axis=0, keepdims=True)
    split = []
    for gain in (gain_q_ref[0:1], gain_k):
        high = gain.astype(bf16).astype(f32)
        split.append(jnp.concatenate([high, gain - high], axis=1))
    row = lax.broadcasted_iota(jnp.int32, (g_ref.shape[0] - rows, 2 * span), 0)
    g_ref[rows:] = jnp.where(row == 0, split[0], jnp.where(row == 1, split[1], 0.0)).astype(bf16)


def weight_grad_kernel(where, turned_ref, *rest):
    blocks, out_ref = rest[:-1], rest[-1]
    count = len(blocks) // 2
    columns = count // 2
    toks = turned_ref.shape[2]
    y, core = where[0], where[1]
    query, rows, gains = 0.0, 0.0, 0.0
    for i in range(count):
        from_y = lax.rem(y + i % columns, columns)
        from_core = core if i < columns else 1 - core
        at = (from_core * 2 + lax.rem(from_y, 2)) * 2 + from_y // 2
        query = query + mm(turned_ref[at], blocks[i][...])
        rows = rows + mm(turned_ref[at], blocks[count + i][:toks])
        gains = gains + blocks[count + i][toks:].astype(f32)
    gain = gains[:8, :span] + gains[:8, span:]
    high = gain.astype(bf16).astype(f32)
    extra = jnp.concatenate([jnp.zeros((8, query.shape[1]), f32), high, gain - high], axis=1)
    total = jnp.concatenate([query, rows], axis=1)
    own_rows = total.shape[0] // out_ref.shape[0]
    for i in range(out_ref.shape[0]):
        part = total[i * own_rows : (i + 1) * own_rows]
        out_ref[i] = jnp.concatenate([part, extra], axis=0).astype(bf16)


def grad_states_kernel(where, gq_ref, gkv_ref, q_ref, q_theirs_ref, kv_ref, kv_theirs_ref, out_ref):
    core = where[1]
    own_rows, group = 40, 640
    transposed = (((1,), (1,)), ((), ()))

    def product(q, kv, i):
        part = slice(i * group, (i + 1) * group)
        return lax.dot_general(
            q[part], gq_ref[...], transposed, preferred_element_type=f32
        ) + lax.dot_general(kv[part], gkv_ref[: gq_ref.shape[0]], transposed, preferred_element_type=f32)

    for i in range(q_ref.shape[0] // group):
        mine, theirs = product(q_ref, kv_ref, i), product(q_theirs_ref, kv_theirs_ref, i)
        sides = (jnp.where(core == 0, mine, theirs), jnp.where(core == 0, theirs, mine))
        rows = jnp.concatenate(
            [side[j : j + own_rows] for j in range(0, group, own_rows) for side in sides], axis=0
        )
        out_ref[:, 2 * i * group : 2 * (i + 1) * group] = rows.astype(bf16).T


def finish_kernel(parts_ref, query_ref, key_ref, value_ref, gain_q_ref, gain_k_ref):
    sums = jnp.sum(parts_ref[...].astype(f32), axis=0)
    rows, cols = query_ref.shape
    query_ref[...] = sums[:rows, :cols]
    key_ref[...] = sums[:rows, cols : cols + span]
    value_ref[...] = sums[:rows, cols + span :]
    gains = sums[rows:, cols : cols + span] + sums[rows:, cols + span :]
    gain_q_ref[...] = gains[0:1]
    gain_k_ref[...] = gains[1:2]


cheap = pl.CostEstimate(flops=1000, bytes_accessed=1000, transcendentals=0)


def call(kernel, shapes, *args, name, after=(), limit=16, scratch=()):
    count = len(args)

    def run(*refs):
        kernel(*refs[:count], *refs[count + len(after) :])

    return pl.pallas_call(
        run,
        out_shape=shapes,
        in_specs=[smem if a.dtype == jnp.int32 else vmem for a in args] + [anywhere] * len(after),
        out_specs=jax.tree.map(lambda _: vmem, shapes),
        scratch_shapes=scratch,
        compiler_params=pltpu.CompilerParams(vmem_limit_bytes=limit * mib),
        cost_estimate=cheap,
        name=name,
    )(*args, *after)


plane = ("x", "z")
column = ("y_hi", "y_lo")
chips = plane + column
swapped = [(0, 0), (1, 2), (2, 1), (3, 3)]
flipped = [(0, 1), (1, 0)]


def swap(array):
    return lax.ppermute(array, ("y_hi", "core"), swapped)


def flip(array):
    return lax.ppermute(array, "core", flipped)


def to_all(array, axes, count):
    return lax.all_to_all(jnp.broadcast_to(array[None], (count,) + array.shape), axes, 0, 0)


def ring(array, step):
    return lax.ppermute(array, column, [(i, (i - step) % 4) for i in range(4)])


def around(array):
    mine = [array] + [ring(array, k) for k in range(1, 4)]
    return mine + [flip(a) for a in mine]


def local(hidden_states, block_order, w_query, w_key, w_value, gain_query, gain_key, cotangent):
    tokens = hidden_states[0]
    tok_rows, width = tokens.shape
    q_cols = w_query.shape[1]
    kv_cols = 2 * span
    own_rows = w_query.shape[0]
    planes, columns = 16, 4
    half = width // 2
    place = lax.axis_index("x") * 4 + lax.axis_index("z")
    y_hi, core = lax.axis_index("y_hi"), lax.axis_index("core")
    y = y_hi * 2 + lax.axis_index("y_lo")
    where = jnp.stack([y, core]).astype(jnp.int32)
    offsets = jnp.arange(span, dtype=jnp.int32)

    def angles_of(part):
        blocks = lax.dynamic_slice_in_dim(block_order, 2 * (place * 2 + part), 2)
        positions = (blocks[:, None] * span + offsets[None, :]).reshape(tok_rows)
        return blocks, rotation(positions, span)

    _, (cosine, sine) = angles_of(y_hi)
    own_blocks, (cos_there, sin_there) = angles_of(core)
    own = jnp.concatenate([own_blocks, core[None].astype(jnp.int32)])
    gain_q, gain_k = gain_query[None, :], gain_key[None, :]
    shape = jax.ShapeDtypeStruct

    kv_mine = to_all(jnp.concatenate([w_key, w_value], axis=1), chips, planes * columns)
    toks_mine, toks_theirs, turned, done = call(
        prepare_kernel,
        (shape((tok_rows, half), bf16),) * 2
        + (shape((2 * columns, width // 8, tok_rows), bf16), shape((8, span), f32)),
        where, tokens.T.reshape(planes, columns, 2, own_rows, tok_rows),
        name="prepare",
        after=(cosine, sine, cos_there, sin_there),
    )
    kv_mine, w_query, done, own = lax.optimization_barrier((kv_mine, w_query, done, own))
    kv_mine = kv_mine.reshape(half, kv_cols)
    kv_theirs = flip(kv_mine)
    q_mine = to_all(w_query, chips, planes * columns).reshape(half, q_cols)

    kv16, raw_k = call(
        key_value_kernel,
        (shape((tok_rows, kv_cols), bf16), shape((tok_rows, span), f32)),
        toks_mine, toks_theirs, kv_mine, kv_theirs, gain_k, cosine, sine,
        name="key_value",
        after=(done,),
    )
    kv16, q_mine = lax.optimization_barrier((swap(kv16), q_mine))
    kv_own = to_all(kv16, plane, planes)
    q_theirs = flip(q_mine)
    grad_out = swap(cotangent[0])
    q16, raw = call(
        query_kernel,
        (shape((tok_rows, q_cols), bf16), shape((tok_rows, q_cols + span), bf16)),
        toks_mine, toks_theirs, q_mine, q_theirs, raw_k, gain_q, cosine, sine,
        name="query",
        after=(grad_out,),
    )
    q16, raw_there = swap(q16), swap(raw)
    kv_own, q16 = lax.optimization_barrier((kv_own, q16))
    kv_other = flip(kv_own)
    turned = lax.all_to_all(turned, column + ("core",), 0, 0)

    ctx, dq, dkv_mine, dkv_theirs = attention(block_order, own, q16, grad_out, kv_own, kv_other)
    dkv_theirs, turned = lax.optimization_barrier((dkv_theirs, turned))
    dkv = (dkv_mine.astype(f32) + flip(dkv_theirs).astype(f32)).astype(bf16)
    dkv = lax.all_to_all(dkv, plane, 0, 0)

    g_q, gains_q = call(
        grad_query_kernel,
        (shape((tok_rows, q_cols), bf16), shape((8, span), f32)),
        raw_there, dq, gain_q, cos_there, sin_there,
        name="grad_query",
    )
    blocks = around(g_q)
    g_q_back = swap(g_q)
    g_kv = call(
        grad_key_value_kernel,
        shape((tok_rows + 16, kv_cols), bf16),
        raw_there, dkv, gain_k, cos_there, sin_there, gains_q,
        name="grad_key_value",
        after=tuple(blocks),
    )
    blocks_kv = around(g_kv)
    g_kv_back = swap(g_kv)
    parts = call(
        weight_grad_kernel,
        shape((planes, own_rows + 8, q_cols + kv_cols), bf16),
        where, turned, *blocks, *blocks_kv,
        name="weight_grad",
        after=(g_q_back, g_kv_back),
    )
    parts = lax.all_to_all(parts, plane, 0, 0)
    own_query, own_key, own_value, gain_sum_q, gain_sum_k = call(
        finish_kernel,
        (shape((own_rows, q_cols), f32),)
        + (shape((own_rows, span), f32),) * 2
        + (shape((1, span), f32),) * 2,
        parts,
        name="finish",
    )
    grad_states = call(
        grad_states_kernel,
        shape((tok_rows, width), bf16),
        where, g_q_back, g_kv_back, q_mine, q_theirs, kv_mine, kv_theirs,
        name="grad_states",
    )
    return (
        swap(ctx)[None],
        grad_states[None],
        own_query,
        own_key,
        own_value,
        gain_sum_q[0],
        gain_sum_k[0],
    )


def solution(mesh):
    fine = Mesh(mesh.devices.reshape(4, 4, 2, 2, 2), ("x", "z", "y_hi", "y_lo", "core"))
    ctx, dp = ("x", "z", "y_hi"), ("y_lo", "core")
    rows = P(ctx + dp, None)
    tokens = P(dp, ctx, None)
    in_specs = (tokens, P(), rows, rows, rows, P(), P(), tokens)
    out_specs = (tokens, tokens, rows, rows, rows, P(), P())
    return jax.shard_map(local, mesh=fine, in_specs=in_specs, out_specs=out_specs, check_vma=False)
```

```python
import math

import jax
import jax.numpy as jnp
from jax import lax
from jax.experimental import pallas as pl
from jax.experimental.pallas import tpu as pltpu
from jax.sharding import Mesh
from jax.sharding import PartitionSpec as P

bf16, f32 = jnp.bfloat16, jnp.float32
theta = 1000000.0
floor_score = -1e30
span = 128
chunk = 512
per_chunk = chunk // span
mib = 2**20
smem = pl.BlockSpec(memory_space=pltpu.SMEM)
vmem = pl.BlockSpec(memory_space=pltpu.VMEM)
anywhere = pl.BlockSpec(memory_space=pl.ANY)


def mm(a, b):
    return jnp.dot(a, b, preferred_element_type=f32)


def rotation(positions, head_width):
    steps_half = jnp.arange(head_width // 2, dtype=f32)
    inverse = jnp.power(f32(theta), -2.0 * steps_half / head_width)
    angles = positions.astype(f32)[:, None] * inverse[None, :]
    cosine = jnp.cos(angles)
    sine = jnp.sin(angles)
    return jnp.concatenate([cosine, cosine], 1), jnp.concatenate([-sine, sine], 1)


def inverse_norm(raw):
    return lax.rsqrt(jnp.mean(raw * raw, axis=-1, keepdims=True) + 1e-06)


def shape_head(raw, gain, cosine, sine):
    normed = raw * inverse_norm(raw) * gain
    return normed * cosine + pltpu.roll(normed, span // 2, 1) * sine


def shape_head_grad(raw, gain, cosine, sine, grad):
    inverse = inverse_norm(raw)
    grad_normed = grad * cosine + pltpu.roll(grad * sine, span // 2, 1)
    grad_unit = grad_normed * gain
    unit = raw * inverse
    shrink = jnp.mean(grad_unit * unit, axis=-1, keepdims=True)
    return inverse * (grad_unit - unit * shrink), grad_normed * unit


def prepare_kernel(where, src_ref, toks_ref, toks_theirs_ref, turned_ref, turned_theirs_ref, done_ref):
    planes, columns = src_ref.shape[:2]
    core = where[1]
    done_ref[...] = jnp.zeros_like(done_ref)

    def piece(plane, y, side):
        return src_ref[plane, y, side].astype(f32)

    group = 4
    for side, out_ref in ((core, toks_ref), (1 - core, toks_theirs_ref)):
        for i in range(0, planes, group):
            rows = jnp.concatenate(
                [piece(i + j, y, side) for j in range(group) for y in range(columns)], axis=0
            ).astype(bf16)
            wide = rows.shape[0]
            out_ref[:, i // group * wide : (i // group + 1) * wide] = rows.T
    for y in range(columns):
        for side, out_ref in ((core, turned_ref), (1 - core, turned_theirs_ref)):
            out_ref[y] = jnp.concatenate([piece(i, y, side) for i in range(planes)], axis=0).astype(bf16)


def pack_kernel(where, mine_ref, other_ref, *outs):
    core = where[1]
    outs, done_ref = outs[:-1], outs[-1]
    done_ref[...] = jnp.zeros_like(done_ref)
    for k, out_ref in enumerate(outs):
        at = lax.rem(where[0] + k, len(outs))
        out_ref[core] = mine_ref[at]
        out_ref[1 - core] = other_ref[at]


def place_kernel(where, *refs):
    blocks, out_ref = refs[:-1], refs[-1]
    for k, block in enumerate(blocks):
        out_ref[lax.rem(where[0] + k, len(blocks))] = block[...]


def key_value_kernel(mine_ref, other_ref, w_ref, w_other_ref, gain_ref, cos_ref, sin_ref, kv_ref, raw_ref):
    raw = mm(mine_ref[...], w_ref[...]) + mm(other_ref[...], w_other_ref[...])
    raw_ref[...] = raw[:, :span]
    kv_ref[:, :span] = shape_head(raw[:, :span], gain_ref[...], cos_ref[...], sin_ref[...]).astype(bf16)
    kv_ref[:, span:] = raw[:, span:].astype(bf16)


def query_kernel(mine_ref, other_ref, w_ref, w_other_ref, raw_k_ref, gain_ref, cos_ref, sin_ref, q_ref, raw_ref):
    rows = mm(mine_ref[...], w_ref[...]) + mm(other_ref[...], w_other_ref[...])
    raw_ref[:, -span:] = raw_k_ref[...].astype(bf16)
    gain = gain_ref[...] * (span**-0.5 / math.log(2.0))
    for h in range(q_ref.shape[1] // span):
        part = slice(h * span, (h + 1) * span)
        raw_ref[:, part] = rows[:, part].astype(bf16)
        q_ref[:, part] = shape_head(rows[:, part], gain, cos_ref[...], sin_ref[...]).astype(bf16)


def attention_kernel(
    order, own, q_ref, g_ref, kv_ref, kv_other_ref, ctx_ref, dq_ref, dkv_ref, dkv_other_ref,
    slot_of, ks, vs, kt, vt, acc_kv, qs, gs, qt, gt, acc_o, row_max, row_sum, row_delta, acc_q,
    sums, sums_other, sems,
):
    spans, heads = order.shape[0], q_ref.shape[1] // span
    chunks = spans // per_chunk
    rows = heads * span
    core = own[2]

    def place(slot, carry):
        slot_of[order[slot]] = slot
        return carry

    lax.fori_loop(0, spans, place, 0)

    def arrange(c, carry):
        for j in range(per_chunk):
            slot = slot_of[c * per_chunk + j]
            pair, rows_at = slot // 4, pl.multiple_of(slot % 2 * span, span)
            mine = (slot // 2) % 2 == core
            both = jnp.where(
                mine, kv_ref[pair, pl.ds(rows_at, span), :], kv_other_ref[pair, pl.ds(rows_at, span), :]
            )
            part = slice(j * span, (j + 1) * span)
            ks[c, part, :] = both[:, :span]
            vs[c, part, :] = both[:, span:]
            kt[c, :, part] = both[:, :span].T
            vt[c, :, part] = both[:, span:].T
        acc_kv[c] = jnp.zeros_like(acc_kv[c])
        return carry

    lax.fori_loop(0, chunks, arrange, 0)

    first_upper = own[0] > own[1]
    for upper in (True, False):
        which = jnp.where(first_upper, 0, 1) if upper else jnp.where(first_upper, 1, 0)
        block = own[which]
        row0 = pl.multiple_of(which * span, span)
        last = block // per_chunk
        for h in range(heads):
            part = slice(h * span, (h + 1) * span)
            qh = q_ref[pl.ds(row0, span), part]
            gh = g_ref[pl.ds(row0, span), part]
            qs[part, :] = qh
            gs[part, :] = gh
            qt[:, part] = qh.T
            gt[:, part] = gh.T

        def allowed(c):
            key_pos = c * chunk + lax.broadcasted_iota(jnp.int32, (chunk, rows), 0)
            row = lax.broadcasted_iota(jnp.int32, (chunk, rows), 1)
            return key_pos <= block * span + jnp.bitwise_and(row, span - 1)

        row_max[...] = jnp.full_like(row_max, floor_score)
        row_sum[...] = jnp.zeros_like(row_sum)
        acc_o[...] = jnp.zeros_like(acc_o)

        def forward(c, masked):
            s = mm(ks[c], qt[...])
            if masked:
                s = jnp.where(allowed(c), s, floor_score)
            old = row_max[...]
            new = jnp.maximum(old, jnp.max(s, axis=0, keepdims=True))
            p = jnp.exp2(s - new)
            alpha = jnp.exp2(old - new)
            row_max[...] = new
            row_sum[...] = row_sum[...] * alpha + jnp.sum(p, axis=0, keepdims=True)
            acc_o[...] = acc_o[...] * alpha + mm(vt[c], p.astype(bf16))

        def forward_step(c, carry):
            forward(c, False)
            return carry

        lax.fori_loop(0, last, forward_step, 0)
        forward(last, True)

        total = row_sum[...]
        ctx_t = (acc_o[...] / total).astype(bf16)
        row_max[...] = row_max[...] + jnp.log2(total)
        row_delta[...] = jnp.sum(ctx_t.astype(f32) * gt[...].astype(f32), axis=0, keepdims=True)
        for h in range(heads):
            part = slice(h * span, (h + 1) * span)
            ctx_ref[pl.ds(row0, span), part] = ctx_t[:, part].T
        acc_q[...] = jnp.zeros_like(acc_q)

        def backward(c, masked):
            s = mm(ks[c], qt[...])
            p = jnp.exp2(s - row_max[...])
            if masked:
                p = jnp.where(allowed(c), p, 0.0)
            dp = mm(vs[c], gt[...])
            ds = (p * (dp - row_delta[...])).astype(bf16)
            acc_kv[c, :, span:] += mm(p.astype(bf16), gs[...])
            acc_kv[c, :, :span] += mm(ds, qs[...])
            acc_q[...] += mm(kt[c], ds)

        def backward_step(c, carry):
            backward(c, False)
            return carry

        lax.fori_loop(0, last, backward_step, 0)
        backward(last, True)
        for h in range(heads):
            part = slice(h * span, (h + 1) * span)
            dq_ref[pl.ds(row0, span), part] = acc_q[:, part].T * (span**-0.5)

    def give(c, carry):
        for j in range(per_chunk):
            part = slice(j * span, (j + 1) * span)
            slot = slot_of[c * per_chunk + j]
            pair, rows_at = slot // 4, pl.multiple_of(slot % 2 * span, span)
            mine = (slot // 2) % 2 == core
            dk = (acc_kv[c, part, :span] * math.log(2.0)).astype(bf16)
            dv = acc_kv[c, part, span:].astype(bf16)

            @pl.when(mine)
            def _():
                sums[pair, pl.ds(rows_at, span), :span] = dk
                sums[pair, pl.ds(rows_at, span), span:] = dv

            @pl.when(jnp.logical_not(mine))
            def _():
                sums_other[pair, pl.ds(rows_at, span), :span] = dk
                sums_other[pair, pl.ds(rows_at, span), span:] = dv

        return carry

    lax.fori_loop(0, chunks, give, 0)
    copies = [
        pltpu.make_async_copy(sums_other, dkv_other_ref, sems.at[0]),
        pltpu.make_async_copy(sums, dkv_ref, sems.at[1]),
    ]
    for copy in copies:
        copy.start()
    for copy in copies:
        copy.wait()


def attention(order, own, q16, g16, kv, kv_other):
    rows_here, cols = q16.shape
    spans = order.shape[0]
    chunks = spans // per_chunk
    rows = cols
    share = jax.ShapeDtypeStruct(kv.shape, bf16)
    return pl.pallas_call(
        attention_kernel,
        out_shape=(
            jax.ShapeDtypeStruct((rows_here, cols), bf16),
            jax.ShapeDtypeStruct((rows_here, cols), f32),
            share,
            share,
        ),
        in_specs=[smem, smem] + [vmem] * 4,
        out_specs=(vmem, vmem, anywhere, anywhere),
        scratch_shapes=[
            pltpu.SMEM((spans,), jnp.int32),
            pltpu.VMEM((chunks, chunk, span), bf16),
            pltpu.VMEM((chunks, chunk, span), bf16),
            pltpu.VMEM((chunks, span, chunk), bf16),
            pltpu.VMEM((chunks, span, chunk), bf16),
            pltpu.VMEM((chunks, chunk, 2 * span), f32),
            pltpu.VMEM((rows, span), bf16),
            pltpu.VMEM((rows, span), bf16),
            pltpu.VMEM((span, rows), bf16),
            pltpu.VMEM((span, rows), bf16),
            pltpu.VMEM((span, rows), f32),
            pltpu.VMEM((1, rows), f32),
            pltpu.VMEM((1, rows), f32),
            pltpu.VMEM((1, rows), f32),
            pltpu.VMEM((span, rows), f32),
            pltpu.VMEM(kv.shape, bf16),
            pltpu.VMEM(kv.shape, bf16),
            pltpu.SemaphoreType.DMA((2,)),
        ],
        compiler_params=pltpu.CompilerParams(vmem_limit_bytes=32 * mib),
        cost_estimate=pl.CostEstimate(
            flops=1000, bytes_accessed=1000, transcendentals=0
        ),
        name="attention",
    )(order, own, q16, g16, kv, kv_other)


def grad_query_kernel(raw_ref, dq_ref, gain_ref, cos_ref, sin_ref, g_ref, gain_out):
    cosine, sine = cos_ref[...], sin_ref[...]
    sums = jnp.zeros((1, span), f32)
    for h in range(dq_ref.shape[1] // span):
        part = slice(h * span, (h + 1) * span)
        grad, terms = shape_head_grad(
            raw_ref[:, part].astype(f32), gain_ref[...], cosine, sine, dq_ref[:, part]
        )
        g_ref[:, part] = grad.astype(bf16)
        sums = sums + jnp.sum(terms, axis=0, keepdims=True)
    gain_out[...] = jnp.broadcast_to(sums, gain_out.shape)


def grad_key_value_kernel(raw_ref, dkv_ref, gain_ref, cos_ref, sin_ref, gain_q_ref, g_ref):
    rows = raw_ref.shape[0]
    dkv = jnp.sum(dkv_ref[...].astype(f32), axis=0)
    grad, terms = shape_head_grad(
        raw_ref[:, -span:].astype(f32), gain_ref[...], cos_ref[...], sin_ref[...], dkv[:, :span]
    )
    g_ref[:rows, :span] = grad.astype(bf16)
    g_ref[:rows, span:] = dkv[:, span:].astype(bf16)
    gain_k = jnp.sum(terms, axis=0, keepdims=True)
    split = []
    for gain in (gain_q_ref[0:1], gain_k):
        high = gain.astype(bf16).astype(f32)
        split.append(jnp.concatenate([high, gain - high], axis=1))
    row = lax.broadcasted_iota(jnp.int32, (g_ref.shape[0] - rows, 2 * span), 0)
    g_ref[rows:] = jnp.where(row == 0, split[0], jnp.where(row == 1, split[1], 0.0)).astype(bf16)


def weight_grad_kernel(where, turned_ref, *rest):
    blocks, out_ref = rest[:-1], rest[-1]
    count = len(blocks) // 2
    columns = count // 2
    toks = turned_ref.shape[2]
    y, core = where[0], where[1]
    query, rows, gains = 0.0, 0.0, 0.0
    for i in range(count):
        from_y = lax.rem(y + i % columns, columns)
        from_core = core if i < columns else 1 - core
        at = (from_core * 2 + lax.rem(from_y, 2)) * 2 + from_y // 2
        query = query + mm(turned_ref[at], blocks[i][...])
        rows = rows + mm(turned_ref[at], blocks[count + i][:toks])
        gains = gains + blocks[count + i][toks:].astype(f32)
    gain = gains[:8, :span] + gains[:8, span:]
    high = gain.astype(bf16).astype(f32)
    extra = jnp.concatenate([jnp.zeros((8, query.shape[1]), f32), high, gain - high], axis=1)
    total = jnp.concatenate([query, rows], axis=1)
    own_rows = total.shape[0] // out_ref.shape[0]
    for i in range(out_ref.shape[0]):
        part = total[i * own_rows : (i + 1) * own_rows]
        out_ref[i] = jnp.concatenate([part, extra], axis=0).astype(bf16)


def grad_states_kernel(where, gq_ref, gkv_ref, q_ref, q_theirs_ref, kv_ref, kv_theirs_ref, out_ref):
    core = where[1]
    own_rows, group = 40, 640
    transposed = (((1,), (1,)), ((), ()))

    def product(q, kv, i):
        part = slice(i * group, (i + 1) * group)
        return lax.dot_general(
            q[part], gq_ref[...], transposed, preferred_element_type=f32
        ) + lax.dot_general(kv[part], gkv_ref[: gq_ref.shape[0]], transposed, preferred_element_type=f32)

    for i in range(q_ref.shape[0] // group):
        mine, theirs = product(q_ref, kv_ref, i), product(q_theirs_ref, kv_theirs_ref, i)
        sides = (jnp.where(core == 0, mine, theirs), jnp.where(core == 0, theirs, mine))
        rows = jnp.concatenate(
            [side[j : j + own_rows] for j in range(0, group, own_rows) for side in sides], axis=0
        )
        out_ref[:, 2 * i * group : 2 * (i + 1) * group] = rows.astype(bf16).T


def finish_kernel(parts_ref, query_ref, key_ref, value_ref, gain_q_ref, gain_k_ref):
    sums = jnp.sum(parts_ref[...].astype(f32), axis=0)
    rows, cols = query_ref.shape
    query_ref[...] = sums[:rows, :cols]
    key_ref[...] = sums[:rows, cols : cols + span]
    value_ref[...] = sums[:rows, cols + span :]
    gains = sums[rows:, cols : cols + span] + sums[rows:, cols + span :]
    gain_q_ref[...] = gains[0:1]
    gain_k_ref[...] = gains[1:2]


cheap = pl.CostEstimate(flops=1000, bytes_accessed=1000, transcendentals=0)


def call(kernel, shapes, *args, name, after=(), limit=16, scratch=()):
    count = len(args)

    def run(*refs):
        kernel(*refs[:count], *refs[count + len(after) :])

    return pl.pallas_call(
        run,
        out_shape=shapes,
        in_specs=[smem if a.dtype == jnp.int32 else vmem for a in args] + [vmem] * len(after),
        out_specs=jax.tree.map(lambda _: vmem, shapes),
        scratch_shapes=scratch,
        compiler_params=pltpu.CompilerParams(vmem_limit_bytes=limit * mib),
        cost_estimate=cheap,
        name=name,
    )(*args, *after)


plane = ("x", "z")
column = ("y_hi", "y_lo")
chips = plane + column
swapped = [(0, 0), (1, 2), (2, 1), (3, 3)]
flipped = [(0, 1), (1, 0)]


def swap(array):
    return lax.ppermute(array, ("y_hi", "core"), swapped)


def flip(array):
    return lax.ppermute(array, "core", flipped)


def to_all(array, axes, count):
    return lax.all_to_all(jnp.broadcast_to(array[None], (count,) + array.shape), axes, 0, 0)


def ring(array, step):
    return lax.ppermute(array, column, [(i, (i - step) % 4) for i in range(4)])


def around(array):
    mine = [array] + [ring(array, k) for k in range(1, 4)]
    return mine + [flip(a) for a in mine]


def local(hidden_states, block_order, w_query, w_key, w_value, gain_query, gain_key, cotangent):
    tokens = hidden_states[0]
    tok_rows, width = tokens.shape
    q_cols = w_query.shape[1]
    kv_cols = 2 * span
    own_rows = w_query.shape[0]
    planes, columns = 16, 4
    half = width // 2
    place = lax.axis_index("x") * 4 + lax.axis_index("z")
    y_hi, core = lax.axis_index("y_hi"), lax.axis_index("core")
    y = y_hi * 2 + lax.axis_index("y_lo")
    where = jnp.stack([y, core]).astype(jnp.int32)
    offsets = jnp.arange(span, dtype=jnp.int32)

    def angles_of(part):
        blocks = lax.dynamic_slice_in_dim(block_order, 2 * (place * 2 + part), 2)
        positions = (blocks[:, None] * span + offsets[None, :]).reshape(tok_rows)
        return blocks, rotation(positions, span)

    _, (cosine, sine) = angles_of(y_hi)
    own_blocks, (cos_there, sin_there) = angles_of(core)
    own = jnp.concatenate([own_blocks, core[None].astype(jnp.int32)])
    gain_q, gain_k = gain_query[None, :], gain_key[None, :]
    shape = jax.ShapeDtypeStruct

    kv_mine = to_all(jnp.concatenate([w_key, w_value], axis=1), chips, planes * columns)
    toks_mine, toks_theirs, turned, turned_theirs, done = call(
        prepare_kernel,
        (shape((tok_rows, half), bf16),) * 2
        + (shape((columns, half // columns, tok_rows), bf16),) * 2
        + (shape((8, span), f32),),
        where, tokens.T.reshape(planes, columns, 2, own_rows, tok_rows),
        name="prepare",
        after=(cosine, sine, cos_there, sin_there),
    )
    kv_mine, w_query, done, own = lax.optimization_barrier((kv_mine, w_query, done, own))
    kv_mine = kv_mine.reshape(half, kv_cols)
    kv_theirs = flip(kv_mine)
    q_mine = to_all(w_query, chips, planes * columns).reshape(half, q_cols)

    kv16, raw_k = call(
        key_value_kernel,
        (shape((tok_rows, kv_cols), bf16), shape((tok_rows, span), f32)),
        toks_mine, toks_theirs, kv_mine, kv_theirs, gain_k, cosine, sine,
        name="key_value",
        after=(done,),
    )
    kv_send = jnp.broadcast_to(swap(kv16)[None], (planes, tok_rows, kv_cols))
    *packed, packed_done = call(
        pack_kernel,
        (shape((2, half // columns, tok_rows), bf16),) * columns + (shape((8, span), f32),),
        where, turned, flip(turned_theirs),
        name="pack",
    )
    kv_send, q_mine = lax.optimization_barrier((kv_send, q_mine))
    kv_own = lax.all_to_all(kv_send, plane, 0, 0)
    q_theirs = flip(q_mine)
    grad_out = swap(cotangent[0])
    q16, raw = call(
        query_kernel,
        (shape((tok_rows, q_cols), bf16), shape((tok_rows, q_cols + span), bf16)),
        toks_mine, toks_theirs, q_mine, q_theirs, raw_k, gain_q, cosine, sine,
        name="query",
        after=(grad_out, packed_done),
    )
    q16, raw_there = swap(q16), swap(raw)
    kv_own, q16 = lax.optimization_barrier((kv_own, q16))
    kv_other = flip(kv_own)
    turned = [packed[0]] + [
        lax.ppermute(packed[k], column, [(i, (i + k) % columns) for i in range(columns)])
        for k in range(1, columns)
    ]

    ctx, dq, dkv_mine, dkv_theirs = attention(block_order, own, q16, grad_out, kv_own, kv_other)
    dkv_theirs, turned = lax.optimization_barrier((dkv_theirs, turned))
    turned = call(
        place_kernel,
        shape((columns, 2, half // columns, tok_rows), bf16),
        where, turned[0], turned[3], turned[2], turned[1],
        name="place",
    ).reshape(2 * columns, half // columns, tok_rows)
    dkv = (dkv_mine.astype(f32) + flip(dkv_theirs).astype(f32)).astype(bf16)
    dkv = lax.all_to_all(dkv, plane, 0, 0)

    g_q, gains_q = call(
        grad_query_kernel,
        (shape((tok_rows, q_cols), bf16), shape((8, span), f32)),
        raw_there, dq, gain_q, cos_there, sin_there,
        name="grad_query",
    )
    blocks = around(g_q)
    g_q_back = swap(g_q)
    g_kv = call(
        grad_key_value_kernel,
        shape((tok_rows + 16, kv_cols), bf16),
        raw_there, dkv, gain_k, cos_there, sin_there, gains_q,
        name="grad_key_value",
        after=tuple(blocks),
    )
    blocks_kv = around(g_kv)
    g_kv_back = swap(g_kv)
    parts = call(
        weight_grad_kernel,
        shape((planes, own_rows + 8, q_cols + kv_cols), bf16),
        where, turned, *blocks, *blocks_kv,
        name="weight_grad",
        after=(g_q_back, g_kv_back),
    )
    parts = lax.all_to_all(parts, plane, 0, 0)
    own_query, own_key, own_value, gain_sum_q, gain_sum_k = call(
        finish_kernel,
        (shape((own_rows, q_cols), f32),)
        + (shape((own_rows, span), f32),) * 2
        + (shape((1, span), f32),) * 2,
        parts,
        name="finish",
    )
    grad_states = call(
        grad_states_kernel,
        shape((tok_rows, width), bf16),
        where, g_q_back, g_kv_back, q_mine, q_theirs, kv_mine, kv_theirs,
        name="grad_states",
    )
    return (
        swap(ctx)[None],
        grad_states[None],
        own_query,
        own_key,
        own_value,
        gain_sum_q[0],
        gain_sum_k[0],
    )


def solution(mesh):
    fine = Mesh(mesh.devices.reshape(4, 4, 2, 2, 2), ("x", "z", "y_hi", "y_lo", "core"))
    ctx, dp = ("x", "z", "y_hi"), ("y_lo", "core")
    rows = P(ctx + dp, None)
    tokens = P(dp, ctx, None)
    in_specs = (tokens, P(), rows, rows, rows, P(), P(), tokens)
    out_specs = (tokens, tokens, rows, rows, rows, P(), P())
    return jax.shard_map(local, mesh=fine, in_specs=in_specs, out_specs=out_specs, check_vma=False)
```

```python
import math

import jax
import jax.numpy as jnp
from jax import lax
from jax.experimental import pallas as pl
from jax.experimental.pallas import tpu as pltpu
from jax.sharding import Mesh
from jax.sharding import PartitionSpec as P

bf16, f32 = jnp.bfloat16, jnp.float32
theta = 1000000.0
floor_score = -1e30
span = 128
chunk = 512
per_chunk = chunk // span
mib = 2**20
smem = pl.BlockSpec(memory_space=pltpu.SMEM)
vmem = pl.BlockSpec(memory_space=pltpu.VMEM)
anywhere = pl.BlockSpec(memory_space=pl.ANY)


def mm(a, b):
    return jnp.dot(a, b, preferred_element_type=f32)


def rotation(positions, head_width):
    steps_half = jnp.arange(head_width // 2, dtype=f32)
    inverse = jnp.power(f32(theta), -2.0 * steps_half / head_width)
    angles = positions.astype(f32)[:, None] * inverse[None, :]
    cosine = jnp.cos(angles)
    sine = jnp.sin(angles)
    return jnp.concatenate([cosine, cosine], 1), jnp.concatenate([-sine, sine], 1)


def inverse_norm(raw):
    return lax.rsqrt(jnp.mean(raw * raw, axis=-1, keepdims=True) + 1e-06)


def shape_head(raw, gain, cosine, sine):
    normed = raw * inverse_norm(raw) * gain
    return normed * cosine + pltpu.roll(normed, span // 2, 1) * sine


def shape_head_grad(raw, gain, cosine, sine, grad):
    inverse = inverse_norm(raw)
    grad_normed = grad * cosine + pltpu.roll(grad * sine, span // 2, 1)
    grad_unit = grad_normed * gain
    unit = raw * inverse
    shrink = jnp.mean(grad_unit * unit, axis=-1, keepdims=True)
    return inverse * (grad_unit - unit * shrink), grad_normed * unit


def prepare_kernel(where, src_ref, toks_ref, toks_theirs_ref, turned_ref, turned_theirs_ref, done_ref):
    planes, columns = src_ref.shape[:2]
    core = where[1]
    done_ref[...] = jnp.zeros_like(done_ref)

    def piece(plane, y, side):
        return src_ref[plane, y, side].astype(f32)

    group = 4
    for side, out_ref in ((core, toks_ref), (1 - core, toks_theirs_ref)):
        for i in range(0, planes, group):
            rows = jnp.concatenate(
                [piece(i + j, y, side) for j in range(group) for y in range(columns)], axis=0
            ).astype(bf16)
            wide = rows.shape[0]
            out_ref[:, i // group * wide : (i // group + 1) * wide] = rows.T
    for y in range(columns):
        for side, out_ref in ((core, turned_ref), (1 - core, turned_theirs_ref)):
            out_ref[y] = jnp.concatenate([piece(i, y, side) for i in range(planes)], axis=0).astype(bf16)


def pack_kernel(where, mine_ref, other_ref, *outs):
    core = where[1]
    outs, done_ref = outs[:-1], outs[-1]
    done_ref[...] = jnp.zeros_like(done_ref)
    for k, out_ref in enumerate(outs):
        at = lax.rem(where[0] + k, len(outs))
        out_ref[core] = mine_ref[at]
        out_ref[1 - core] = other_ref[at]


def place_kernel(where, dkv_ref, *refs):
    blocks, out_ref = refs[:-2], refs[-1]
    for k, block in enumerate(blocks):
        out_ref[lax.rem(where[0] + k, len(blocks))] = block[...]


def key_value_kernel(mine_ref, other_ref, w_ref, w_other_ref, gain_ref, cos_ref, sin_ref, kv_ref, raw_ref):
    raw = mm(mine_ref[...], w_ref[...]) + mm(other_ref[...], w_other_ref[...])
    raw_ref[...] = raw[:, :span]
    kv_ref[:, :span] = shape_head(raw[:, :span], gain_ref[...], cos_ref[...], sin_ref[...]).astype(bf16)
    kv_ref[:, span:] = raw[:, span:].astype(bf16)


def query_kernel(mine_ref, other_ref, w_ref, w_other_ref, raw_k_ref, gain_ref, cos_ref, sin_ref, q_ref, raw_ref):
    rows = mm(mine_ref[...], w_ref[...]) + mm(other_ref[...], w_other_ref[...])
    raw_ref[:, -span:] = raw_k_ref[...].astype(bf16)
    gain = gain_ref[...] * (span**-0.5 / math.log(2.0))
    for h in range(q_ref.shape[1] // span):
        part = slice(h * span, (h + 1) * span)
        raw_ref[:, part] = rows[:, part].astype(bf16)
        q_ref[:, part] = shape_head(rows[:, part], gain, cos_ref[...], sin_ref[...]).astype(bf16)


def attention_kernel(
    order, own, q_ref, g_ref, kv_ref, kv_other_ref, ctx_ref, dq_ref, dkv_ref, dkv_other_ref,
    slot_of, ks, vs, kt, vt, acc_kv, qs, gs, qt, gt, acc_o, row_max, row_sum, row_delta, acc_q,
    sums, sums_other, sems,
):
    spans, heads = order.shape[0], q_ref.shape[1] // span
    chunks = spans // per_chunk
    rows = heads * span
    core = own[2]

    def place(slot, carry):
        slot_of[order[slot]] = slot
        return carry

    lax.fori_loop(0, spans, place, 0)

    def arrange(c, carry):
        for j in range(per_chunk):
            slot = slot_of[c * per_chunk + j]
            pair, rows_at = slot // 4, pl.multiple_of(slot % 2 * span, span)
            mine = (slot // 2) % 2 == core
            both = jnp.where(
                mine, kv_ref[pair, pl.ds(rows_at, span), :], kv_other_ref[pair, pl.ds(rows_at, span), :]
            )
            part = slice(j * span, (j + 1) * span)
            ks[c, part, :] = both[:, :span]
            vs[c, part, :] = both[:, span:]
            kt[c, :, part] = both[:, :span].T
            vt[c, :, part] = both[:, span:].T
        acc_kv[c] = jnp.zeros_like(acc_kv[c])
        return carry

    lax.fori_loop(0, chunks, arrange, 0)

    first_upper = own[0] > own[1]
    for upper in (True, False):
        which = jnp.where(first_upper, 0, 1) if upper else jnp.where(first_upper, 1, 0)
        block = own[which]
        row0 = pl.multiple_of(which * span, span)
        last = block // per_chunk
        for h in range(heads):
            part = slice(h * span, (h + 1) * span)
            qh = q_ref[pl.ds(row0, span), part]
            gh = g_ref[pl.ds(row0, span), part]
            qs[part, :] = qh
            gs[part, :] = gh
            qt[:, part] = qh.T
            gt[:, part] = gh.T

        def allowed(c):
            key_pos = c * chunk + lax.broadcasted_iota(jnp.int32, (chunk, rows), 0)
            row = lax.broadcasted_iota(jnp.int32, (chunk, rows), 1)
            return key_pos <= block * span + jnp.bitwise_and(row, span - 1)

        row_max[...] = jnp.full_like(row_max, floor_score)
        row_sum[...] = jnp.zeros_like(row_sum)
        acc_o[...] = jnp.zeros_like(acc_o)

        def forward(c, masked):
            s = mm(ks[c], qt[...])
            if masked:
                s = jnp.where(allowed(c), s, floor_score)
            old = row_max[...]
            new = jnp.maximum(old, jnp.max(s, axis=0, keepdims=True))
            p = jnp.exp2(s - new)
            alpha = jnp.exp2(old - new)
            row_max[...] = new
            row_sum[...] = row_sum[...] * alpha + jnp.sum(p, axis=0, keepdims=True)
            acc_o[...] = acc_o[...] * alpha + mm(vt[c], p.astype(bf16))

        def forward_step(c, carry):
            forward(c, False)
            return carry

        lax.fori_loop(0, last, forward_step, 0)
        forward(last, True)

        total = row_sum[...]
        ctx_t = (acc_o[...] / total).astype(bf16)
        row_max[...] = row_max[...] + jnp.log2(total)
        row_delta[...] = jnp.sum(ctx_t.astype(f32) * gt[...].astype(f32), axis=0, keepdims=True)
        for h in range(heads):
            part = slice(h * span, (h + 1) * span)
            ctx_ref[pl.ds(row0, span), part] = ctx_t[:, part].T
        acc_q[...] = jnp.zeros_like(acc_q)

        def backward(c, masked):
            s = mm(ks[c], qt[...])
            p = jnp.exp2(s - row_max[...])
            if masked:
                p = jnp.where(allowed(c), p, 0.0)
            dp = mm(vs[c], gt[...])
            ds = (p * (dp - row_delta[...])).astype(bf16)
            acc_kv[c, :, span:] += mm(p.astype(bf16), gs[...])
            acc_kv[c, :, :span] += mm(ds, qs[...])
            acc_q[...] += mm(kt[c], ds)

        def backward_step(c, carry):
            backward(c, False)
            return carry

        lax.fori_loop(0, last, backward_step, 0)
        backward(last, True)
        for h in range(heads):
            part = slice(h * span, (h + 1) * span)
            dq_ref[pl.ds(row0, span), part] = acc_q[:, part].T * (span**-0.5)

    def give(c, carry):
        for j in range(per_chunk):
            part = slice(j * span, (j + 1) * span)
            slot = slot_of[c * per_chunk + j]
            pair, rows_at = slot // 4, pl.multiple_of(slot % 2 * span, span)
            mine = (slot // 2) % 2 == core
            dk = (acc_kv[c, part, :span] * math.log(2.0)).astype(bf16)
            dv = acc_kv[c, part, span:].astype(bf16)

            @pl.when(mine)
            def _():
                sums[pair, pl.ds(rows_at, span), :span] = dk
                sums[pair, pl.ds(rows_at, span), span:] = dv

            @pl.when(jnp.logical_not(mine))
            def _():
                sums_other[pair, pl.ds(rows_at, span), :span] = dk
                sums_other[pair, pl.ds(rows_at, span), span:] = dv

        return carry

    lax.fori_loop(0, chunks, give, 0)
    copies = [
        pltpu.make_async_copy(sums_other, dkv_other_ref, sems.at[0]),
        pltpu.make_async_copy(sums, dkv_ref, sems.at[1]),
    ]
    for copy in copies:
        copy.start()
    for copy in copies:
        copy.wait()


def attention(order, own, q16, g16, kv, kv_other):
    rows_here, cols = q16.shape
    spans = order.shape[0]
    chunks = spans // per_chunk
    rows = cols
    share = jax.ShapeDtypeStruct(kv.shape, bf16)
    return pl.pallas_call(
        attention_kernel,
        out_shape=(
            jax.ShapeDtypeStruct((rows_here, cols), bf16),
            jax.ShapeDtypeStruct((rows_here, cols), f32),
            share,
            share,
        ),
        in_specs=[smem, smem] + [vmem] * 4,
        out_specs=(vmem, vmem, anywhere, anywhere),
        scratch_shapes=[
            pltpu.SMEM((spans,), jnp.int32),
            pltpu.VMEM((chunks, chunk, span), bf16),
            pltpu.VMEM((chunks, chunk, span), bf16),
            pltpu.VMEM((chunks, span, chunk), bf16),
            pltpu.VMEM((chunks, span, chunk), bf16),
            pltpu.VMEM((chunks, chunk, 2 * span), f32),
            pltpu.VMEM((rows, span), bf16),
            pltpu.VMEM((rows, span), bf16),
            pltpu.VMEM((span, rows), bf16),
            pltpu.VMEM((span, rows), bf16),
            pltpu.VMEM((span, rows), f32),
            pltpu.VMEM((1, rows), f32),
            pltpu.VMEM((1, rows), f32),
            pltpu.VMEM((1, rows), f32),
            pltpu.VMEM((span, rows), f32),
            pltpu.VMEM(kv.shape, bf16),
            pltpu.VMEM(kv.shape, bf16),
            pltpu.SemaphoreType.DMA((2,)),
        ],
        compiler_params=pltpu.CompilerParams(vmem_limit_bytes=32 * mib),
        cost_estimate=pl.CostEstimate(
            flops=1000, bytes_accessed=1000, transcendentals=0
        ),
        name="attention",
    )(order, own, q16, g16, kv, kv_other)


def grad_query_kernel(raw_ref, dq_ref, gain_ref, cos_ref, sin_ref, g_ref, gain_out):
    cosine, sine = cos_ref[...], sin_ref[...]
    sums = jnp.zeros((1, span), f32)
    for h in range(dq_ref.shape[1] // span):
        part = slice(h * span, (h + 1) * span)
        grad, terms = shape_head_grad(
            raw_ref[:, part].astype(f32), gain_ref[...], cosine, sine, dq_ref[:, part]
        )
        g_ref[:, part] = grad.astype(bf16)
        sums = sums + jnp.sum(terms, axis=0, keepdims=True)
    gain_out[...] = jnp.broadcast_to(sums, gain_out.shape)


def grad_key_value_kernel(raw_ref, dkv_ref, gain_ref, cos_ref, sin_ref, gain_q_ref, g_ref):
    rows = raw_ref.shape[0]
    dkv = jnp.sum(dkv_ref[...].astype(f32), axis=0)
    grad, terms = shape_head_grad(
        raw_ref[:, -span:].astype(f32), gain_ref[...], cos_ref[...], sin_ref[...], dkv[:, :span]
    )
    g_ref[:rows, :span] = grad.astype(bf16)
    g_ref[:rows, span:] = dkv[:, span:].astype(bf16)
    gain_k = jnp.sum(terms, axis=0, keepdims=True)
    split = []
    for gain in (gain_q_ref[0:1], gain_k):
        high = gain.astype(bf16).astype(f32)
        split.append(jnp.concatenate([high, gain - high], axis=1))
    row = lax.broadcasted_iota(jnp.int32, (g_ref.shape[0] - rows, 2 * span), 0)
    g_ref[rows:] = jnp.where(row == 0, split[0], jnp.where(row == 1, split[1], 0.0)).astype(bf16)


def over_tokens(where, turned_ref, blocks):
    columns = len(blocks) // 2
    toks = turned_ref.shape[2]
    y, core = where[0], where[1]
    total = 0.0
    for i, block in enumerate(blocks):
        from_y = lax.rem(y + i % columns, columns)
        from_core = core if i < columns else 1 - core
        at = (from_core * 2 + lax.rem(from_y, 2)) * 2 + from_y // 2
        total = total + mm(turned_ref[at], block[:toks])
    return total


def query_weight_grad_kernel(where, turned_ref, *rest):
    blocks, (out_ref, done_ref) = rest[:-2], rest[-2:]
    out_ref[...] = over_tokens(where, turned_ref, blocks).astype(bf16)
    done_ref[...] = jnp.zeros_like(done_ref)


def weight_grad_kernel(where, turned_ref, query_ref, *rest):
    blocks, out_ref = rest[:-1], rest[-1]
    toks = turned_ref.shape[2]
    gains = sum(block[toks:].astype(f32) for block in blocks)
    gain = gains[:8, :span] + gains[:8, span:]
    high = gain.astype(bf16).astype(f32)
    extra = jnp.concatenate([jnp.zeros((8, query_ref.shape[1]), f32), high, gain - high], axis=1)
    total = jnp.concatenate(
        [query_ref[...].astype(f32), over_tokens(where, turned_ref, blocks)], axis=1
    )
    own_rows = total.shape[0] // out_ref.shape[0]
    for i in range(out_ref.shape[0]):
        part = total[i * own_rows : (i + 1) * own_rows]
        out_ref[i] = jnp.concatenate([part, extra], axis=0).astype(bf16)


def grad_states_kernel(where, gq_ref, gkv_ref, q_ref, q_theirs_ref, kv_ref, kv_theirs_ref, out_ref):
    core = where[1]
    own_rows, group = 40, 640
    transposed = (((1,), (1,)), ((), ()))

    def product(q, kv, i):
        part = slice(i * group, (i + 1) * group)
        return lax.dot_general(
            q[part], gq_ref[...], transposed, preferred_element_type=f32
        ) + lax.dot_general(kv[part], gkv_ref[: gq_ref.shape[0]], transposed, preferred_element_type=f32)

    for i in range(q_ref.shape[0] // group):
        mine, theirs = product(q_ref, kv_ref, i), product(q_theirs_ref, kv_theirs_ref, i)
        sides = (jnp.where(core == 0, mine, theirs), jnp.where(core == 0, theirs, mine))
        rows = jnp.concatenate(
            [side[j : j + own_rows] for j in range(0, group, own_rows) for side in sides], axis=0
        )
        out_ref[:, 2 * i * group : 2 * (i + 1) * group] = rows.astype(bf16).T


def finish_kernel(parts_ref, query_ref, key_ref, value_ref, gain_q_ref, gain_k_ref):
    sums = jnp.sum(parts_ref[...].astype(f32), axis=0)
    rows, cols = query_ref.shape
    query_ref[...] = sums[:rows, :cols]
    key_ref[...] = sums[:rows, cols : cols + span]
    value_ref[...] = sums[:rows, cols + span :]
    gains = sums[rows:, cols : cols + span] + sums[rows:, cols + span :]
    gain_q_ref[...] = gains[0:1]
    gain_k_ref[...] = gains[1:2]


cheap = pl.CostEstimate(flops=1000, bytes_accessed=1000, transcendentals=0)


def call(kernel, shapes, *args, name, after=(), limit=16, scratch=()):
    count = len(args)

    def run(*refs):
        kernel(*refs[:count], *refs[count + len(after) :])

    return pl.pallas_call(
        run,
        out_shape=shapes,
        in_specs=[smem if a.dtype == jnp.int32 else vmem for a in args] + [vmem] * len(after),
        out_specs=jax.tree.map(lambda _: vmem, shapes),
        scratch_shapes=scratch,
        compiler_params=pltpu.CompilerParams(vmem_limit_bytes=limit * mib),
        cost_estimate=cheap,
        name=name,
    )(*args, *after)


plane = ("x", "z")
column = ("y_hi", "y_lo")
chips = plane + column
swapped = [(0, 0), (1, 2), (2, 1), (3, 3)]
flipped = [(0, 1), (1, 0)]


def swap(array):
    return lax.ppermute(array, ("y_hi", "core"), swapped)


def flip(array):
    return lax.ppermute(array, "core", flipped)


def to_all(array, axes, count):
    return lax.all_to_all(jnp.broadcast_to(array[None], (count,) + array.shape), axes, 0, 0)


def ring(array, step):
    return lax.ppermute(array, column, [(i, (i - step) % 4) for i in range(4)])


def around(array):
    mine = [array] + [ring(array, k) for k in range(1, 4)]
    return mine + [flip(a) for a in mine]


def local(hidden_states, block_order, w_query, w_key, w_value, gain_query, gain_key, cotangent):
    tokens = hidden_states[0]
    tok_rows, width = tokens.shape
    q_cols = w_query.shape[1]
    kv_cols = 2 * span
    own_rows = w_query.shape[0]
    planes, columns = 16, 4
    half = width // 2
    place = lax.axis_index("x") * 4 + lax.axis_index("z")
    y_hi, core = lax.axis_index("y_hi"), lax.axis_index("core")
    y = y_hi * 2 + lax.axis_index("y_lo")
    where = jnp.stack([y, core]).astype(jnp.int32)
    offsets = jnp.arange(span, dtype=jnp.int32)

    def angles_of(part):
        blocks = lax.dynamic_slice_in_dim(block_order, 2 * (place * 2 + part), 2)
        positions = (blocks[:, None] * span + offsets[None, :]).reshape(tok_rows)
        return blocks, rotation(positions, span)

    _, (cosine, sine) = angles_of(y_hi)
    own_blocks, (cos_there, sin_there) = angles_of(core)
    own = jnp.concatenate([own_blocks, core[None].astype(jnp.int32)])
    gain_q, gain_k = gain_query[None, :], gain_key[None, :]
    shape = jax.ShapeDtypeStruct

    kv_mine = to_all(jnp.concatenate([w_key, w_value], axis=1), chips, planes * columns)
    toks_mine, toks_theirs, turned, turned_theirs, done = call(
        prepare_kernel,
        (shape((tok_rows, half), bf16),) * 2
        + (shape((columns, half // columns, tok_rows), bf16),) * 2
        + (shape((8, span), f32),),
        where, tokens.T.reshape(planes, columns, 2, own_rows, tok_rows),
        name="prepare",
        after=(cosine, sine, cos_there, sin_there),
    )
    kv_mine, w_query, done, own = lax.optimization_barrier((kv_mine, w_query, done, own))
    kv_mine = kv_mine.reshape(half, kv_cols)
    kv_theirs = flip(kv_mine)
    q_mine = to_all(w_query, chips, planes * columns).reshape(half, q_cols)

    kv16, raw_k = call(
        key_value_kernel,
        (shape((tok_rows, kv_cols), bf16), shape((tok_rows, span), f32)),
        toks_mine, toks_theirs, kv_mine, kv_theirs, gain_k, cosine, sine,
        name="key_value",
        after=(done,),
    )
    kv_send = jnp.broadcast_to(swap(kv16)[None], (planes, tok_rows, kv_cols))
    *packed, packed_done = call(
        pack_kernel,
        (shape((2, half // columns, tok_rows), bf16),) * columns + (shape((8, span), f32),),
        where, turned, flip(turned_theirs),
        name="pack",
    )
    kv_send, q_mine = lax.optimization_barrier((kv_send, q_mine))
    kv_own = lax.all_to_all(kv_send, plane, 0, 0)
    q_theirs = flip(q_mine)
    grad_out = swap(cotangent[0])
    q16, raw = call(
        query_kernel,
        (shape((tok_rows, q_cols), bf16), shape((tok_rows, q_cols + span), bf16)),
        toks_mine, toks_theirs, q_mine, q_theirs, raw_k, gain_q, cosine, sine,
        name="query",
        after=(grad_out, packed_done),
    )
    q16, raw_there = swap(q16), swap(raw)
    kv_own, q16 = lax.optimization_barrier((kv_own, q16))
    kv_other = flip(kv_own)
    turned = [packed[0]] + [
        lax.ppermute(packed[k], column, [(i, (i + k) % columns) for i in range(columns)])
        for k in range(1, columns)
    ]

    ctx, dq, dkv_mine, dkv_theirs = attention(block_order, own, q16, grad_out, kv_own, kv_other)
    dkv_theirs, turned = pl.pallas_call(
        place_kernel,
        out_shape=(
            shape(dkv_theirs.shape, bf16),
            shape((columns, 2, half // columns, tok_rows), bf16),
        ),
        in_specs=[smem, anywhere] + [vmem] * columns,
        out_specs=(anywhere, vmem),
        input_output_aliases={1: 0},
        compiler_params=pltpu.CompilerParams(vmem_limit_bytes=16 * mib),
        cost_estimate=cheap,
        name="place",
    )(where, dkv_theirs, turned[0], turned[3], turned[2], turned[1])
    turned = turned.reshape(2 * columns, half // columns, tok_rows)
    dkv = (dkv_mine.astype(f32) + flip(dkv_theirs).astype(f32)).astype(bf16)
    dkv = lax.all_to_all(dkv, plane, 0, 0)

    g_q, gains_q = call(
        grad_query_kernel,
        (shape((tok_rows, q_cols), bf16), shape((8, span), f32)),
        raw_there, dq, gain_q, cos_there, sin_there,
        name="grad_query",
    )
    query_parts, done = call(
        query_weight_grad_kernel,
        (shape((half // columns, q_cols), bf16), shape((8, span), f32)),
        where, turned, *around(g_q),
        name="query_weight_grad",
    )
    g_q_back = swap(g_q)
    g_kv = call(
        grad_key_value_kernel,
        shape((tok_rows + 16, kv_cols), bf16),
        raw_there, dkv, gain_k, cos_there, sin_there, gains_q,
        name="grad_key_value",
        after=(done,),
    )
    blocks_kv = around(g_kv)
    g_kv_back = swap(g_kv)
    parts = call(
        weight_grad_kernel,
        shape((planes, own_rows + 8, q_cols + kv_cols), bf16),
        where, turned, query_parts, *blocks_kv,
        name="weight_grad",
        after=(g_q_back, g_kv_back),
    )
    parts = lax.all_to_all(parts, plane, 0, 0)
    own_query, own_key, own_value, gain_sum_q, gain_sum_k = call(
        finish_kernel,
        (shape((own_rows, q_cols), f32),)
        + (shape((own_rows, span), f32),) * 2
        + (shape((1, span), f32),) * 2,
        parts,
        name="finish",
    )
    grad_states = call(
        grad_states_kernel,
        shape((tok_rows, width), bf16),
        where, g_q_back, g_kv_back, q_mine, q_theirs, kv_mine, kv_theirs,
        name="grad_states",
    )
    return (
        swap(ctx)[None],
        grad_states[None],
        own_query,
        own_key,
        own_value,
        gain_sum_q[0],
        gain_sum_k[0],
    )


def solution(mesh):
    fine = Mesh(mesh.devices.reshape(4, 4, 2, 2, 2), ("x", "z", "y_hi", "y_lo", "core"))
    ctx, dp = ("x", "z", "y_hi"), ("y_lo", "core")
    rows = P(ctx + dp, None)
    tokens = P(dp, ctx, None)
    in_specs = (tokens, P(), rows, rows, rows, P(), P(), tokens)
    out_specs = (tokens, tokens, rows, rows, rows, P(), P())
    return jax.shard_map(local, mesh=fine, in_specs=in_specs, out_specs=out_specs, check_vma=False)
```

```python
import math

import jax
import jax.numpy as jnp
from jax import lax
from jax.experimental import pallas as pl
from jax.experimental.pallas import tpu as pltpu
from jax.sharding import Mesh
from jax.sharding import PartitionSpec as P

bf16, f32 = jnp.bfloat16, jnp.float32
theta = 1000000.0
floor_score = -1e30
span = 128
chunk = 512
per_chunk = chunk // span
mib = 2**20
smem = pl.BlockSpec(memory_space=pltpu.SMEM)
vmem = pl.BlockSpec(memory_space=pltpu.VMEM)
anywhere = pl.BlockSpec(memory_space=pl.ANY)


def mm(a, b):
    return jnp.dot(a, b, preferred_element_type=f32)


def rotation(positions, head_width):
    steps_half = jnp.arange(head_width // 2, dtype=f32)
    inverse = jnp.power(f32(theta), -2.0 * steps_half / head_width)
    angles = positions.astype(f32)[:, None] * inverse[None, :]
    cosine = jnp.cos(angles)
    sine = jnp.sin(angles)
    return jnp.concatenate([cosine, cosine], 1), jnp.concatenate([-sine, sine], 1)


def inverse_norm(raw):
    return lax.rsqrt(jnp.mean(raw * raw, axis=-1, keepdims=True) + 1e-06)


def shape_head(raw, gain, cosine, sine):
    normed = raw * inverse_norm(raw) * gain
    return normed * cosine + pltpu.roll(normed, span // 2, 1) * sine


def shape_head_grad(raw, gain, cosine, sine, grad):
    inverse = inverse_norm(raw)
    grad_normed = grad * cosine + pltpu.roll(grad * sine, span // 2, 1)
    grad_unit = grad_normed * gain
    unit = raw * inverse
    shrink = jnp.mean(grad_unit * unit, axis=-1, keepdims=True)
    return inverse * (grad_unit - unit * shrink), grad_normed * unit


def prepare_kernel(where, src_ref, toks_ref, toks_theirs_ref, turned_ref, turned_theirs_ref, done_ref):
    planes, columns = src_ref.shape[:2]
    core = where[1]
    done_ref[...] = jnp.zeros_like(done_ref)

    def piece(plane, y, side):
        return src_ref[plane, y, side].astype(f32)

    group = 4
    for side, out_ref in ((core, toks_ref), (1 - core, toks_theirs_ref)):
        for i in range(0, planes, group):
            rows = jnp.concatenate(
                [piece(i + j, y, side) for j in range(group) for y in range(columns)], axis=0
            ).astype(bf16)
            wide = rows.shape[0]
            out_ref[:, i // group * wide : (i // group + 1) * wide] = rows.T
    for y in range(columns):
        for side, out_ref in ((core, turned_ref), (1 - core, turned_theirs_ref)):
            out_ref[y] = jnp.concatenate([piece(i, y, side) for i in range(planes)], axis=0).astype(bf16)


def pack_kernel(where, mine_ref, other_ref, *outs):
    core = where[1]
    outs, done_ref = outs[:-1], outs[-1]
    done_ref[...] = jnp.zeros_like(done_ref)
    for k, out_ref in enumerate(outs):
        at = lax.rem(where[0] + k, len(outs))
        out_ref[core] = mine_ref[at]
        out_ref[1 - core] = other_ref[at]


def place_kernel(where, dkv_ref, raw_ref, *refs):
    blocks, out_ref = refs[:-2], refs[-1]
    for k, block in enumerate(blocks):
        out_ref[lax.rem(where[0] + k, len(blocks))] = block[...]


def key_value_kernel(mine_ref, other_ref, w_ref, w_other_ref, gain_ref, cos_ref, sin_ref, kv_ref, raw_ref):
    raw = mm(mine_ref[...], w_ref[...]) + mm(other_ref[...], w_other_ref[...])
    raw_ref[...] = raw[:, :span]
    kv_ref[:, :span] = shape_head(raw[:, :span], gain_ref[...], cos_ref[...], sin_ref[...]).astype(bf16)
    kv_ref[:, span:] = raw[:, span:].astype(bf16)


def query_kernel(mine_ref, other_ref, w_ref, w_other_ref, raw_k_ref, gain_ref, cos_ref, sin_ref, q_ref, raw_ref):
    rows = mm(mine_ref[...], w_ref[...]) + mm(other_ref[...], w_other_ref[...])
    raw_ref[:, -span:] = raw_k_ref[...].astype(bf16)
    gain = gain_ref[...] * (span**-0.5 / math.log(2.0))
    for h in range(q_ref.shape[1] // span):
        part = slice(h * span, (h + 1) * span)
        raw_ref[:, part] = rows[:, part].astype(bf16)
        q_ref[:, part] = shape_head(rows[:, part], gain, cos_ref[...], sin_ref[...]).astype(bf16)


def attention_kernel(
    order, own, q_ref, g_ref, kv_ref, kv_other_ref, ctx_ref, dq_ref, dkv_ref, dkv_other_ref,
    slot_of, ks, vs, kt, vt, acc_kv, qs, gs, qt, gt, acc_o, row_max, row_sum, row_delta, acc_q,
    sums, sems,
):
    spans, heads = order.shape[0], q_ref.shape[1] // span
    chunks = spans // per_chunk
    rows = heads * span
    core = own[2]

    def place(slot, carry):
        slot_of[order[slot]] = slot
        return carry

    lax.fori_loop(0, spans, place, 0)

    def arrange(c, carry):
        for j in range(per_chunk):
            slot = slot_of[c * per_chunk + j]
            pair, rows_at = slot // 4, pl.multiple_of(slot % 2 * span, span)
            mine = (slot // 2) % 2 == core
            both = jnp.where(
                mine, kv_ref[pair, pl.ds(rows_at, span), :], kv_other_ref[pair, pl.ds(rows_at, span), :]
            )
            part = slice(j * span, (j + 1) * span)
            ks[c, part, :] = both[:, :span]
            vs[c, part, :] = both[:, span:]
            kt[c, :, part] = both[:, :span].T
            vt[c, :, part] = both[:, span:].T
        return carry

    lax.fori_loop(0, chunks, arrange, 0)

    def clear(c, carry):
        acc_kv[c] = jnp.zeros_like(acc_kv[c])
        return carry

    first_upper = own[0] > own[1]
    for upper in (True, False):
        which = jnp.where(first_upper, 0, 1) if upper else jnp.where(first_upper, 1, 0)
        block = own[which]
        row0 = pl.multiple_of(which * span, span)
        last = block // per_chunk
        for h in range(heads):
            part = slice(h * span, (h + 1) * span)
            qh = q_ref[pl.ds(row0, span), part]
            gh = g_ref[pl.ds(row0, span), part]
            qs[part, :] = qh
            gs[part, :] = gh
            qt[:, part] = qh.T
            gt[:, part] = gh.T

        def allowed(c):
            key_pos = c * chunk + lax.broadcasted_iota(jnp.int32, (chunk, rows), 0)
            row = lax.broadcasted_iota(jnp.int32, (chunk, rows), 1)
            return key_pos <= block * span + jnp.bitwise_and(row, span - 1)

        row_max[...] = jnp.full_like(row_max, floor_score)
        row_sum[...] = jnp.zeros_like(row_sum)
        acc_o[...] = jnp.zeros_like(acc_o)

        def forward(c, masked):
            s = mm(ks[c], qt[...])
            if masked:
                s = jnp.where(allowed(c), s, floor_score)
            old = row_max[...]
            new = jnp.maximum(old, jnp.max(s, axis=0, keepdims=True))
            p = jnp.exp2(s - new)
            alpha = jnp.exp2(old - new)
            row_max[...] = new
            row_sum[...] = row_sum[...] * alpha + jnp.sum(p, axis=0, keepdims=True)
            acc_o[...] = acc_o[...] * alpha + mm(vt[c], p.astype(bf16))

        def forward_step(c, carry):
            forward(c, False)
            return carry

        def forward_pair(i, carry):
            c = 2 * i
            s = [mm(ks[c + j], qt[...]) for j in range(2)]
            old = row_max[...]
            new = jnp.maximum(old, jnp.max(jnp.maximum(s[0], s[1]), axis=0, keepdims=True))
            p = [jnp.exp2(part - new) for part in s]
            alpha = jnp.exp2(old - new)
            row_max[...] = new
            row_sum[...] = row_sum[...] * alpha + jnp.sum(p[0] + p[1], axis=0, keepdims=True)
            acc_o[...] = (
                acc_o[...] * alpha + mm(vt[c], p[0].astype(bf16)) + mm(vt[c + 1], p[1].astype(bf16))
            )
            return carry

        lax.fori_loop(0, last // 2, forward_pair, 0)
        lax.fori_loop(last // 2 * 2, last, forward_step, 0)
        forward(last, True)

        total = row_sum[...]
        ctx_t = (acc_o[...] / total).astype(bf16)
        row_max[...] = row_max[...] + jnp.log2(total)
        row_delta[...] = jnp.sum(ctx_t.astype(f32) * gt[...].astype(f32), axis=0, keepdims=True)
        for h in range(heads):
            part = slice(h * span, (h + 1) * span)
            ctx_ref[pl.ds(row0, span), part] = ctx_t[:, part].T
        acc_q[...] = jnp.zeros_like(acc_q)

        def backward(c, masked):
            s = mm(ks[c], qt[...])
            p = jnp.exp2(s - row_max[...])
            if masked:
                p = jnp.where(allowed(c), p, 0.0)
            dp = mm(vs[c], gt[...])
            ds = (p * (dp - row_delta[...])).astype(bf16)
            dv, dk = mm(p.astype(bf16), gs[...]), mm(ds, qs[...])
            if upper:
                acc_kv[c, :, span:] = dv
                acc_kv[c, :, :span] = dk
            else:
                acc_kv[c, :, span:] += dv
                acc_kv[c, :, :span] += dk
            acc_q[...] += mm(kt[c], ds)

        def backward_step(c, carry):
            backward(c, False)
            return carry

        def backward_pair(i, carry):
            c = 2 * i
            s = [mm(ks[c + j], qt[...]) for j in range(2)]
            p = [jnp.exp2(part - row_max[...]) for part in s]
            dp = [mm(vs[c + j], gt[...]) for j in range(2)]
            ds = [(p[j] * (dp[j] - row_delta[...])).astype(bf16) for j in range(2)]
            for j in range(2):
                dv, dk = mm(p[j].astype(bf16), gs[...]), mm(ds[j], qs[...])
                if upper:
                    acc_kv[c + j, :, span:] = dv
                    acc_kv[c + j, :, :span] = dk
                else:
                    acc_kv[c + j, :, span:] += dv
                    acc_kv[c + j, :, :span] += dk
            acc_q[...] += mm(kt[c], ds[0]) + mm(kt[c + 1], ds[1])
            return carry

        lax.fori_loop(0, last // 2, backward_pair, 0)
        lax.fori_loop(last // 2 * 2, last, backward_step, 0)
        backward(last, True)
        if upper:
            lax.fori_loop(last + 1, chunks, clear, 0)
        for h in range(heads):
            part = slice(h * span, (h + 1) * span)
            dq_ref[pl.ds(row0, span), part] = acc_q[:, part].T * (span**-0.5)

    def give(c, carry):
        for j in range(per_chunk):
            part = slice(j * span, (j + 1) * span)
            slot = slot_of[c * per_chunk + j]
            pair, rows_at = slot // 4, pl.multiple_of(slot % 2 * span, span)
            side = jnp.where((slot // 2) % 2 == core, 0, 1)
            at = pl.ds(rows_at, span)
            sums[side, pair, at, :span] = (acc_kv[c, part, :span] * math.log(2.0)).astype(bf16)
            sums[side, pair, at, span:] = acc_kv[c, part, span:].astype(bf16)

        return carry

    lax.fori_loop(0, chunks, give, 0)
    copies = [
        pltpu.make_async_copy(sums.at[1], dkv_other_ref, sems.at[0]),
        pltpu.make_async_copy(sums.at[0], dkv_ref, sems.at[1]),
    ]
    for copy in copies:
        copy.start()
    for copy in copies:
        copy.wait()


def attention(order, own, q16, g16, kv, kv_other):
    rows_here, cols = q16.shape
    spans = order.shape[0]
    chunks = spans // per_chunk
    rows = cols
    share = jax.ShapeDtypeStruct(kv.shape, bf16)
    return pl.pallas_call(
        attention_kernel,
        out_shape=(
            jax.ShapeDtypeStruct((rows_here, cols), bf16),
            jax.ShapeDtypeStruct((rows_here, cols), f32),
            share,
            share,
        ),
        in_specs=[smem, smem] + [vmem] * 4,
        out_specs=(vmem, vmem, anywhere, anywhere),
        scratch_shapes=[
            pltpu.SMEM((spans,), jnp.int32),
            pltpu.VMEM((chunks, chunk, span), bf16),
            pltpu.VMEM((chunks, chunk, span), bf16),
            pltpu.VMEM((chunks, span, chunk), bf16),
            pltpu.VMEM((chunks, span, chunk), bf16),
            pltpu.VMEM((chunks, chunk, 2 * span), f32),
            pltpu.VMEM((rows, span), bf16),
            pltpu.VMEM((rows, span), bf16),
            pltpu.VMEM((span, rows), bf16),
            pltpu.VMEM((span, rows), bf16),
            pltpu.VMEM((span, rows), f32),
            pltpu.VMEM((1, rows), f32),
            pltpu.VMEM((1, rows), f32),
            pltpu.VMEM((1, rows), f32),
            pltpu.VMEM((span, rows), f32),
            pltpu.VMEM((2,) + kv.shape, bf16),
            pltpu.SemaphoreType.DMA((2,)),
        ],
        compiler_params=pltpu.CompilerParams(vmem_limit_bytes=36 * mib),
        cost_estimate=pl.CostEstimate(
            flops=1000, bytes_accessed=1000, transcendentals=0
        ),
        name="attention",
    )(order, own, q16, g16, kv, kv_other)


def grad_query_kernel(raw_ref, dq_ref, gain_ref, cos_ref, sin_ref, g_ref, gain_out):
    cosine, sine = cos_ref[...], sin_ref[...]
    sums = jnp.zeros((1, span), f32)
    for h in range(dq_ref.shape[1] // span):
        part = slice(h * span, (h + 1) * span)
        grad, terms = shape_head_grad(
            raw_ref[:, part].astype(f32), gain_ref[...], cosine, sine, dq_ref[:, part]
        )
        g_ref[:, part] = grad.astype(bf16)
        sums = sums + jnp.sum(terms, axis=0, keepdims=True)
    gain_out[...] = jnp.broadcast_to(sums, gain_out.shape)


def grad_key_value_kernel(raw_ref, dkv_ref, gain_ref, cos_ref, sin_ref, gain_q_ref, g_ref):
    rows = raw_ref.shape[0]
    dkv = jnp.sum(dkv_ref[...].astype(f32), axis=0)
    grad, terms = shape_head_grad(
        raw_ref[:, -span:].astype(f32), gain_ref[...], cos_ref[...], sin_ref[...], dkv[:, :span]
    )
    g_ref[:rows, :span] = grad.astype(bf16)
    g_ref[:rows, span:] = dkv[:, span:].astype(bf16)
    gain_k = jnp.sum(terms, axis=0, keepdims=True)
    split = []
    for gain in (gain_q_ref[0:1], gain_k):
        high = gain.astype(bf16).astype(f32)
        split.append(jnp.concatenate([high, gain - high], axis=1))
    row = lax.broadcasted_iota(jnp.int32, (g_ref.shape[0] - rows, 2 * span), 0)
    g_ref[rows:] = jnp.where(row == 0, split[0], jnp.where(row == 1, split[1], 0.0)).astype(bf16)


def over_tokens(where, turned_ref, blocks):
    columns = len(blocks) // 2
    toks = turned_ref.shape[2]
    y, core = where[0], where[1]
    total = 0.0
    for i, block in enumerate(blocks):
        from_y = lax.rem(y + i % columns, columns)
        from_core = core if i < columns else 1 - core
        at = (from_core * 2 + lax.rem(from_y, 2)) * 2 + from_y // 2
        total = total + mm(turned_ref[at], block[:toks])
    return total


def query_weight_grad_kernel(where, turned_ref, *rest):
    blocks, (out_ref, done_ref) = rest[:-2], rest[-2:]
    out_ref[...] = over_tokens(where, turned_ref, blocks).astype(bf16)
    done_ref[...] = jnp.zeros_like(done_ref)


def weight_grad_kernel(where, turned_ref, query_ref, *rest):
    blocks, out_ref = rest[:-1], rest[-1]
    toks = turned_ref.shape[2]
    gains = sum(block[toks:].astype(f32) for block in blocks)
    gain = gains[:8, :span] + gains[:8, span:]
    high = gain.astype(bf16).astype(f32)
    extra = jnp.concatenate([jnp.zeros((8, query_ref.shape[1]), f32), high, gain - high], axis=1)
    total = jnp.concatenate(
        [query_ref[...].astype(f32), over_tokens(where, turned_ref, blocks)], axis=1
    )
    own_rows = total.shape[0] // out_ref.shape[0]
    for i in range(out_ref.shape[0]):
        part = total[i * own_rows : (i + 1) * own_rows]
        out_ref[i] = jnp.concatenate([part, extra], axis=0).astype(bf16)


def grad_states_kernel(where, gq_ref, gkv_ref, q_ref, q_theirs_ref, kv_ref, kv_theirs_ref, out_ref):
    core = where[1]
    own_rows, group = 40, 640
    transposed = (((1,), (1,)), ((), ()))

    def product(q, kv, i):
        part = slice(i * group, (i + 1) * group)
        return lax.dot_general(
            q[part], gq_ref[...], transposed, preferred_element_type=f32
        ) + lax.dot_general(kv[part], gkv_ref[: gq_ref.shape[0]], transposed, preferred_element_type=f32)

    for i in range(q_ref.shape[0] // group):
        mine, theirs = product(q_ref, kv_ref, i), product(q_theirs_ref, kv_theirs_ref, i)
        sides = (jnp.where(core == 0, mine, theirs), jnp.where(core == 0, theirs, mine))
        rows = jnp.concatenate(
            [side[j : j + own_rows] for j in range(0, group, own_rows) for side in sides], axis=0
        )
        out_ref[:, 2 * i * group : 2 * (i + 1) * group] = rows.astype(bf16).T


def finish_kernel(parts_ref, query_ref, key_ref, value_ref, gain_q_ref, gain_k_ref):
    sums = jnp.sum(parts_ref[...].astype(f32), axis=0)
    rows, cols = query_ref.shape
    query_ref[...] = sums[:rows, :cols]
    key_ref[...] = sums[:rows, cols : cols + span]
    value_ref[...] = sums[:rows, cols + span :]
    gains = sums[rows:, cols : cols + span] + sums[rows:, cols + span :]
    gain_q_ref[...] = gains[0:1]
    gain_k_ref[...] = gains[1:2]


cheap = pl.CostEstimate(flops=1000, bytes_accessed=1000, transcendentals=0)


def call(kernel, shapes, *args, name, after=(), limit=16, scratch=()):
    count = len(args)

    def run(*refs):
        kernel(*refs[:count], *refs[count + len(after) :])

    return pl.pallas_call(
        run,
        out_shape=shapes,
        in_specs=[smem if a.dtype == jnp.int32 else vmem for a in args] + [vmem] * len(after),
        out_specs=jax.tree.map(lambda _: vmem, shapes),
        scratch_shapes=scratch,
        compiler_params=pltpu.CompilerParams(vmem_limit_bytes=limit * mib),
        cost_estimate=cheap,
        name=name,
    )(*args, *after)


plane = ("x", "z")
column = ("y_hi", "y_lo")
chips = plane + column
swapped = [(0, 0), (1, 2), (2, 1), (3, 3)]
flipped = [(0, 1), (1, 0)]


def swap(array):
    return lax.ppermute(array, ("y_hi", "core"), swapped)


def flip(array):
    return lax.ppermute(array, "core", flipped)


def to_all(array, axes, count):
    return lax.all_to_all(jnp.broadcast_to(array[None], (count,) + array.shape), axes, 0, 0)


def ring(array, step):
    return lax.ppermute(array, column, [(i, (i - step) % 4) for i in range(4)])


def around(array):
    mine = [array] + [ring(array, k) for k in range(1, 4)]
    return mine + [flip(a) for a in mine]


def local(hidden_states, block_order, w_query, w_key, w_value, gain_query, gain_key, cotangent):
    tokens = hidden_states[0]
    tok_rows, width = tokens.shape
    q_cols = w_query.shape[1]
    kv_cols = 2 * span
    own_rows = w_query.shape[0]
    planes, columns = 16, 4
    half = width // 2
    place = lax.axis_index("x") * 4 + lax.axis_index("z")
    y_hi, core = lax.axis_index("y_hi"), lax.axis_index("core")
    y = y_hi * 2 + lax.axis_index("y_lo")
    where = jnp.stack([y, core]).astype(jnp.int32)
    offsets = jnp.arange(span, dtype=jnp.int32)

    def angles_of(part):
        blocks = lax.dynamic_slice_in_dim(block_order, 2 * (place * 2 + part), 2)
        positions = (blocks[:, None] * span + offsets[None, :]).reshape(tok_rows)
        return blocks, rotation(positions, span)

    _, (cosine, sine) = angles_of(y_hi)
    own_blocks, (cos_there, sin_there) = angles_of(core)
    own = jnp.concatenate([own_blocks, core[None].astype(jnp.int32)])
    gain_q, gain_k = gain_query[None, :], gain_key[None, :]
    shape = jax.ShapeDtypeStruct

    kv_mine = to_all(jnp.concatenate([w_key, w_value], axis=1), chips, planes * columns)
    toks_mine, toks_theirs, turned, turned_theirs, done = call(
        prepare_kernel,
        (shape((tok_rows, half), bf16),) * 2
        + (shape((columns, half // columns, tok_rows), bf16),) * 2
        + (shape((8, span), f32),),
        where, tokens.T.reshape(planes, columns, 2, own_rows, tok_rows),
        name="prepare",
        after=(cosine, sine, cos_there, sin_there),
    )
    q_send = jnp.broadcast_to(w_query[None], (planes * columns, own_rows, q_cols))
    kv_mine, q_send, done, own = lax.optimization_barrier((kv_mine, q_send, done, own))
    kv_mine = kv_mine.reshape(half, kv_cols)
    kv_theirs = flip(kv_mine)
    q_mine = lax.all_to_all(q_send, chips, 0, 0).reshape(half, q_cols)

    kv16, raw_k = call(
        key_value_kernel,
        (shape((tok_rows, kv_cols), bf16), shape((tok_rows, span), f32)),
        toks_mine, toks_theirs, kv_mine, kv_theirs, gain_k, cosine, sine,
        name="key_value",
        after=(done,),
    )
    kv_send = jnp.broadcast_to(swap(kv16)[None], (planes, tok_rows, kv_cols))
    *packed, packed_done = call(
        pack_kernel,
        (shape((2, half // columns, tok_rows), bf16),) * columns + (shape((8, span), f32),),
        where, turned, flip(turned_theirs),
        name="pack",
    )
    kv_send, q_mine = lax.optimization_barrier((kv_send, q_mine))
    kv_own = lax.all_to_all(kv_send, plane, 0, 0)
    q_theirs = flip(q_mine)
    grad_out = swap(cotangent[0])
    q16, raw = call(
        query_kernel,
        (shape((tok_rows, q_cols), bf16), shape((tok_rows, q_cols + span), bf16)),
        toks_mine, toks_theirs, q_mine, q_theirs, raw_k, gain_q, cosine, sine,
        name="query",
        after=(grad_out, packed_done),
    )
    q16, raw_there = swap(q16), swap(raw)
    kv_own, q16 = lax.optimization_barrier((kv_own, q16))
    kv_other = flip(kv_own)
    turned = [packed[0]] + [
        lax.ppermute(packed[k], column, [(i, (i + k) % columns) for i in range(columns)])
        for k in range(1, columns)
    ]

    ctx, dq, dkv_mine, dkv_theirs = attention(block_order, own, q16, grad_out, kv_own, kv_other)
    dkv_theirs, turned = pl.pallas_call(
        place_kernel,
        out_shape=(
            shape(dkv_theirs.shape, bf16),
            shape((columns, 2, half // columns, tok_rows), bf16),
        ),
        in_specs=[smem, anywhere] + [vmem] * (1 + columns),
        out_specs=(anywhere, vmem),
        input_output_aliases={1: 0},
        compiler_params=pltpu.CompilerParams(vmem_limit_bytes=16 * mib),
        cost_estimate=cheap,
        name="place",
    )(where, dkv_theirs, raw_there, turned[0], turned[3], turned[2], turned[1])
    turned = turned.reshape(2 * columns, half // columns, tok_rows)
    dkv = (dkv_mine.astype(f32) + flip(dkv_theirs).astype(f32)).astype(bf16)
    dkv = lax.all_to_all(dkv, plane, 0, 0)

    g_q, gains_q = call(
        grad_query_kernel,
        (shape((tok_rows, q_cols), bf16), shape((8, span), f32)),
        raw_there, dq, gain_q, cos_there, sin_there,
        name="grad_query",
    )
    query_parts, done = call(
        query_weight_grad_kernel,
        (shape((half // columns, q_cols), bf16), shape((8, span), f32)),
        where, turned, *around(g_q),
        name="query_weight_grad",
    )
    g_q_back = swap(g_q)
    g_kv = call(
        grad_key_value_kernel,
        shape((tok_rows + 16, kv_cols), bf16),
        raw_there, dkv, gain_k, cos_there, sin_there, gains_q,
        name="grad_key_value",
        after=(done,),
    )
    blocks_kv = around(g_kv)
    g_kv_back = swap(g_kv)
    parts = call(
        weight_grad_kernel,
        shape((planes, own_rows + 8, q_cols + kv_cols), bf16),
        where, turned, query_parts, *blocks_kv,
        name="weight_grad",
        after=(g_q_back, g_kv_back),
    )
    parts = lax.all_to_all(parts, plane, 0, 0)
    own_query, own_key, own_value, gain_sum_q, gain_sum_k = call(
        finish_kernel,
        (shape((own_rows, q_cols), f32),)
        + (shape((own_rows, span), f32),) * 2
        + (shape((1, span), f32),) * 2,
        parts,
        name="finish",
    )
    grad_states = call(
        grad_states_kernel,
        shape((tok_rows, width), bf16),
        where, g_q_back, g_kv_back, q_mine, q_theirs, kv_mine, kv_theirs,
        name="grad_states",
    )
    return (
        swap(ctx)[None],
        grad_states[None],
        own_query,
        own_key,
        own_value,
        gain_sum_q[0],
        gain_sum_k[0],
    )


def solution(mesh):
    fine = Mesh(mesh.devices.reshape(4, 4, 2, 2, 2), ("x", "z", "y_hi", "y_lo", "core"))
    ctx, dp = ("x", "z", "y_hi"), ("y_lo", "core")
    rows = P(ctx + dp, None)
    tokens = P(dp, ctx, None)
    in_specs = (tokens, P(), rows, rows, rows, P(), P(), tokens)
    out_specs = (tokens, tokens, rows, rows, rows, P(), P())
    return jax.shard_map(local, mesh=fine, in_specs=in_specs, out_specs=out_specs, check_vma=False)
```

```python
import math

import jax
import jax.numpy as jnp
from jax import lax
from jax.experimental import pallas as pl
from jax.experimental.pallas import tpu as pltpu
from jax.sharding import Mesh
from jax.sharding import PartitionSpec as P

bf16, f32 = jnp.bfloat16, jnp.float32
theta = 1000000.0
floor_score = -1e30
span = 128
chunk = 512
per_chunk = chunk // span
mib = 2**20
smem = pl.BlockSpec(memory_space=pltpu.SMEM)
vmem = pl.BlockSpec(memory_space=pltpu.VMEM)
anywhere = pl.BlockSpec(memory_space=pl.ANY)


def mm(a, b):
    return jnp.dot(a, b, preferred_element_type=f32)


def rotation(positions, head_width):
    steps_half = jnp.arange(head_width // 2, dtype=f32)
    inverse = jnp.power(f32(theta), -2.0 * steps_half / head_width)
    angles = positions.astype(f32)[:, None] * inverse[None, :]
    cosine = jnp.cos(angles)
    sine = jnp.sin(angles)
    return jnp.concatenate([cosine, cosine], 1), jnp.concatenate([-sine, sine], 1)


def inverse_norm(raw):
    return lax.rsqrt(jnp.mean(raw * raw, axis=-1, keepdims=True) + 1e-06)


def shape_head(raw, gain, cosine, sine):
    normed = raw * inverse_norm(raw) * gain
    return normed * cosine + pltpu.roll(normed, span // 2, 1) * sine


def shape_head_grad(raw, gain, cosine, sine, grad):
    inverse = inverse_norm(raw)
    grad_normed = grad * cosine + pltpu.roll(grad * sine, span // 2, 1)
    grad_unit = grad_normed * gain
    unit = raw * inverse
    shrink = jnp.mean(grad_unit * unit, axis=-1, keepdims=True)
    return inverse * (grad_unit - unit * shrink), grad_normed * unit


def spread_kernel(block_ref, out_ref):
    for i in range(out_ref.shape[0]):
        out_ref[i] = block_ref[...]


def prepare_kernel(where, src_ref, w_ref, send_ref, toks_ref, toks_theirs_ref, turned_ref, turned_theirs_ref, done_ref):
    planes, columns = src_ref.shape[:2]
    core = where[1]
    done_ref[...] = jnp.zeros_like(done_ref)
    spread_kernel(w_ref, send_ref)

    def piece(plane, y, side):
        return src_ref[plane, y, side].astype(f32)

    group = 4
    for side, out_ref in ((core, toks_ref), (1 - core, toks_theirs_ref)):
        for i in range(0, planes, group):
            rows = jnp.concatenate(
                [piece(i + j, y, side) for j in range(group) for y in range(columns)], axis=0
            ).astype(bf16)
            wide = rows.shape[0]
            out_ref[:, i // group * wide : (i // group + 1) * wide] = rows.T
    for y in range(columns):
        for side, out_ref in ((core, turned_ref), (1 - core, turned_theirs_ref)):
            out_ref[y] = jnp.concatenate([piece(i, y, side) for i in range(planes)], axis=0).astype(bf16)


def pack_kernel(where, mine_ref, other_ref, *outs):
    core = where[1]
    outs, done_ref = outs[:-1], outs[-1]
    done_ref[...] = jnp.zeros_like(done_ref)
    for k, out_ref in enumerate(outs):
        at = lax.rem(where[0] + k, len(outs))
        out_ref[core] = mine_ref[at]
        out_ref[1 - core] = other_ref[at]


def place_kernel(where, dkv_ref, raw_ref, *refs):
    blocks, out_ref, sems = refs[:-3], refs[-2], refs[-1]
    copies = [
        pltpu.make_async_copy(block, out_ref.at[lax.rem(where[0] + k, len(blocks))], sems.at[k])
        for k, block in enumerate(blocks)
    ]
    for copy in copies:
        copy.start()
    for copy in copies:
        copy.wait()


def key_value_kernel(mine_ref, other_ref, w_ref, w_other_ref, gain_ref, cos_ref, sin_ref, kv_ref, raw_ref):
    raw = mm(mine_ref[...], w_ref[...]) + mm(other_ref[...], w_other_ref[...])
    raw_ref[...] = raw[:, :span]
    kv_ref[:, :span] = shape_head(raw[:, :span], gain_ref[...], cos_ref[...], sin_ref[...]).astype(bf16)
    kv_ref[:, span:] = raw[:, span:].astype(bf16)


def query_kernel(mine_ref, other_ref, w_ref, w_other_ref, raw_k_ref, gain_ref, cos_ref, sin_ref, q_ref, raw_ref):
    rows = mm(mine_ref[...], w_ref[...]) + mm(other_ref[...], w_other_ref[...])
    raw_ref[:, -span:] = raw_k_ref[...].astype(bf16)
    gain = gain_ref[...] * (span**-0.5 / math.log(2.0))
    for h in range(q_ref.shape[1] // span):
        part = slice(h * span, (h + 1) * span)
        raw_ref[:, part] = rows[:, part].astype(bf16)
        q_ref[:, part] = shape_head(rows[:, part], gain, cos_ref[...], sin_ref[...]).astype(bf16)


def attention_kernel(
    order, own, q_ref, g_ref, kv_ref, kv_other_ref, ctx_ref, dq_ref, dkv_ref, dkv_other_ref,
    slot_of, ks, vs, kt, vt, acc_kv, qs, gs, qt, gt, acc_o, row_max, row_sum, row_delta, acc_q,
    sums, sems,
):
    spans, heads = order.shape[0], q_ref.shape[1] // span
    chunks = spans // per_chunk
    rows = heads * span
    core = own[2]

    def place(slot, carry):
        slot_of[order[slot]] = slot
        return carry

    lax.fori_loop(0, spans, place, 0)

    def arrange(c, carry):
        for j in range(per_chunk):
            slot = slot_of[c * per_chunk + j]
            pair, rows_at = slot // 4, pl.multiple_of(slot % 2 * span, span)
            mine = (slot // 2) % 2 == core
            both = jnp.where(
                mine, kv_ref[pair, pl.ds(rows_at, span), :], kv_other_ref[pair, pl.ds(rows_at, span), :]
            )
            part = slice(j * span, (j + 1) * span)
            ks[c, part, :] = both[:, :span]
            vs[c, part, :] = both[:, span:]
            kt[c, :, part] = both[:, :span].T
            vt[c, :, part] = both[:, span:].T
        return carry

    lax.fori_loop(0, chunks, arrange, 0)

    def clear(c, carry):
        acc_kv[c] = jnp.zeros_like(acc_kv[c])
        return carry

    first_upper = own[0] > own[1]
    for upper in (True, False):
        which = jnp.where(first_upper, 0, 1) if upper else jnp.where(first_upper, 1, 0)
        block = own[which]
        row0 = pl.multiple_of(which * span, span)
        last = block // per_chunk
        for h in range(heads):
            part = slice(h * span, (h + 1) * span)
            qh = q_ref[pl.ds(row0, span), part]
            gh = g_ref[pl.ds(row0, span), part]
            qs[part, :] = qh
            gs[part, :] = gh
            qt[:, part] = qh.T
            gt[:, part] = gh.T

        def allowed(c):
            key_pos = c * chunk + lax.broadcasted_iota(jnp.int32, (chunk, rows), 0)
            row = lax.broadcasted_iota(jnp.int32, (chunk, rows), 1)
            return key_pos <= block * span + jnp.bitwise_and(row, span - 1)

        row_max[...] = jnp.full_like(row_max, floor_score)
        row_sum[...] = jnp.zeros_like(row_sum)
        acc_o[...] = jnp.zeros_like(acc_o)

        def forward(c, masked):
            s = mm(ks[c], qt[...])
            if masked:
                s = jnp.where(allowed(c), s, floor_score)
            old = row_max[...]
            new = jnp.maximum(old, jnp.max(s, axis=0, keepdims=True))
            p = jnp.exp2(s - new)
            alpha = jnp.exp2(old - new)
            row_max[...] = new
            row_sum[...] = row_sum[...] * alpha + jnp.sum(p, axis=0, keepdims=True)
            acc_o[...] = acc_o[...] * alpha + mm(vt[c], p.astype(bf16))

        def forward_step(c, carry):
            forward(c, False)
            return carry

        def forward_pair(i, carry):
            c = 2 * i
            s = [mm(ks[c + j], qt[...]) for j in range(2)]
            old = row_max[...]
            new = jnp.maximum(old, jnp.max(jnp.maximum(s[0], s[1]), axis=0, keepdims=True))
            p = [jnp.exp2(part - new) for part in s]
            alpha = jnp.exp2(old - new)
            row_max[...] = new
            row_sum[...] = row_sum[...] * alpha + jnp.sum(p[0] + p[1], axis=0, keepdims=True)
            acc_o[...] = (
                acc_o[...] * alpha + mm(vt[c], p[0].astype(bf16)) + mm(vt[c + 1], p[1].astype(bf16))
            )
            return carry

        lax.fori_loop(0, last // 2, forward_pair, 0)
        lax.fori_loop(last // 2 * 2, last, forward_step, 0)
        forward(last, True)

        total = row_sum[...]
        ctx_t = (acc_o[...] / total).astype(bf16)
        row_max[...] = row_max[...] + jnp.log2(total)
        row_delta[...] = jnp.sum(ctx_t.astype(f32) * gt[...].astype(f32), axis=0, keepdims=True)
        for h in range(heads):
            part = slice(h * span, (h + 1) * span)
            ctx_ref[pl.ds(row0, span), part] = ctx_t[:, part].T
        acc_q[...] = jnp.zeros_like(acc_q)

        def backward(c, masked):
            s = mm(ks[c], qt[...])
            p = jnp.exp2(s - row_max[...])
            if masked:
                p = jnp.where(allowed(c), p, 0.0)
            dp = mm(vs[c], gt[...])
            ds = (p * (dp - row_delta[...])).astype(bf16)
            dv, dk = mm(p.astype(bf16), gs[...]), mm(ds, qs[...])
            if upper:
                acc_kv[c, :, span:] = dv
                acc_kv[c, :, :span] = dk
            else:
                acc_kv[c, :, span:] += dv
                acc_kv[c, :, :span] += dk
            acc_q[...] += mm(kt[c], ds)

        def backward_step(c, carry):
            backward(c, False)
            return carry

        def backward_pair(i, carry):
            c = 2 * i
            s = [mm(ks[c + j], qt[...]) for j in range(2)]
            p = [jnp.exp2(part - row_max[...]) for part in s]
            dp = [mm(vs[c + j], gt[...]) for j in range(2)]
            ds = [(p[j] * (dp[j] - row_delta[...])).astype(bf16) for j in range(2)]
            for j in range(2):
                dv, dk = mm(p[j].astype(bf16), gs[...]), mm(ds[j], qs[...])
                if upper:
                    acc_kv[c + j, :, span:] = dv
                    acc_kv[c + j, :, :span] = dk
                else:
                    acc_kv[c + j, :, span:] += dv
                    acc_kv[c + j, :, :span] += dk
            acc_q[...] += mm(kt[c], ds[0]) + mm(kt[c + 1], ds[1])
            return carry

        lax.fori_loop(0, last // 2, backward_pair, 0)
        lax.fori_loop(last // 2 * 2, last, backward_step, 0)
        backward(last, True)
        if upper:
            lax.fori_loop(last + 1, chunks, clear, 0)
        for h in range(heads):
            part = slice(h * span, (h + 1) * span)
            dq_ref[pl.ds(row0, span), part] = acc_q[:, part].T * (span**-0.5)

    def give(c, carry):
        for j in range(per_chunk):
            part = slice(j * span, (j + 1) * span)
            slot = slot_of[c * per_chunk + j]
            pair, rows_at = slot // 4, pl.multiple_of(slot % 2 * span, span)
            side = jnp.where((slot // 2) % 2 == core, 0, 1)
            at = pl.ds(rows_at, span)
            sums[side, pair, at, :span] = (acc_kv[c, part, :span] * math.log(2.0)).astype(bf16)
            sums[side, pair, at, span:] = acc_kv[c, part, span:].astype(bf16)

        return carry

    lax.fori_loop(0, chunks, give, 0)
    copies = [
        pltpu.make_async_copy(sums.at[1], dkv_other_ref, sems.at[0]),
        pltpu.make_async_copy(sums.at[0], dkv_ref, sems.at[1]),
    ]
    for copy in copies:
        copy.start()
    for copy in copies:
        copy.wait()


def attention(order, own, q16, g16, kv, kv_other):
    rows_here, cols = q16.shape
    spans = order.shape[0]
    chunks = spans // per_chunk
    rows = cols
    share = jax.ShapeDtypeStruct(kv.shape, bf16)
    return pl.pallas_call(
        attention_kernel,
        out_shape=(
            jax.ShapeDtypeStruct((rows_here, cols), bf16),
            jax.ShapeDtypeStruct((rows_here, cols), f32),
            share,
            share,
        ),
        in_specs=[smem, smem] + [vmem] * 4,
        out_specs=(vmem, vmem, anywhere, anywhere),
        scratch_shapes=[
            pltpu.SMEM((spans,), jnp.int32),
            pltpu.VMEM((chunks, chunk, span), bf16),
            pltpu.VMEM((chunks, chunk, span), bf16),
            pltpu.VMEM((chunks, span, chunk), bf16),
            pltpu.VMEM((chunks, span, chunk), bf16),
            pltpu.VMEM((chunks, chunk, 2 * span), f32),
            pltpu.VMEM((rows, span), bf16),
            pltpu.VMEM((rows, span), bf16),
            pltpu.VMEM((span, rows), bf16),
            pltpu.VMEM((span, rows), bf16),
            pltpu.VMEM((span, rows), f32),
            pltpu.VMEM((1, rows), f32),
            pltpu.VMEM((1, rows), f32),
            pltpu.VMEM((1, rows), f32),
            pltpu.VMEM((span, rows), f32),
            pltpu.VMEM((2,) + kv.shape, bf16),
            pltpu.SemaphoreType.DMA((2,)),
        ],
        compiler_params=pltpu.CompilerParams(vmem_limit_bytes=36 * mib),
        cost_estimate=pl.CostEstimate(
            flops=1000, bytes_accessed=1000, transcendentals=0
        ),
        name="attention",
    )(order, own, q16, g16, kv, kv_other)


def grad_query_kernel(raw_ref, dq_ref, gain_ref, cos_ref, sin_ref, g_ref, gain_out):
    cosine, sine = cos_ref[...], sin_ref[...]
    sums = jnp.zeros((1, span), f32)
    for h in range(dq_ref.shape[1] // span):
        part = slice(h * span, (h + 1) * span)
        grad, terms = shape_head_grad(
            raw_ref[:, part].astype(f32), gain_ref[...], cosine, sine, dq_ref[:, part]
        )
        g_ref[:, part] = grad.astype(bf16)
        sums = sums + jnp.sum(terms, axis=0, keepdims=True)
    gain_out[...] = jnp.broadcast_to(sums, gain_out.shape)


def grad_key_value_kernel(raw_ref, dkv_ref, gain_ref, cos_ref, sin_ref, gain_q_ref, g_ref):
    rows = raw_ref.shape[0]
    dkv = jnp.sum(dkv_ref[...].astype(f32), axis=0)
    grad, terms = shape_head_grad(
        raw_ref[:, -span:].astype(f32), gain_ref[...], cos_ref[...], sin_ref[...], dkv[:, :span]
    )
    g_ref[:rows, :span] = grad.astype(bf16)
    g_ref[:rows, span:] = dkv[:, span:].astype(bf16)
    gain_k = jnp.sum(terms, axis=0, keepdims=True)
    split = []
    for gain in (gain_q_ref[0:1], gain_k):
        high = gain.astype(bf16).astype(f32)
        split.append(jnp.concatenate([high, gain - high], axis=1))
    row = lax.broadcasted_iota(jnp.int32, (g_ref.shape[0] - rows, 2 * span), 0)
    g_ref[rows:] = jnp.where(row == 0, split[0], jnp.where(row == 1, split[1], 0.0)).astype(bf16)


def over_tokens(where, turned_ref, blocks):
    columns = len(blocks) // 2
    toks = turned_ref.shape[2]
    y, core = where[0], where[1]
    total = 0.0
    for i, block in enumerate(blocks):
        from_y = lax.rem(y + i % columns, columns)
        from_core = core if i < columns else 1 - core
        at = (from_core * 2 + lax.rem(from_y, 2)) * 2 + from_y // 2
        total = total + mm(turned_ref[at], block[:toks])
    return total


def query_weight_grad_kernel(where, turned_ref, *rest):
    blocks, (out_ref, done_ref) = rest[:-2], rest[-2:]
    out_ref[...] = over_tokens(where, turned_ref, blocks).astype(bf16)
    done_ref[...] = jnp.zeros_like(done_ref)


def weight_grad_kernel(where, turned_ref, query_ref, *rest):
    blocks, (out_ref, parts, sems) = rest[:-3], rest[-3:]
    toks = turned_ref.shape[2]
    gains = sum(block[toks:].astype(f32) for block in blocks)
    gain = gains[:8, :span] + gains[:8, span:]
    high = gain.astype(bf16).astype(f32)
    extra = jnp.concatenate([jnp.zeros((8, query_ref.shape[1]), f32), high, gain - high], axis=1)
    total = jnp.concatenate(
        [query_ref[...].astype(f32), over_tokens(where, turned_ref, blocks)], axis=1
    )
    own_rows = total.shape[0] // out_ref.shape[0]
    copies = []
    for i in range(out_ref.shape[0]):
        part = total[i * own_rows : (i + 1) * own_rows]
        parts[i] = jnp.concatenate([part, extra], axis=0).astype(bf16)
        copies.append(pltpu.make_async_copy(parts.at[i], out_ref.at[i], sems.at[i]))
        copies[-1].start()
    for copy in copies:
        copy.wait()


def grad_states_kernel(where, gq_ref, gkv_ref, q_ref, q_theirs_ref, kv_ref, kv_theirs_ref, out_ref):
    core = where[1]
    own_rows, group = 40, 640
    transposed = (((1,), (1,)), ((), ()))

    def product(q, kv, i):
        part = slice(i * group, (i + 1) * group)
        return lax.dot_general(
            q[part], gq_ref[...], transposed, preferred_element_type=f32
        ) + lax.dot_general(kv[part], gkv_ref[: gq_ref.shape[0]], transposed, preferred_element_type=f32)

    for i in range(q_ref.shape[0] // group):
        mine, theirs = product(q_ref, kv_ref, i), product(q_theirs_ref, kv_theirs_ref, i)
        sides = (jnp.where(core == 0, mine, theirs), jnp.where(core == 0, theirs, mine))
        rows = jnp.concatenate(
            [side[j : j + own_rows] for j in range(0, group, own_rows) for side in sides], axis=0
        )
        out_ref[:, 2 * i * group : 2 * (i + 1) * group] = rows.astype(bf16).T


def finish_kernel(parts_ref, query_ref, key_ref, value_ref, gain_q_ref, gain_k_ref):
    sums = jnp.sum(parts_ref[...].astype(f32), axis=0)
    rows, cols = query_ref.shape
    query_ref[...] = sums[:rows, :cols]
    key_ref[...] = sums[:rows, cols : cols + span]
    value_ref[...] = sums[:rows, cols + span :]
    gains = sums[rows:, cols : cols + span] + sums[rows:, cols + span :]
    gain_q_ref[...] = gains[0:1]
    gain_k_ref[...] = gains[1:2]


cheap = pl.CostEstimate(flops=1000, bytes_accessed=1000, transcendentals=0)


def call(kernel, shapes, *args, name, after=(), limit=16, scratch=(), out_spec=vmem):
    count = len(args)

    def run(*refs):
        kernel(*refs[:count], *refs[count + len(after) :])

    return pl.pallas_call(
        run,
        out_shape=shapes,
        in_specs=[smem if a.dtype == jnp.int32 else vmem for a in args] + [vmem] * len(after),
        out_specs=jax.tree.map(lambda _: out_spec, shapes),
        scratch_shapes=scratch,
        compiler_params=pltpu.CompilerParams(vmem_limit_bytes=limit * mib),
        cost_estimate=cheap,
        name=name,
    )(*args, *after)


plane = ("x", "z")
column = ("y_hi", "y_lo")
chips = plane + column
swapped = [(0, 0), (1, 2), (2, 1), (3, 3)]
flipped = [(0, 1), (1, 0)]


def swap(array):
    return lax.ppermute(array, ("y_hi", "core"), swapped)


def flip(array):
    return lax.ppermute(array, "core", flipped)


def to_all(array, axes, count):
    return lax.all_to_all(jnp.broadcast_to(array[None], (count,) + array.shape), axes, 0, 0)


def ring(array, step):
    return lax.ppermute(array, column, [(i, (i - step) % 4) for i in range(4)])


def around(array):
    mine = [array] + [ring(array, k) for k in range(1, 4)]
    return mine + [flip(a) for a in mine]


def local(hidden_states, block_order, w_query, w_key, w_value, gain_query, gain_key, cotangent):
    tokens = hidden_states[0]
    tok_rows, width = tokens.shape
    q_cols = w_query.shape[1]
    kv_cols = 2 * span
    own_rows = w_query.shape[0]
    planes, columns = 16, 4
    half = width // 2
    place = lax.axis_index("x") * 4 + lax.axis_index("z")
    y_hi, core = lax.axis_index("y_hi"), lax.axis_index("core")
    y = y_hi * 2 + lax.axis_index("y_lo")
    where = jnp.stack([y, core]).astype(jnp.int32)
    offsets = jnp.arange(span, dtype=jnp.int32)

    def angles_of(part):
        blocks = lax.dynamic_slice_in_dim(block_order, 2 * (place * 2 + part), 2)
        positions = (blocks[:, None] * span + offsets[None, :]).reshape(tok_rows)
        return blocks, rotation(positions, span)

    _, (cosine, sine) = angles_of(y_hi)
    own_blocks, (cos_there, sin_there) = angles_of(core)
    own = jnp.concatenate([own_blocks, core[None].astype(jnp.int32)])
    gain_q, gain_k = gain_query[None, :], gain_key[None, :]
    shape = jax.ShapeDtypeStruct

    kv_mine = to_all(jnp.concatenate([w_key, w_value], axis=1), chips, planes * columns)
    q_send, toks_mine, toks_theirs, turned, turned_theirs, done = call(
        prepare_kernel,
        (shape((planes * columns, own_rows, q_cols), bf16),)
        + (shape((tok_rows, half), bf16),) * 2
        + (shape((columns, half // columns, tok_rows), bf16),) * 2
        + (shape((8, span), f32),),
        where, tokens.T.reshape(planes, columns, 2, own_rows, tok_rows), w_query,
        name="prepare",
        after=(cosine, sine, cos_there, sin_there),
    )
    kv_mine, q_send, done, own = lax.optimization_barrier((kv_mine, q_send, done, own))
    kv_mine = kv_mine.reshape(half, kv_cols)
    kv_theirs = flip(kv_mine)
    q_mine = lax.all_to_all(q_send, chips, 0, 0).reshape(half, q_cols)

    kv16, raw_k = call(
        key_value_kernel,
        (shape((tok_rows, kv_cols), bf16), shape((tok_rows, span), f32)),
        toks_mine, toks_theirs, kv_mine, kv_theirs, gain_k, cosine, sine,
        name="key_value",
        after=(done,),
    )
    kv_send = call(
        spread_kernel, shape((planes, tok_rows, kv_cols), bf16), swap(kv16), name="spread"
    )
    *packed, packed_done = call(
        pack_kernel,
        (shape((2, half // columns, tok_rows), bf16),) * columns + (shape((8, span), f32),),
        where, turned, flip(turned_theirs),
        name="pack",
    )
    kv_send, q_mine = lax.optimization_barrier((kv_send, q_mine))
    kv_own = lax.all_to_all(kv_send, plane, 0, 0)
    q_theirs = flip(q_mine)
    grad_out = swap(cotangent[0])
    q16, raw = call(
        query_kernel,
        (shape((tok_rows, q_cols), bf16), shape((tok_rows, q_cols + span), bf16)),
        toks_mine, toks_theirs, q_mine, q_theirs, raw_k, gain_q, cosine, sine,
        name="query",
        after=(grad_out, packed_done),
    )
    q16, raw_there = swap(q16), swap(raw)
    kv_own, q16 = lax.optimization_barrier((kv_own, q16))
    kv_other = flip(kv_own)
    turned = [packed[0]] + [
        lax.ppermute(packed[k], column, [(i, (i + k) % columns) for i in range(columns)])
        for k in range(1, columns)
    ]

    ctx, dq, dkv_mine, dkv_theirs = attention(block_order, own, q16, grad_out, kv_own, kv_other)
    dkv_theirs, turned = pl.pallas_call(
        place_kernel,
        out_shape=(
            shape(dkv_theirs.shape, bf16),
            shape((columns, 2, half // columns, tok_rows), bf16),
        ),
        in_specs=[smem, anywhere] + [vmem] * (1 + columns),
        out_specs=(anywhere, anywhere),
        scratch_shapes=[pltpu.SemaphoreType.DMA((columns,))],
        input_output_aliases={1: 0},
        compiler_params=pltpu.CompilerParams(vmem_limit_bytes=16 * mib),
        cost_estimate=cheap,
        name="place",
    )(where, dkv_theirs, raw_there, turned[0], turned[3], turned[2], turned[1])
    turned = turned.reshape(2 * columns, half // columns, tok_rows)
    dkv = (dkv_mine.astype(f32) + flip(dkv_theirs).astype(f32)).astype(bf16)
    dkv = lax.all_to_all(dkv, plane, 0, 0)

    g_q, gains_q = call(
        grad_query_kernel,
        (shape((tok_rows, q_cols), bf16), shape((8, span), f32)),
        raw_there, dq, gain_q, cos_there, sin_there,
        name="grad_query",
    )
    query_parts, done = call(
        query_weight_grad_kernel,
        (shape((half // columns, q_cols), bf16), shape((8, span), f32)),
        where, turned, *around(g_q),
        name="query_weight_grad",
    )
    g_q_back = swap(g_q)
    g_kv = call(
        grad_key_value_kernel,
        shape((tok_rows + 16, kv_cols), bf16),
        raw_there, dkv, gain_k, cos_there, sin_there, gains_q,
        name="grad_key_value",
        after=(done,),
    )
    blocks_kv = around(g_kv)
    g_kv_back = swap(g_kv)
    all_parts = shape((planes, own_rows + 8, q_cols + kv_cols), bf16)
    parts = call(
        weight_grad_kernel,
        all_parts,
        where, turned, query_parts, *blocks_kv,
        name="weight_grad",
        after=(g_q_back,),
        out_spec=anywhere,
        scratch=[pltpu.VMEM(all_parts.shape, bf16), pltpu.SemaphoreType.DMA((planes,))],
    )
    parts = lax.all_to_all(parts, plane, 0, 0)
    own_query, own_key, own_value, gain_sum_q, gain_sum_k = call(
        finish_kernel,
        (shape((own_rows, q_cols), f32),)
        + (shape((own_rows, span), f32),) * 2
        + (shape((1, span), f32),) * 2,
        parts,
        name="finish",
    )
    grad_states = call(
        grad_states_kernel,
        shape((tok_rows, width), bf16),
        where, g_q_back, g_kv_back, q_mine, q_theirs, kv_mine, kv_theirs,
        name="grad_states",
    )
    return (
        swap(ctx)[None],
        grad_states[None],
        own_query,
        own_key,
        own_value,
        gain_sum_q[0],
        gain_sum_k[0],
    )


def solution(mesh):
    fine = Mesh(mesh.devices.reshape(4, 4, 2, 2, 2), ("x", "z", "y_hi", "y_lo", "core"))
    ctx, dp = ("x", "z", "y_hi"), ("y_lo", "core")
    rows = P(ctx + dp, None)
    tokens = P(dp, ctx, None)
    in_specs = (tokens, P(), rows, rows, rows, P(), P(), tokens)
    out_specs = (tokens, tokens, rows, rows, rows, P(), P())
    return jax.shard_map(local, mesh=fine, in_specs=in_specs, out_specs=out_specs, check_vma=False)
```

```python
import math

import jax
import jax.numpy as jnp
from jax import lax
from jax.experimental import pallas as pl
from jax.experimental.pallas import tpu as pltpu
from jax.sharding import Mesh
from jax.sharding import PartitionSpec as P

bf16, f32 = jnp.bfloat16, jnp.float32
theta = 1000000.0
floor_score = -1e30
span = 128
chunk = 512
per_chunk = chunk // span
mib = 2**20
smem = pl.BlockSpec(memory_space=pltpu.SMEM)
vmem = pl.BlockSpec(memory_space=pltpu.VMEM)
anywhere = pl.BlockSpec(memory_space=pl.ANY)
hbm = pl.BlockSpec(memory_space=pltpu.HBM)


def mm(a, b):
    return jnp.dot(a, b, preferred_element_type=f32)


def rotation(positions, head_width):
    steps_half = jnp.arange(head_width // 2, dtype=f32)
    inverse = jnp.power(f32(theta), -2.0 * steps_half / head_width)
    angles = positions.astype(f32)[:, None] * inverse[None, :]
    cosine = jnp.cos(angles)
    sine = jnp.sin(angles)
    return jnp.concatenate([cosine, cosine], 1), jnp.concatenate([-sine, sine], 1)


def inverse_norm(raw):
    return lax.rsqrt(jnp.mean(raw * raw, axis=-1, keepdims=True) + 1e-06)


def shape_head(raw, gain, cosine, sine):
    normed = raw * inverse_norm(raw) * gain
    return normed * cosine + pltpu.roll(normed, span // 2, 1) * sine


def shape_head_grad(raw, gain, cosine, sine, grad):
    inverse = inverse_norm(raw)
    grad_normed = grad * cosine + pltpu.roll(grad * sine, span // 2, 1)
    grad_unit = grad_normed * gain
    unit = raw * inverse
    shrink = jnp.mean(grad_unit * unit, axis=-1, keepdims=True)
    return inverse * (grad_unit - unit * shrink), grad_normed * unit


def spread_kernel(block_ref, out_ref):
    for i in range(out_ref.shape[0]):
        out_ref[i] = block_ref[...]


def prepare_kernel(where, src_ref, w_ref, send_ref, toks_ref, toks_theirs_ref, turned_ref, turned_theirs_ref, done_ref):
    planes, columns = src_ref.shape[:2]
    core = where[1]
    done_ref[...] = jnp.zeros_like(done_ref)
    spread_kernel(w_ref, send_ref)

    def piece(plane, y, side):
        return src_ref[plane, y, side].astype(f32)

    group = 4
    for side, out_ref in ((core, toks_ref), (1 - core, toks_theirs_ref)):
        for i in range(0, planes, group):
            rows = jnp.concatenate(
                [piece(i + j, y, side) for j in range(group) for y in range(columns)], axis=0
            ).astype(bf16)
            wide = rows.shape[0]
            out_ref[:, i // group * wide : (i // group + 1) * wide] = rows.T
    for y in range(columns):
        for side, out_ref in ((core, turned_ref), (1 - core, turned_theirs_ref)):
            out_ref[y] = jnp.concatenate([piece(i, y, side) for i in range(planes)], axis=0).astype(bf16)


def pack_kernel(where, mine_ref, other_ref, *outs):
    core = where[1]
    outs, done_ref = outs[:-1], outs[-1]
    done_ref[...] = jnp.zeros_like(done_ref)
    for k, out_ref in enumerate(outs):
        at = lax.rem(where[0] + k, len(outs))
        out_ref[core] = mine_ref[at]
        out_ref[1 - core] = other_ref[at]


def place_kernel(where, dkv_ref, raw_ref, *refs):
    blocks, out_ref, sems = refs[:-3], refs[-2], refs[-1]
    copies = [
        pltpu.make_async_copy(block, out_ref.at[lax.rem(where[0] + k, len(blocks))], sems.at[k])
        for k, block in enumerate(blocks)
    ]
    for copy in copies:
        copy.start()
    for copy in copies:
        copy.wait()


def key_value_kernel(mine_ref, other_ref, w_ref, w_other_ref, gain_ref, cos_ref, sin_ref, kv_ref, raw_ref):
    raw = mm(mine_ref[...], w_ref[...]) + mm(other_ref[...], w_other_ref[...])
    raw_ref[...] = raw[:, :span]
    kv_ref[:, :span] = shape_head(raw[:, :span], gain_ref[...], cos_ref[...], sin_ref[...]).astype(bf16)
    kv_ref[:, span:] = raw[:, span:].astype(bf16)


def query_kernel(mine_ref, other_ref, w_ref, w_other_ref, raw_k_ref, gain_ref, cos_ref, sin_ref, q_ref, raw_ref):
    rows = mm(mine_ref[...], w_ref[...]) + mm(other_ref[...], w_other_ref[...])
    raw_ref[:, -span:] = raw_k_ref[...].astype(bf16)
    gain = gain_ref[...] * (span**-0.5 / math.log(2.0))
    for h in range(q_ref.shape[1] // span):
        part = slice(h * span, (h + 1) * span)
        raw_ref[:, part] = rows[:, part].astype(bf16)
        q_ref[:, part] = shape_head(rows[:, part], gain, cos_ref[...], sin_ref[...]).astype(bf16)


def attention_kernel(
    order, own, q_ref, g_ref, kv_ref, kv_other_ref, ctx_ref, dq_ref, dkv_ref, dkv_other_ref,
    slot_of, ks, vs, kt, vt, acc_kv, qs, gs, qt, gt, acc_o, row_max, row_sum, row_delta, acc_q,
    sums, sems,
):
    spans, heads = order.shape[0], q_ref.shape[1] // span
    chunks = spans // per_chunk
    rows = heads * span
    core = own[2]

    def place(slot, carry):
        slot_of[order[slot]] = slot
        return carry

    lax.fori_loop(0, spans, place, 0)

    def arrange(c, carry):
        for j in range(per_chunk):
            slot = slot_of[c * per_chunk + j]
            pair, rows_at = slot // 4, pl.multiple_of(slot % 2 * span, span)
            mine = (slot // 2) % 2 == core
            both = jnp.where(
                mine, kv_ref[pair, pl.ds(rows_at, span), :], kv_other_ref[pair, pl.ds(rows_at, span), :]
            )
            part = slice(j * span, (j + 1) * span)
            ks[c, part, :] = both[:, :span]
            vs[c, part, :] = both[:, span:]
            kt[c, :, part] = both[:, :span].T
            vt[c, :, part] = both[:, span:].T
        return carry

    lax.fori_loop(0, chunks, arrange, 0)

    def clear(c, carry):
        acc_kv[c] = jnp.zeros_like(acc_kv[c])
        return carry

    first_upper = own[0] > own[1]
    for upper in (True, False):
        which = jnp.where(first_upper, 0, 1) if upper else jnp.where(first_upper, 1, 0)
        block = own[which]
        row0 = pl.multiple_of(which * span, span)
        last = block // per_chunk
        for h in range(heads):
            part = slice(h * span, (h + 1) * span)
            qh = q_ref[pl.ds(row0, span), part]
            gh = g_ref[pl.ds(row0, span), part]
            qs[part, :] = qh
            gs[part, :] = gh
            qt[:, part] = qh.T
            gt[:, part] = gh.T

        def allowed(c):
            key_pos = c * chunk + lax.broadcasted_iota(jnp.int32, (chunk, rows), 0)
            row = lax.broadcasted_iota(jnp.int32, (chunk, rows), 1)
            return key_pos <= block * span + jnp.bitwise_and(row, span - 1)

        row_max[...] = jnp.full_like(row_max, floor_score)
        row_sum[...] = jnp.zeros_like(row_sum)
        acc_o[...] = jnp.zeros_like(acc_o)

        def forward(c, masked):
            s = mm(ks[c], qt[...])
            if masked:
                s = jnp.where(allowed(c), s, floor_score)
            old = row_max[...]
            new = jnp.maximum(old, jnp.max(s, axis=0, keepdims=True))
            p = jnp.exp2(s - new)
            alpha = jnp.exp2(old - new)
            row_max[...] = new
            row_sum[...] = row_sum[...] * alpha + jnp.sum(p, axis=0, keepdims=True)
            acc_o[...] = acc_o[...] * alpha + mm(vt[c], p.astype(bf16))

        def forward_step(c, carry):
            forward(c, False)
            return carry

        def forward_pair(i, carry):
            c = 2 * i
            s = [mm(ks[c + j], qt[...]) for j in range(2)]
            old = row_max[...]
            new = jnp.maximum(old, jnp.max(jnp.maximum(s[0], s[1]), axis=0, keepdims=True))
            p = [jnp.exp2(part - new) for part in s]
            alpha = jnp.exp2(old - new)
            row_max[...] = new
            row_sum[...] = row_sum[...] * alpha + jnp.sum(p[0] + p[1], axis=0, keepdims=True)
            acc_o[...] = (
                acc_o[...] * alpha + mm(vt[c], p[0].astype(bf16)) + mm(vt[c + 1], p[1].astype(bf16))
            )
            return carry

        lax.fori_loop(0, last // 2, forward_pair, 0)
        lax.fori_loop(last // 2 * 2, last, forward_step, 0)
        forward(last, True)

        total = row_sum[...]
        ctx_t = (acc_o[...] / total).astype(bf16)
        row_max[...] = row_max[...] + jnp.log2(total)
        row_delta[...] = jnp.sum(ctx_t.astype(f32) * gt[...].astype(f32), axis=0, keepdims=True)
        for h in range(heads):
            part = slice(h * span, (h + 1) * span)
            ctx_ref[pl.ds(row0, span), part] = ctx_t[:, part].T
        acc_q[...] = jnp.zeros_like(acc_q)

        def backward(c, masked):
            s = mm(ks[c], qt[...])
            p = jnp.exp2(s - row_max[...])
            if masked:
                p = jnp.where(allowed(c), p, 0.0)
            dp = mm(vs[c], gt[...])
            ds = (p * (dp - row_delta[...])).astype(bf16)
            dv, dk = mm(p.astype(bf16), gs[...]), mm(ds, qs[...])
            if upper:
                acc_kv[c, :, span:] = dv
                acc_kv[c, :, :span] = dk
            else:
                acc_kv[c, :, span:] += dv
                acc_kv[c, :, :span] += dk
            acc_q[...] += mm(kt[c], ds)

        def backward_step(c, carry):
            backward(c, False)
            return carry

        def backward_pair(i, carry):
            c = 2 * i
            s = [mm(ks[c + j], qt[...]) for j in range(2)]
            p = [jnp.exp2(part - row_max[...]) for part in s]
            dp = [mm(vs[c + j], gt[...]) for j in range(2)]
            ds = [(p[j] * (dp[j] - row_delta[...])).astype(bf16) for j in range(2)]
            for j in range(2):
                dv, dk = mm(p[j].astype(bf16), gs[...]), mm(ds[j], qs[...])
                if upper:
                    acc_kv[c + j, :, span:] = dv
                    acc_kv[c + j, :, :span] = dk
                else:
                    acc_kv[c + j, :, span:] += dv
                    acc_kv[c + j, :, :span] += dk
            acc_q[...] += mm(kt[c], ds[0]) + mm(kt[c + 1], ds[1])
            return carry

        lax.fori_loop(0, last // 2, backward_pair, 0)
        lax.fori_loop(last // 2 * 2, last, backward_step, 0)
        backward(last, True)
        if upper:
            lax.fori_loop(last + 1, chunks, clear, 0)
        for h in range(heads):
            part = slice(h * span, (h + 1) * span)
            dq_ref[pl.ds(row0, span), part] = acc_q[:, part].T * (span**-0.5)

    def give(c, carry):
        for j in range(per_chunk):
            part = slice(j * span, (j + 1) * span)
            slot = slot_of[c * per_chunk + j]
            pair, rows_at = slot // 4, pl.multiple_of(slot % 2 * span, span)
            side = jnp.where((slot // 2) % 2 == core, 0, 1)
            at = pl.ds(rows_at, span)
            sums[side, pair, at, :span] = (acc_kv[c, part, :span] * math.log(2.0)).astype(bf16)
            sums[side, pair, at, span:] = acc_kv[c, part, span:].astype(bf16)

        return carry

    lax.fori_loop(0, chunks, give, 0)
    copies = [
        pltpu.make_async_copy(sums.at[1], dkv_other_ref, sems.at[0]),
        pltpu.make_async_copy(sums.at[0], dkv_ref, sems.at[1]),
    ]
    for copy in copies:
        copy.start()
    for copy in copies:
        copy.wait()


def attention(order, own, q16, g16, kv, kv_other):
    rows_here, cols = q16.shape
    spans = order.shape[0]
    chunks = spans // per_chunk
    rows = cols
    share = jax.ShapeDtypeStruct(kv.shape, bf16)
    return pl.pallas_call(
        attention_kernel,
        out_shape=(
            jax.ShapeDtypeStruct((rows_here, cols), bf16),
            jax.ShapeDtypeStruct((rows_here, cols), f32),
            share,
            share,
        ),
        in_specs=[smem, smem] + [vmem] * 4,
        out_specs=(vmem, vmem, anywhere, anywhere),
        scratch_shapes=[
            pltpu.SMEM((spans,), jnp.int32),
            pltpu.VMEM((chunks, chunk, span), bf16),
            pltpu.VMEM((chunks, chunk, span), bf16),
            pltpu.VMEM((chunks, span, chunk), bf16),
            pltpu.VMEM((chunks, span, chunk), bf16),
            pltpu.VMEM((chunks, chunk, 2 * span), f32),
            pltpu.VMEM((rows, span), bf16),
            pltpu.VMEM((rows, span), bf16),
            pltpu.VMEM((span, rows), bf16),
            pltpu.VMEM((span, rows), bf16),
            pltpu.VMEM((span, rows), f32),
            pltpu.VMEM((1, rows), f32),
            pltpu.VMEM((1, rows), f32),
            pltpu.VMEM((1, rows), f32),
            pltpu.VMEM((span, rows), f32),
            pltpu.VMEM((2,) + kv.shape, bf16),
            pltpu.SemaphoreType.DMA((2,)),
        ],
        compiler_params=pltpu.CompilerParams(vmem_limit_bytes=36 * mib),
        cost_estimate=pl.CostEstimate(
            flops=1000, bytes_accessed=1000, transcendentals=0
        ),
        name="attention",
    )(order, own, q16, g16, kv, kv_other)


def grad_query_kernel(raw_ref, dq_ref, gain_ref, cos_ref, sin_ref, g_ref, gain_out):
    cosine, sine = cos_ref[...], sin_ref[...]
    sums = jnp.zeros((1, span), f32)
    for h in range(dq_ref.shape[1] // span):
        part = slice(h * span, (h + 1) * span)
        grad, terms = shape_head_grad(
            raw_ref[:, part].astype(f32), gain_ref[...], cosine, sine, dq_ref[:, part]
        )
        g_ref[:, part] = grad.astype(bf16)
        sums = sums + jnp.sum(terms, axis=0, keepdims=True)
    gain_out[...] = jnp.broadcast_to(sums, gain_out.shape)


def grad_key_value_kernel(raw_ref, dkv_ref, gain_ref, cos_ref, sin_ref, gain_q_ref, g_ref):
    rows = raw_ref.shape[0]
    dkv = jnp.sum(dkv_ref[...].astype(f32), axis=0)
    grad, terms = shape_head_grad(
        raw_ref[:, -span:].astype(f32), gain_ref[...], cos_ref[...], sin_ref[...], dkv[:, :span]
    )
    g_ref[:rows, :span] = grad.astype(bf16)
    g_ref[:rows, span:] = dkv[:, span:].astype(bf16)
    gain_k = jnp.sum(terms, axis=0, keepdims=True)
    split = []
    for gain in (gain_q_ref[0:1], gain_k):
        high = gain.astype(bf16).astype(f32)
        split.append(jnp.concatenate([high, gain - high], axis=1))
    row = lax.broadcasted_iota(jnp.int32, (g_ref.shape[0] - rows, 2 * span), 0)
    g_ref[rows:] = jnp.where(row == 0, split[0], jnp.where(row == 1, split[1], 0.0)).astype(bf16)


def over_tokens(where, turned_ref, blocks):
    columns = len(blocks) // 2
    toks = turned_ref.shape[2]
    y, core = where[0], where[1]
    total = 0.0
    for i, block in enumerate(blocks):
        from_y = lax.rem(y + i % columns, columns)
        from_core = core if i < columns else 1 - core
        at = (from_core * 2 + lax.rem(from_y, 2)) * 2 + from_y // 2
        total = total + mm(turned_ref[at], block[:toks])
    return total


def query_weight_grad_kernel(where, turned_ref, *rest):
    blocks, (out_ref, done_ref) = rest[:-2], rest[-2:]
    out_ref[...] = over_tokens(where, turned_ref, blocks).astype(bf16)
    done_ref[...] = jnp.zeros_like(done_ref)


def weight_grad_kernel(where, turned_ref, query_ref, *rest):
    blocks, (out_ref, parts, sems) = rest[:-3], rest[-3:]
    toks = turned_ref.shape[2]
    gains = sum(block[toks:].astype(f32) for block in blocks)
    gain = gains[:8, :span] + gains[:8, span:]
    high = gain.astype(bf16).astype(f32)
    extra = jnp.concatenate([jnp.zeros((8, query_ref.shape[1]), f32), high, gain - high], axis=1)
    total = jnp.concatenate(
        [query_ref[...].astype(f32), over_tokens(where, turned_ref, blocks)], axis=1
    )
    own_rows = total.shape[0] // out_ref.shape[0]
    copies = []
    for i in range(out_ref.shape[0]):
        part = total[i * own_rows : (i + 1) * own_rows]
        parts[i] = jnp.concatenate([part, extra], axis=0).astype(bf16)
        copies.append(pltpu.make_async_copy(parts.at[i], out_ref.at[i], sems.at[i]))
        copies[-1].start()
    for copy in copies:
        copy.wait()


def grad_states_kernel(where, gq_ref, gkv_ref, q_ref, q_theirs_ref, kv_ref, kv_theirs_ref, out_ref):
    core = where[1]
    own_rows, group = 40, 640
    transposed = (((1,), (1,)), ((), ()))

    def product(q, kv, i):
        part = slice(i * group, (i + 1) * group)
        return lax.dot_general(
            q[part], gq_ref[...], transposed, preferred_element_type=f32
        ) + lax.dot_general(kv[part], gkv_ref[: gq_ref.shape[0]], transposed, preferred_element_type=f32)

    for i in range(q_ref.shape[0] // group):
        mine, theirs = product(q_ref, kv_ref, i), product(q_theirs_ref, kv_theirs_ref, i)
        sides = (jnp.where(core == 0, mine, theirs), jnp.where(core == 0, theirs, mine))
        rows = jnp.concatenate(
            [side[j : j + own_rows] for j in range(0, group, own_rows) for side in sides], axis=0
        )
        out_ref[:, 2 * i * group : 2 * (i + 1) * group] = rows.astype(bf16).T


def finish_kernel(parts_ref, query_ref, key_ref, value_ref, gain_q_ref, gain_k_ref):
    sums = jnp.sum(parts_ref[...].astype(f32), axis=0)
    rows, cols = query_ref.shape
    query_ref[...] = sums[:rows, :cols]
    key_ref[...] = sums[:rows, cols : cols + span]
    value_ref[...] = sums[:rows, cols + span :]
    gains = sums[rows:, cols : cols + span] + sums[rows:, cols + span :]
    gain_q_ref[...] = gains[0:1]
    gain_k_ref[...] = gains[1:2]


cheap = pl.CostEstimate(flops=1000, bytes_accessed=1000, transcendentals=0)


def call(kernel, shapes, *args, name, after=(), limit=16, scratch=(), out_spec=vmem):
    count = len(args)

    def run(*refs):
        kernel(*refs[:count], *refs[count + len(after) :])

    return pl.pallas_call(
        run,
        out_shape=shapes,
        in_specs=[smem if a.dtype == jnp.int32 else vmem for a in args] + [vmem] * len(after),
        out_specs=jax.tree.map(lambda _: out_spec, shapes),
        scratch_shapes=scratch,
        compiler_params=pltpu.CompilerParams(vmem_limit_bytes=limit * mib),
        cost_estimate=cheap,
        name=name,
    )(*args, *after)


plane = ("x", "z")
column = ("y_hi", "y_lo")
chips = plane + column
swapped = [(0, 0), (1, 2), (2, 1), (3, 3)]
flipped = [(0, 1), (1, 0)]


def swap(array):
    return lax.ppermute(array, ("y_hi", "core"), swapped)


def flip(array):
    return lax.ppermute(array, "core", flipped)


def to_all(array, axes, count):
    return lax.all_to_all(jnp.broadcast_to(array[None], (count,) + array.shape), axes, 0, 0)


def ring(array, step):
    return lax.ppermute(array, column, [(i, (i - step) % 4) for i in range(4)])


def around(array):
    mine = [array] + [ring(array, k) for k in range(1, 4)]
    return mine + [flip(a) for a in mine]


def local(hidden_states, block_order, w_query, w_key, w_value, gain_query, gain_key, cotangent):
    tokens = hidden_states[0]
    tok_rows, width = tokens.shape
    q_cols = w_query.shape[1]
    kv_cols = 2 * span
    own_rows = w_query.shape[0]
    planes, columns = 16, 4
    half = width // 2
    place = lax.axis_index("x") * 4 + lax.axis_index("z")
    y_hi, core = lax.axis_index("y_hi"), lax.axis_index("core")
    y = y_hi * 2 + lax.axis_index("y_lo")
    where = jnp.stack([y, core]).astype(jnp.int32)
    offsets = jnp.arange(span, dtype=jnp.int32)

    def angles_of(part):
        blocks = lax.dynamic_slice_in_dim(block_order, 2 * (place * 2 + part), 2)
        positions = (blocks[:, None] * span + offsets[None, :]).reshape(tok_rows)
        return blocks, rotation(positions, span)

    _, (cosine, sine) = angles_of(y_hi)
    own_blocks, (cos_there, sin_there) = angles_of(core)
    own = jnp.concatenate([own_blocks, core[None].astype(jnp.int32)])
    gain_q, gain_k = gain_query[None, :], gain_key[None, :]
    shape = jax.ShapeDtypeStruct

    kv_mine = to_all(jnp.concatenate([w_key, w_value], axis=1), chips, planes * columns)
    q_send, toks_mine, toks_theirs, turned, turned_theirs, done = call(
        prepare_kernel,
        (shape((planes * columns, own_rows, q_cols), bf16),)
        + (shape((tok_rows, half), bf16),) * 2
        + (shape((columns, half // columns, tok_rows), bf16),) * 2
        + (shape((8, span), f32),),
        where, tokens.T.reshape(planes, columns, 2, own_rows, tok_rows), w_query,
        name="prepare",
        after=(cosine, sine, cos_there, sin_there),
    )
    kv_mine, q_send, done, own = lax.optimization_barrier((kv_mine, q_send, done, own))
    kv_mine = kv_mine.reshape(half, kv_cols)
    kv_theirs = flip(kv_mine)
    q_mine = lax.all_to_all(q_send, chips, 0, 0).reshape(half, q_cols)

    kv16, raw_k = call(
        key_value_kernel,
        (shape((tok_rows, kv_cols), bf16), shape((tok_rows, span), f32)),
        toks_mine, toks_theirs, kv_mine, kv_theirs, gain_k, cosine, sine,
        name="key_value",
        after=(done,),
    )
    kv_send = call(
        spread_kernel, shape((planes, tok_rows, kv_cols), bf16), swap(kv16), name="spread"
    )
    *packed, packed_done = call(
        pack_kernel,
        (shape((2, half // columns, tok_rows), bf16),) * columns + (shape((8, span), f32),),
        where, turned, flip(turned_theirs),
        name="pack",
    )
    kv_send, q_mine = lax.optimization_barrier((kv_send, q_mine))
    kv_own = lax.all_to_all(kv_send, plane, 0, 0)
    q_theirs = flip(q_mine)
    grad_out = swap(cotangent[0])
    q16, raw = call(
        query_kernel,
        (shape((tok_rows, q_cols), bf16), shape((tok_rows, q_cols + span), bf16)),
        toks_mine, toks_theirs, q_mine, q_theirs, raw_k, gain_q, cosine, sine,
        name="query",
        after=(grad_out, packed_done),
    )
    q16, raw_there = swap(q16), swap(raw)
    kv_own, q16 = lax.optimization_barrier((kv_own, q16))
    kv_other = flip(kv_own)
    turned = [packed[0]] + [
        lax.ppermute(packed[k], column, [(i, (i + k) % columns) for i in range(columns)])
        for k in range(1, columns)
    ]

    ctx, dq, dkv_mine, dkv_theirs = attention(block_order, own, q16, grad_out, kv_own, kv_other)
    dkv_theirs, turned = pl.pallas_call(
        place_kernel,
        out_shape=(
            shape(dkv_theirs.shape, bf16),
            shape((columns, 2, half // columns, tok_rows), bf16),
        ),
        in_specs=[smem, anywhere] + [vmem] * (1 + columns),
        out_specs=(anywhere, hbm),
        scratch_shapes=[pltpu.SemaphoreType.DMA((columns,))],
        input_output_aliases={1: 0},
        compiler_params=pltpu.CompilerParams(vmem_limit_bytes=16 * mib),
        cost_estimate=cheap,
        name="place",
    )(where, dkv_theirs, raw_there, turned[0], turned[3], turned[2], turned[1])
    turned = turned.reshape(2 * columns, half // columns, tok_rows)
    dkv = (dkv_mine.astype(f32) + flip(dkv_theirs).astype(f32)).astype(bf16)
    dkv = lax.all_to_all(dkv, plane, 0, 0)

    g_q, gains_q = call(
        grad_query_kernel,
        (shape((tok_rows, q_cols), bf16), shape((8, span), f32)),
        raw_there, dq, gain_q, cos_there, sin_there,
        name="grad_query",
    )
    query_parts, done = call(
        query_weight_grad_kernel,
        (shape((half // columns, q_cols), bf16), shape((8, span), f32)),
        where, turned, *around(g_q),
        name="query_weight_grad",
    )
    g_q_back = swap(g_q)
    g_kv = call(
        grad_key_value_kernel,
        shape((tok_rows + 16, kv_cols), bf16),
        raw_there, dkv, gain_k, cos_there, sin_there, gains_q,
        name="grad_key_value",
        after=(done, g_q_back),
    )
    blocks_kv = around(g_kv)
    g_kv_back = swap(g_kv)
    all_parts = shape((planes, own_rows + 8, q_cols + kv_cols), bf16)
    parts = call(
        weight_grad_kernel,
        all_parts,
        where, turned, query_parts, *blocks_kv,
        name="weight_grad",
        out_spec=hbm,
        scratch=[pltpu.VMEM(all_parts.shape, bf16), pltpu.SemaphoreType.DMA((planes,))],
    )
    parts = lax.all_to_all(parts, plane, 0, 0)
    own_query, own_key, own_value, gain_sum_q, gain_sum_k = call(
        finish_kernel,
        (shape((own_rows, q_cols), f32),)
        + (shape((own_rows, span), f32),) * 2
        + (shape((1, span), f32),) * 2,
        parts,
        name="finish",
    )
    grad_states = call(
        grad_states_kernel,
        shape((tok_rows, width), bf16),
        where, g_q_back, g_kv_back, q_mine, q_theirs, kv_mine, kv_theirs,
        name="grad_states",
    )
    return (
        swap(ctx)[None],
        grad_states[None],
        own_query,
        own_key,
        own_value,
        gain_sum_q[0],
        gain_sum_k[0],
    )


def solution(mesh):
    fine = Mesh(mesh.devices.reshape(4, 4, 2, 2, 2), ("x", "z", "y_hi", "y_lo", "core"))
    ctx, dp = ("x", "z", "y_hi"), ("y_lo", "core")
    rows = P(ctx + dp, None)
    tokens = P(dp, ctx, None)
    in_specs = (tokens, P(), rows, rows, rows, P(), P(), tokens)
    out_specs = (tokens, tokens, rows, rows, rows, P(), P())
    return jax.shard_map(local, mesh=fine, in_specs=in_specs, out_specs=out_specs, check_vma=False)
```

```python
import math

import jax
import jax.numpy as jnp
from jax import lax
from jax.experimental import pallas as pl
from jax.experimental.pallas import tpu as pltpu
from jax.sharding import Mesh
from jax.sharding import PartitionSpec as P

bf16, f32 = jnp.bfloat16, jnp.float32
theta = 1000000.0
floor_score = -1e30
span = 128
chunk = 512
per_chunk = chunk // span
mib = 2**20
smem = pl.BlockSpec(memory_space=pltpu.SMEM)
vmem = pl.BlockSpec(memory_space=pltpu.VMEM)
anywhere = pl.BlockSpec(memory_space=pl.ANY)
hbm = pl.BlockSpec(memory_space=pltpu.HBM)


def mm(a, b):
    return jnp.dot(a, b, preferred_element_type=f32)


def rotation(positions, head_width):
    steps_half = jnp.arange(head_width // 2, dtype=f32)
    inverse = jnp.power(f32(theta), -2.0 * steps_half / head_width)
    angles = positions.astype(f32)[:, None] * inverse[None, :]
    cosine = jnp.cos(angles)
    sine = jnp.sin(angles)
    return jnp.concatenate([cosine, cosine], 1), jnp.concatenate([-sine, sine], 1)


def inverse_norm(raw):
    return lax.rsqrt(jnp.mean(raw * raw, axis=-1, keepdims=True) + 1e-06)


def shape_head(raw, gain, cosine, sine):
    normed = raw * inverse_norm(raw) * gain
    return normed * cosine + pltpu.roll(normed, span // 2, 1) * sine


def shape_head_grad(raw, gain, cosine, sine, grad):
    inverse = inverse_norm(raw)
    grad_normed = grad * cosine + pltpu.roll(grad * sine, span // 2, 1)
    grad_unit = grad_normed * gain
    unit = raw * inverse
    shrink = jnp.mean(grad_unit * unit, axis=-1, keepdims=True)
    return inverse * (grad_unit - unit * shrink), grad_normed * unit


def spread_kernel(block_ref, out_ref):
    for i in range(out_ref.shape[0]):
        out_ref[i] = block_ref[...]


def prepare_kernel(where, src_ref, w_ref, send_ref, toks_ref, toks_theirs_ref, turned_ref, turned_theirs_ref, done_ref):
    planes, columns = src_ref.shape[:2]
    core = where[1]
    done_ref[...] = jnp.zeros_like(done_ref)
    spread_kernel(w_ref, send_ref)

    def piece(plane, y, side):
        return src_ref[plane, y, side].astype(f32)

    group = 4
    for side, out_ref in ((core, toks_ref), (1 - core, toks_theirs_ref)):
        for i in range(0, planes, group):
            rows = jnp.concatenate(
                [piece(i + j, y, side) for j in range(group) for y in range(columns)], axis=0
            ).astype(bf16)
            wide = rows.shape[0]
            out_ref[:, i // group * wide : (i // group + 1) * wide] = rows.T
    for y in range(columns):
        for side, out_ref in ((core, turned_ref), (1 - core, turned_theirs_ref)):
            out_ref[y] = jnp.concatenate([piece(i, y, side) for i in range(planes)], axis=0).astype(bf16)


def pack_kernel(where, mine_ref, other_ref, *outs):
    core = where[1]
    outs, done_ref = outs[:-1], outs[-1]
    done_ref[...] = jnp.zeros_like(done_ref)
    for k, out_ref in enumerate(outs):
        at = lax.rem(where[0] + k, len(outs))
        out_ref[core] = mine_ref[at]
        out_ref[1 - core] = other_ref[at]


def place_kernel(where, dkv_ref, raw_ref, *refs):
    blocks, out_ref = refs[:-2], refs[-1]
    for k, block in enumerate(blocks):
        out_ref[lax.rem(where[0] + k, len(blocks))] = block[...]


def key_value_kernel(mine_ref, other_ref, w_ref, w_other_ref, gain_ref, cos_ref, sin_ref, kv_ref, raw_ref):
    raw = mm(mine_ref[...], w_ref[...]) + mm(other_ref[...], w_other_ref[...])
    raw_ref[...] = raw[:, :span]
    kv_ref[:, :span] = shape_head(raw[:, :span], gain_ref[...], cos_ref[...], sin_ref[...]).astype(bf16)
    kv_ref[:, span:] = raw[:, span:].astype(bf16)


def query_kernel(mine_ref, other_ref, w_ref, w_other_ref, raw_k_ref, gain_ref, cos_ref, sin_ref, q_ref, raw_ref):
    rows = mm(mine_ref[...], w_ref[...]) + mm(other_ref[...], w_other_ref[...])
    raw_ref[:, -span:] = raw_k_ref[...].astype(bf16)
    gain = gain_ref[...] * (span**-0.5 / math.log(2.0))
    for h in range(q_ref.shape[1] // span):
        part = slice(h * span, (h + 1) * span)
        raw_ref[:, part] = rows[:, part].astype(bf16)
        q_ref[:, part] = shape_head(rows[:, part], gain, cos_ref[...], sin_ref[...]).astype(bf16)


def attention_kernel(
    order, own, q_ref, g_ref, kv_ref, kv_other_ref, ctx_ref, dq_ref, dkv_ref, dkv_other_ref,
    slot_of, ks, vs, kt, vt, acc_kv, qs, gs, qt, gt, acc_o, row_max, row_sum, row_delta, acc_q,
    sums, sems,
):
    spans, heads = order.shape[0], q_ref.shape[1] // span
    chunks = spans // per_chunk
    rows = heads * span
    core = own[2]

    def place(slot, carry):
        slot_of[order[slot]] = slot
        return carry

    lax.fori_loop(0, spans, place, 0)

    def arrange(c, carry):
        for j in range(per_chunk):
            slot = slot_of[c * per_chunk + j]
            pair, rows_at = slot // 4, pl.multiple_of(slot % 2 * span, span)
            mine = (slot // 2) % 2 == core
            both = jnp.where(
                mine, kv_ref[pair, pl.ds(rows_at, span), :], kv_other_ref[pair, pl.ds(rows_at, span), :]
            )
            part = slice(j * span, (j + 1) * span)
            ks[c, part, :] = both[:, :span]
            vs[c, part, :] = both[:, span:]
            kt[c, :, part] = both[:, :span].T
            vt[c, :, part] = both[:, span:].T
        return carry

    lax.fori_loop(0, chunks, arrange, 0)

    def clear(c, carry):
        acc_kv[c] = jnp.zeros_like(acc_kv[c])
        return carry

    first_upper = own[0] > own[1]
    for upper in (True, False):
        which = jnp.where(first_upper, 0, 1) if upper else jnp.where(first_upper, 1, 0)
        block = own[which]
        row0 = pl.multiple_of(which * span, span)
        last = block // per_chunk
        for h in range(heads):
            part = slice(h * span, (h + 1) * span)
            qh = q_ref[pl.ds(row0, span), part]
            gh = g_ref[pl.ds(row0, span), part]
            qs[part, :] = qh
            gs[part, :] = gh
            qt[:, part] = qh.T
            gt[:, part] = gh.T

        def allowed(c):
            key_pos = c * chunk + lax.broadcasted_iota(jnp.int32, (chunk, rows), 0)
            row = lax.broadcasted_iota(jnp.int32, (chunk, rows), 1)
            return key_pos <= block * span + jnp.bitwise_and(row, span - 1)

        row_max[...] = jnp.full_like(row_max, floor_score)
        row_sum[...] = jnp.zeros_like(row_sum)
        acc_o[...] = jnp.zeros_like(acc_o)

        def forward(c, masked):
            s = mm(ks[c], qt[...])
            if masked:
                s = jnp.where(allowed(c), s, floor_score)
            old = row_max[...]
            new = jnp.maximum(old, jnp.max(s, axis=0, keepdims=True))
            p = jnp.exp2(s - new)
            alpha = jnp.exp2(old - new)
            row_max[...] = new
            row_sum[...] = row_sum[...] * alpha + jnp.sum(p, axis=0, keepdims=True)
            acc_o[...] = acc_o[...] * alpha + mm(vt[c], p.astype(bf16))

        def forward_step(c, carry):
            forward(c, False)
            return carry

        def forward_pair(i, carry):
            c = 2 * i
            s = [mm(ks[c + j], qt[...]) for j in range(2)]
            old = row_max[...]
            new = jnp.maximum(old, jnp.max(jnp.maximum(s[0], s[1]), axis=0, keepdims=True))
            p = [jnp.exp2(part - new) for part in s]
            alpha = jnp.exp2(old - new)
            row_max[...] = new
            row_sum[...] = row_sum[...] * alpha + jnp.sum(p[0] + p[1], axis=0, keepdims=True)
            acc_o[...] = (
                acc_o[...] * alpha + mm(vt[c], p[0].astype(bf16)) + mm(vt[c + 1], p[1].astype(bf16))
            )
            return carry

        lax.fori_loop(0, last // 2, forward_pair, 0)
        lax.fori_loop(last // 2 * 2, last, forward_step, 0)
        forward(last, True)

        total = row_sum[...]
        ctx_t = (acc_o[...] / total).astype(bf16)
        row_max[...] = row_max[...] + jnp.log2(total)
        row_delta[...] = jnp.sum(ctx_t.astype(f32) * gt[...].astype(f32), axis=0, keepdims=True)
        for h in range(heads):
            part = slice(h * span, (h + 1) * span)
            ctx_ref[pl.ds(row0, span), part] = ctx_t[:, part].T
        acc_q[...] = jnp.zeros_like(acc_q)

        def backward(c, masked):
            s = mm(ks[c], qt[...])
            p = jnp.exp2(s - row_max[...])
            if masked:
                p = jnp.where(allowed(c), p, 0.0)
            dp = mm(vs[c], gt[...])
            ds = (p * (dp - row_delta[...])).astype(bf16)
            dv, dk = mm(p.astype(bf16), gs[...]), mm(ds, qs[...])
            if upper:
                acc_kv[c, :, span:] = dv
                acc_kv[c, :, :span] = dk
            else:
                acc_kv[c, :, span:] += dv
                acc_kv[c, :, :span] += dk
            acc_q[...] += mm(kt[c], ds)

        def backward_step(c, carry):
            backward(c, False)
            return carry

        def backward_pair(i, carry):
            c = 2 * i
            s = [mm(ks[c + j], qt[...]) for j in range(2)]
            p = [jnp.exp2(part - row_max[...]) for part in s]
            dp = [mm(vs[c + j], gt[...]) for j in range(2)]
            ds = [(p[j] * (dp[j] - row_delta[...])).astype(bf16) for j in range(2)]
            for j in range(2):
                dv, dk = mm(p[j].astype(bf16), gs[...]), mm(ds[j], qs[...])
                if upper:
                    acc_kv[c + j, :, span:] = dv
                    acc_kv[c + j, :, :span] = dk
                else:
                    acc_kv[c + j, :, span:] += dv
                    acc_kv[c + j, :, :span] += dk
            acc_q[...] += mm(kt[c], ds[0]) + mm(kt[c + 1], ds[1])
            return carry

        lax.fori_loop(0, last // 2, backward_pair, 0)
        lax.fori_loop(last // 2 * 2, last, backward_step, 0)
        backward(last, True)
        if upper:
            lax.fori_loop(last + 1, chunks, clear, 0)
        for h in range(heads):
            part = slice(h * span, (h + 1) * span)
            dq_ref[pl.ds(row0, span), part] = acc_q[:, part].T * (span**-0.5)

    def give(c, carry):
        for j in range(per_chunk):
            part = slice(j * span, (j + 1) * span)
            slot = slot_of[c * per_chunk + j]
            pair, rows_at = slot // 4, pl.multiple_of(slot % 2 * span, span)
            side = jnp.where((slot // 2) % 2 == core, 0, 1)
            at = pl.ds(rows_at, span)
            sums[side, pair, at, :span] = (acc_kv[c, part, :span] * math.log(2.0)).astype(bf16)
            sums[side, pair, at, span:] = acc_kv[c, part, span:].astype(bf16)

        return carry

    lax.fori_loop(0, chunks, give, 0)
    copies = [
        pltpu.make_async_copy(sums.at[1], dkv_other_ref, sems.at[0]),
        pltpu.make_async_copy(sums.at[0], dkv_ref, sems.at[1]),
    ]
    for copy in copies:
        copy.start()
    for copy in copies:
        copy.wait()


def attention(order, own, q16, g16, kv, kv_other):
    rows_here, cols = q16.shape
    spans = order.shape[0]
    chunks = spans // per_chunk
    rows = cols
    share = jax.ShapeDtypeStruct(kv.shape, bf16)
    return pl.pallas_call(
        attention_kernel,
        out_shape=(
            jax.ShapeDtypeStruct((rows_here, cols), bf16),
            jax.ShapeDtypeStruct((rows_here, cols), f32),
            share,
            share,
        ),
        in_specs=[smem, smem] + [vmem] * 4,
        out_specs=(vmem, vmem, anywhere, anywhere),
        scratch_shapes=[
            pltpu.SMEM((spans,), jnp.int32),
            pltpu.VMEM((chunks, chunk, span), bf16),
            pltpu.VMEM((chunks, chunk, span), bf16),
            pltpu.VMEM((chunks, span, chunk), bf16),
            pltpu.VMEM((chunks, span, chunk), bf16),
            pltpu.VMEM((chunks, chunk, 2 * span), f32),
            pltpu.VMEM((rows, span), bf16),
            pltpu.VMEM((rows, span), bf16),
            pltpu.VMEM((span, rows), bf16),
            pltpu.VMEM((span, rows), bf16),
            pltpu.VMEM((span, rows), f32),
            pltpu.VMEM((1, rows), f32),
            pltpu.VMEM((1, rows), f32),
            pltpu.VMEM((1, rows), f32),
            pltpu.VMEM((span, rows), f32),
            pltpu.VMEM((2,) + kv.shape, bf16),
            pltpu.SemaphoreType.DMA((2,)),
        ],
        compiler_params=pltpu.CompilerParams(vmem_limit_bytes=36 * mib),
        cost_estimate=pl.CostEstimate(
            flops=1000, bytes_accessed=1000, transcendentals=0
        ),
        name="attention",
    )(order, own, q16, g16, kv, kv_other)


def grad_query_kernel(raw_ref, dq_ref, gain_ref, cos_ref, sin_ref, g_ref, gain_out):
    cosine, sine = cos_ref[...], sin_ref[...]
    sums = jnp.zeros((1, span), f32)
    for h in range(dq_ref.shape[1] // span):
        part = slice(h * span, (h + 1) * span)
        grad, terms = shape_head_grad(
            raw_ref[:, part].astype(f32), gain_ref[...], cosine, sine, dq_ref[:, part]
        )
        g_ref[:, part] = grad.astype(bf16)
        sums = sums + jnp.sum(terms, axis=0, keepdims=True)
    gain_out[...] = jnp.broadcast_to(sums, gain_out.shape)


def grad_key_value_kernel(raw_ref, dkv_ref, gain_ref, cos_ref, sin_ref, gain_q_ref, g_ref):
    rows = raw_ref.shape[0]
    dkv = jnp.sum(dkv_ref[...].astype(f32), axis=0)
    grad, terms = shape_head_grad(
        raw_ref[:, -span:].astype(f32), gain_ref[...], cos_ref[...], sin_ref[...], dkv[:, :span]
    )
    g_ref[:rows, :span] = grad.astype(bf16)
    g_ref[:rows, span:] = dkv[:, span:].astype(bf16)
    gain_k = jnp.sum(terms, axis=0, keepdims=True)
    split = []
    for gain in (gain_q_ref[0:1], gain_k):
        high = gain.astype(bf16).astype(f32)
        split.append(jnp.concatenate([high, gain - high], axis=1))
    row = lax.broadcasted_iota(jnp.int32, (g_ref.shape[0] - rows, 2 * span), 0)
    g_ref[rows:] = jnp.where(row == 0, split[0], jnp.where(row == 1, split[1], 0.0)).astype(bf16)


def over_tokens(where, turned_ref, blocks):
    columns = len(blocks) // 2
    toks = turned_ref.shape[2]
    y, core = where[0], where[1]
    total = 0.0
    for i, block in enumerate(blocks):
        from_y = lax.rem(y + i % columns, columns)
        from_core = core if i < columns else 1 - core
        at = (from_core * 2 + lax.rem(from_y, 2)) * 2 + from_y // 2
        total = total + mm(turned_ref[at], block[:toks])
    return total


def query_weight_grad_kernel(where, turned_ref, *rest):
    blocks, (out_ref, done_ref) = rest[:-2], rest[-2:]
    out_ref[...] = over_tokens(where, turned_ref, blocks).astype(bf16)
    done_ref[...] = jnp.zeros_like(done_ref)


def weight_grad_kernel(where, turned_ref, query_ref, *rest):
    blocks, out_ref = rest[:-1], rest[-1]
    toks = turned_ref.shape[2]
    gains = sum(block[toks:].astype(f32) for block in blocks)
    gain = gains[:8, :span] + gains[:8, span:]
    high = gain.astype(bf16).astype(f32)
    extra = jnp.concatenate([jnp.zeros((8, query_ref.shape[1]), f32), high, gain - high], axis=1)
    total = jnp.concatenate(
        [query_ref[...].astype(f32), over_tokens(where, turned_ref, blocks)], axis=1
    )
    own_rows = total.shape[0] // out_ref.shape[0]
    for i in range(out_ref.shape[0]):
        part = total[i * own_rows : (i + 1) * own_rows]
        out_ref[i] = jnp.concatenate([part, extra], axis=0).astype(bf16)


def grad_states_kernel(where, gq_ref, gkv_ref, q_ref, q_theirs_ref, kv_ref, kv_theirs_ref, out_ref):
    core = where[1]
    own_rows, group = 40, 640
    transposed = (((1,), (1,)), ((), ()))

    def product(q, kv, i):
        part = slice(i * group, (i + 1) * group)
        return lax.dot_general(
            q[part], gq_ref[...], transposed, preferred_element_type=f32
        ) + lax.dot_general(kv[part], gkv_ref[: gq_ref.shape[0]], transposed, preferred_element_type=f32)

    for i in range(q_ref.shape[0] // group):
        mine, theirs = product(q_ref, kv_ref, i), product(q_theirs_ref, kv_theirs_ref, i)
        sides = (jnp.where(core == 0, mine, theirs), jnp.where(core == 0, theirs, mine))
        rows = jnp.concatenate(
            [side[j : j + own_rows] for j in range(0, group, own_rows) for side in sides], axis=0
        )
        out_ref[:, 2 * i * group : 2 * (i + 1) * group] = rows.astype(bf16).T


def finish_kernel(parts_ref, query_ref, key_ref, value_ref, gain_q_ref, gain_k_ref):
    sums = jnp.sum(parts_ref[...].astype(f32), axis=0)
    rows, cols = query_ref.shape
    query_ref[...] = sums[:rows, :cols]
    key_ref[...] = sums[:rows, cols : cols + span]
    value_ref[...] = sums[:rows, cols + span :]
    gains = sums[rows:, cols : cols + span] + sums[rows:, cols + span :]
    gain_q_ref[...] = gains[0:1]
    gain_k_ref[...] = gains[1:2]


cheap = pl.CostEstimate(flops=1000, bytes_accessed=1000, transcendentals=0)


def call(kernel, shapes, *args, name, after=(), limit=16, scratch=(), out_spec=vmem):
    count = len(args)

    def run(*refs):
        kernel(*refs[:count], *refs[count + len(after) :])

    return pl.pallas_call(
        run,
        out_shape=shapes,
        in_specs=[smem if a.dtype == jnp.int32 else vmem for a in args] + [vmem] * len(after),
        out_specs=jax.tree.map(lambda _: out_spec, shapes),
        scratch_shapes=scratch,
        compiler_params=pltpu.CompilerParams(vmem_limit_bytes=limit * mib),
        cost_estimate=cheap,
        name=name,
    )(*args, *after)


plane = ("x", "z")
column = ("y_hi", "y_lo")
chips = plane + column
swapped = [(0, 0), (1, 2), (2, 1), (3, 3)]
flipped = [(0, 1), (1, 0)]


def swap(array):
    return lax.ppermute(array, ("y_hi", "core"), swapped)


def flip(array):
    return lax.ppermute(array, "core", flipped)


def to_all(array, axes, count):
    return lax.all_to_all(jnp.broadcast_to(array[None], (count,) + array.shape), axes, 0, 0)


def ring(array, step):
    return lax.ppermute(array, column, [(i, (i - step) % 4) for i in range(4)])


def around(array):
    mine = [array] + [ring(array, k) for k in range(1, 4)]
    return mine + [flip(a) for a in mine]


def local(hidden_states, block_order, w_query, w_key, w_value, gain_query, gain_key, cotangent):
    tokens = hidden_states[0]
    tok_rows, width = tokens.shape
    q_cols = w_query.shape[1]
    kv_cols = 2 * span
    own_rows = w_query.shape[0]
    planes, columns = 16, 4
    half = width // 2
    place = lax.axis_index("x") * 4 + lax.axis_index("z")
    y_hi, core = lax.axis_index("y_hi"), lax.axis_index("core")
    y = y_hi * 2 + lax.axis_index("y_lo")
    where = jnp.stack([y, core]).astype(jnp.int32)
    offsets = jnp.arange(span, dtype=jnp.int32)

    def angles_of(part):
        blocks = lax.dynamic_slice_in_dim(block_order, 2 * (place * 2 + part), 2)
        positions = (blocks[:, None] * span + offsets[None, :]).reshape(tok_rows)
        return blocks, rotation(positions, span)

    _, (cosine, sine) = angles_of(y_hi)
    own_blocks, (cos_there, sin_there) = angles_of(core)
    own = jnp.concatenate([own_blocks, core[None].astype(jnp.int32)])
    gain_q, gain_k = gain_query[None, :], gain_key[None, :]
    shape = jax.ShapeDtypeStruct

    kv_mine = to_all(jnp.concatenate([w_key, w_value], axis=1), chips, planes * columns)
    q_send, toks_mine, toks_theirs, turned, turned_theirs, done = call(
        prepare_kernel,
        (shape((planes * columns, own_rows, q_cols), bf16),)
        + (shape((tok_rows, half), bf16),) * 2
        + (shape((columns, half // columns, tok_rows), bf16),) * 2
        + (shape((8, span), f32),),
        where, tokens.T.reshape(planes, columns, 2, own_rows, tok_rows), w_query,
        name="prepare",
        after=(cosine, sine, cos_there, sin_there),
    )
    kv_mine, q_send, done, own = lax.optimization_barrier((kv_mine, q_send, done, own))
    kv_mine = kv_mine.reshape(half, kv_cols)
    kv_theirs = flip(kv_mine)
    q_mine = lax.all_to_all(q_send, chips, 0, 0).reshape(half, q_cols)

    kv16, raw_k = call(
        key_value_kernel,
        (shape((tok_rows, kv_cols), bf16), shape((tok_rows, span), f32)),
        toks_mine, toks_theirs, kv_mine, kv_theirs, gain_k, cosine, sine,
        name="key_value",
        after=(done,),
    )
    kv_send = call(
        spread_kernel, shape((planes, tok_rows, kv_cols), bf16), swap(kv16), name="spread"
    )
    *packed, packed_done = call(
        pack_kernel,
        (shape((2, half // columns, tok_rows), bf16),) * columns + (shape((8, span), f32),),
        where, turned, flip(turned_theirs),
        name="pack",
    )
    kv_send, q_mine = lax.optimization_barrier((kv_send, q_mine))
    kv_own = lax.all_to_all(kv_send, plane, 0, 0)
    q_theirs = flip(q_mine)
    grad_out = swap(cotangent[0])
    q16, raw = call(
        query_kernel,
        (shape((tok_rows, q_cols), bf16), shape((tok_rows, q_cols + span), bf16)),
        toks_mine, toks_theirs, q_mine, q_theirs, raw_k, gain_q, cosine, sine,
        name="query",
        after=(grad_out, packed_done),
    )
    q16, raw_there = swap(q16), swap(raw)
    kv_own, q16 = lax.optimization_barrier((kv_own, q16))
    kv_other = flip(kv_own)
    turned = [packed[0]] + [
        lax.ppermute(packed[k], column, [(i, (i + k) % columns) for i in range(columns)])
        for k in range(1, columns)
    ]

    ctx, dq, dkv_mine, dkv_theirs = attention(block_order, own, q16, grad_out, kv_own, kv_other)
    dkv_theirs, turned = pl.pallas_call(
        place_kernel,
        out_shape=(
            shape(dkv_theirs.shape, bf16),
            shape((columns, 2, half // columns, tok_rows), bf16),
        ),
        in_specs=[smem, anywhere] + [vmem] * (1 + columns),
        out_specs=(anywhere, vmem),
        input_output_aliases={1: 0},
        compiler_params=pltpu.CompilerParams(vmem_limit_bytes=16 * mib),
        cost_estimate=cheap,
        name="place",
    )(where, dkv_theirs, raw_there, turned[0], turned[3], turned[2], turned[1])
    turned = turned.reshape(2 * columns, half // columns, tok_rows)
    dkv = (dkv_mine.astype(f32) + flip(dkv_theirs).astype(f32)).astype(bf16)
    dkv = lax.all_to_all(dkv, plane, 0, 0)

    g_q, gains_q = call(
        grad_query_kernel,
        (shape((tok_rows, q_cols), bf16), shape((8, span), f32)),
        raw_there, dq, gain_q, cos_there, sin_there,
        name="grad_query",
    )
    query_parts, done = call(
        query_weight_grad_kernel,
        (shape((half // columns, q_cols), bf16), shape((8, span), f32)),
        where, turned, *around(g_q),
        name="query_weight_grad",
    )
    g_q_back = swap(g_q)
    g_kv = call(
        grad_key_value_kernel,
        shape((tok_rows + 16, kv_cols), bf16),
        raw_there, dkv, gain_k, cos_there, sin_there, gains_q,
        name="grad_key_value",
        after=(done, g_q_back),
    )
    blocks_kv = around(g_kv)
    g_kv_back = swap(g_kv)
    all_parts = shape((planes, own_rows + 8, q_cols + kv_cols), bf16)
    parts = call(
        weight_grad_kernel,
        all_parts,
        where, turned, query_parts, *blocks_kv,
        name="weight_grad",
    )
    parts = lax.all_to_all(parts, plane, 0, 0)
    own_query, own_key, own_value, gain_sum_q, gain_sum_k = call(
        finish_kernel,
        (shape((own_rows, q_cols), f32),)
        + (shape((own_rows, span), f32),) * 2
        + (shape((1, span), f32),) * 2,
        parts,
        name="finish",
    )
    grad_states = call(
        grad_states_kernel,
        shape((tok_rows, width), bf16),
        where, g_q_back, g_kv_back, q_mine, q_theirs, kv_mine, kv_theirs,
        name="grad_states",
    )
    return (
        swap(ctx)[None],
        grad_states[None],
        own_query,
        own_key,
        own_value,
        gain_sum_q[0],
        gain_sum_k[0],
    )


def solution(mesh):
    fine = Mesh(mesh.devices.reshape(4, 4, 2, 2, 2), ("x", "z", "y_hi", "y_lo", "core"))
    ctx, dp = ("x", "z", "y_hi"), ("y_lo", "core")
    rows = P(ctx + dp, None)
    tokens = P(dp, ctx, None)
    in_specs = (tokens, P(), rows, rows, rows, P(), P(), tokens)
    out_specs = (tokens, tokens, rows, rows, rows, P(), P())
    return jax.shard_map(local, mesh=fine, in_specs=in_specs, out_specs=out_specs, check_vma=False)
```
